32 devices in a mesh: dp: 16 (over z, y, core), mp: 2 (over x).
Axes of the slice: x: 2, y: 2, z: 4, core: 2. Of those that a mesh axis runs over, the one named last changes fastest.
Arguments:
- features: bfloat16 [1024, 4096], P('dp', 'mp'), may hold values from -6 to 6
- norm_gain: bfloat16 [4096], replicated, may hold values from 0.099609375 to 1.8984375
- w_key: bfloat16 [4096, 512], P('dp', 'mp'), may hold values from -0.09375 to 0.09375
- w_value: bfloat16 [4096, 512], P('dp', 'mp'), may hold values from -0.09375 to 0.09375
- queries: bfloat16 [1024, 2048], P('dp', 'mp'), may hold values from -150 to 150
- key_pool: bfloat16 [48, 128, 512], P('dp', None, 'mp'), may hold values from -5 to 5
- value_pool: bfloat16 [48, 128, 512], P('dp', None, 'mp'), may hold values from -5 to 5
- cache_lens: int32 [3], replicated, may hold values from 2 to 1920, as said below
- page_table: int32 [3, 25], replicated, may hold values from -1 to 47, as said below
- token_request: int32 [1024], replicated, may hold values from 0 to 2, as said below
Outputs:
- attended: bfloat16 [1024, 2048], P('dp', 'mp')
- keys_out: bfloat16 [48, 128, 512], P('dp', None, 'mp')
- values_out: bfloat16 [48, 128, 512], P('dp', None, 'mp')
The draws below stay inside these ranges and needn't reach their ends.
Inputs may be any that keep to these rules, and one draw needn't show every extreme that they name: `cache_lens`: exactly one request has 1920 cached tokens, each other request has at most 512. `page_table`: row r lists the pool pages of request r in logical order: its first ceil(cache_lens[r] / 128) entries are pages among the first 2 slots of some device, the entries up to the page of its last new token are pages among the other slots of some device, later entries are -1; no pool page is listed twice. `token_request`: never falling along the new tokens; every request has 256 or more new tokens.
All inputs are finite; a program needn't handle non-finite values.
Results may differ from the reference program's by a relative error of at most 0.0068.
Values may be sent and summed in bfloat16 or wider, within the bound.
No kernel may reach another device: no remote copies, remote signals or barrier semaphores. Data moves between devices by JAX's collectives and lax.ppermute only.
A program may use at most 64 MiB of HBM per device.

```python
import math
import jax
import jax.numpy as jnp
from jax import lax

D = 4096
HD = 128
HQ = 16
KVH = 4
PAGE = 128
SHORT = 512
REQS = 3
NEW = 1024
CTX = 1920
OLD_DEV = 2
NEW_DEV = 1
PAGES_DEV = 3
POOL = 48
SLOTS_OLD = 32
SLOTS_NEW = 16
MAXP = 25


def plan_requests(key):
    base = jax.random.fold_in(key, 11)
    key_list = jax.random.split(base, 6)
    first_size = jax.random.randint(key_list[0], (), NEW // 4, NEW // 3 + 1, dtype=jnp.int32)
    second_size = jax.random.randint(key_list[1], (), NEW // 4, NEW // 3 + 1, dtype=jnp.int32)
    third_size = NEW - first_size - second_size
    block_sizes = jnp.stack([first_size, second_size, third_size]).astype(jnp.int32)
    longest = jax.random.randint(key_list[2], (), 0, REQS, dtype=jnp.int32)
    shorts = jax.random.randint(key_list[3], (REQS,), 2, SHORT + 1, dtype=jnp.int32)
    lengths = jnp.where(jnp.arange(REQS, dtype=jnp.int32) == longest, CTX, shorts).astype(jnp.int32)
    old_count = (lengths + PAGE - 1) // PAGE
    all_count = (lengths + block_sizes + PAGE - 1) // PAGE
    fresh_count = all_count - old_count
    old_ids = jnp.arange(SLOTS_OLD, dtype=jnp.int32)
    old_pages = jax.random.permutation(key_list[4], old_ids // OLD_DEV * PAGES_DEV + old_ids % OLD_DEV)
    fresh_ids = jnp.arange(SLOTS_NEW, dtype=jnp.int32)
    fresh_pages = jax.random.permutation(key_list[5], fresh_ids // NEW_DEV * PAGES_DEV + OLD_DEV + fresh_ids % NEW_DEV)
    top_page = jnp.max(fresh_pages).astype(jnp.int32)
    top_at = jnp.argmax(fresh_pages).astype(jnp.int32)
    first_page = fresh_pages[0]
    fresh_pages = fresh_pages.at[top_at].set(first_page).at[0].set(top_page).astype(jnp.int32)
    old_start = jnp.cumsum(old_count).astype(jnp.int32) - old_count
    fresh_start = jnp.cumsum(fresh_count).astype(jnp.int32) - fresh_count
    logical = jnp.arange(MAXP, dtype=jnp.int32)[None, :]
    old_pick = jnp.take(old_pages, jnp.clip(old_start[:, None] + logical, 0, SLOTS_OLD - 1))
    fresh_pick = jnp.take(fresh_pages, jnp.clip(fresh_start[:, None] + logical - old_count[:, None], 0, SLOTS_NEW - 1))
    page_map = jnp.where(logical < old_count[:, None], old_pick, jnp.where(logical < all_count[:, None], fresh_pick, -1)).astype(jnp.int32)
    token_ids = jnp.arange(NEW, dtype=jnp.int32)
    request_map = ((token_ids >= first_size).astype(jnp.int32) + (token_ids >= first_size + second_size).astype(jnp.int32)).astype(jnp.int32)
    return (lengths, page_map, request_map)


def pool_keys(key):
    values = jnp.clip(jax.random.normal(jax.random.fold_in(key, 21), (POOL, PAGE, KVH * HD), jnp.float32), -5.0, 5.0)
    return values


def draw_cache_lens(key, part):
    return plan_requests(key)[0]


def draw_page_table(key, part):
    return plan_requests(key)[1]


def draw_token_request(key, part):
    return plan_requests(key)[2]


def draw_key_pool(key, part):
    return pool_keys(key).astype(jnp.bfloat16)


def draw_queries(key, part):
    values = jnp.clip(jax.random.normal(jax.random.fold_in(key, 31), (NEW, HQ * HD), jnp.float32), -5.0, 5.0)
    return values.astype(jnp.bfloat16)


def block_scale(own_key, dims, cuts, smallest, top_value):
    def one(axis_at, parts):
        steps = jax.random.uniform(jax.random.fold_in(jax.random.fold_in(own_key, 6), axis_at), (parts,), jnp.float32, smallest / len(cuts), top_value / len(cuts))
        return jnp.repeat(jnp.exp(steps), dims[axis_at] // parts).reshape((-1,) + (1,) * (len(dims) - axis_at - 1))

    level = one(*cuts[0])
    for cut in cuts[1:]:
        level = level * one(*cut)
    return level


def scatter_about(key, dims, scale, bound, shards=(), kind=jnp.bfloat16):
    loudness = block_scale(key, dims, shards, -0.22, 0.18) if shards else 1.0
    values = jax.random.normal(key, dims, jnp.float32) * scale * loudness
    return jnp.minimum(jnp.maximum(values, -bound), bound).astype(kind)


def setup_inputs(seed: int = 0) -> dict:
    key_of = jax.random.split(jax.random.key(seed), 11)
    features = scatter_about(key_of[0], (NEW, D), 1.0, 6.0, ((0, 16), (1, 2)))
    norm_gain = jnp.clip(1.0 + 0.18 * jax.random.normal(key_of[1], (D,), jnp.float32), 0.099609375, 1.8984375).astype(jnp.bfloat16)
    w_key = scatter_about(key_of[2], (D, KVH * HD), D ** -0.5, 0.09375, ((0, 16), (1, 2)))
    w_value = scatter_about(key_of[3], (D, KVH * HD), D ** -0.5, 0.09375, ((0, 16), (1, 2)))
    queries = draw_queries(jax.random.fold_in(key_of[10], 71), 0)
    key_pool = draw_key_pool(jax.random.fold_in(key_of[10], 71), 0)
    value_pool = scatter_about(key_of[6], (POOL, PAGE, KVH * HD), 1.0, 5.0, ((0, 16), (2, 2)))
    cache_lens = draw_cache_lens(jax.random.fold_in(key_of[10], 71), 0)
    page_table = draw_page_table(jax.random.fold_in(key_of[10], 71), 0)
    token_request = draw_token_request(jax.random.fold_in(key_of[10], 71), 0)
    return {"features": features, "norm_gain": norm_gain, "w_key": w_key, "w_value": w_value, "queries": queries, "key_pool": key_pool, "value_pool": value_pool, "cache_lens": cache_lens, "page_table": page_table, "token_request": token_request}


THETA = 500000.0

def rotate(values, positions, head_size):
    halfway = head_size // 2
    inverse = THETA ** (-(jnp.arange(halfway, dtype=jnp.float32) * 2.0) / head_size)
    angles = positions.astype(jnp.float32)[:, None] * inverse[None, :]
    cosine = jnp.cos(angles)[:, None, :]
    sine = jnp.sin(angles)[:, None, :]
    first_half = values[..., :halfway]
    second_half = values[..., halfway:]
    return jnp.concatenate([first_half * cosine - second_half * sine, second_half * cosine + first_half * sine], axis=-1)

def reference(features, norm_gain, w_key, w_value, queries, key_pool, value_pool, cache_lens, page_table, token_request):
    widened = features.astype(jnp.float32)
    mean_square = lax.optimization_barrier(jnp.mean(widened * widened, axis=1, keepdims=True))
    normed = (widened * lax.rsqrt(mean_square + 1e-05) * norm_gain.astype(jnp.float32)).astype(jnp.bfloat16)
    key_sums = jnp.dot(normed, w_key, preferred_element_type=jnp.float32)
    value_sums = jnp.dot(normed, w_value, preferred_element_type=jnp.float32)
    request_ids = jnp.arange(REQS, dtype=jnp.int32)
    member = (token_request[:, None] == request_ids[None, :]).astype(jnp.int32)
    counts = lax.optimization_barrier(jnp.sum(member, axis=0)).astype(jnp.int32)
    starts = (jnp.cumsum(counts) - counts).astype(jnp.int32)
    token_index = jnp.arange(NEW, dtype=jnp.int32)
    token_pos = (lax.optimization_barrier(jnp.sum(member * (cache_lens - starts)[None, :], axis=1)) + token_index).astype(jnp.int32)
    new_keys = rotate(key_sums.reshape(NEW, KVH, HD), token_pos, HD).reshape(NEW, KVH * HD).astype(jnp.bfloat16)
    new_values = value_sums.astype(jnp.bfloat16)
    slots = page_table[token_request, token_pos // PAGE].astype(jnp.int32)
    rows_in = (token_pos % PAGE).astype(jnp.int32)
    keys_out = key_pool.at[slots, rows_in].set(new_keys)
    values_out = value_pool.at[slots, rows_in].set(new_values)
    safe_pages = jnp.maximum(page_table, 0).astype(jnp.int32)
    logical_keys = keys_out[safe_pages].reshape(REQS, MAXP * PAGE, KVH, HD)
    logical_values = values_out[safe_pages].reshape(REQS, MAXP * PAGE, KVH, HD)
    key_limit = (cache_lens + counts).astype(jnp.int32)
    positions = jnp.arange(MAXP * PAGE, dtype=jnp.int32)
    group_size = HQ // KVH
    grouped = queries.reshape(NEW, KVH, group_size, HD)
    scale = 1.0 / math.sqrt(HD)
    block_rows = 128

    def one_block(block_start):
        block_queries = lax.dynamic_slice_in_dim(grouped, block_start, block_rows).astype(jnp.float32)
        block_request = lax.dynamic_slice_in_dim(token_request, block_start, block_rows)
        block_pos = lax.dynamic_slice_in_dim(token_pos, block_start, block_rows)
        result = jnp.zeros((block_rows, KVH, group_size, HD), jnp.float32)
        for which in range(REQS):

            def compute(current):
                keys_wide = logical_keys[which].astype(jnp.float32)
                values_wide = logical_values[which].astype(jnp.float32)
                scores = jnp.einsum('thgd,khd->thgk', block_queries, keys_wide) * scale
                visible = (positions[None, :] < key_limit[which]) & (positions[None, :] <= block_pos[:, None]) & (block_request[:, None] == which)
                mask_full = visible[:, None, None, :]
                masked = jnp.where(mask_full, scores, -jnp.inf)
                top_score = lax.optimization_barrier(jnp.max(masked, axis=-1, keepdims=True))
                top_score = jnp.where(jnp.isfinite(top_score), top_score, 0.0)
                weights = jnp.where(mask_full, jnp.exp(jnp.where(mask_full, scores - top_score, 0.0)), 0.0)
                total = lax.optimization_barrier(jnp.sum(weights, axis=-1))
                rounded = lax.optimization_barrier(weights.astype(jnp.bfloat16)).astype(jnp.float32)
                mixed = jnp.einsum('thgk,khd->thgd', rounded, values_wide)
                safe_total = jnp.where(total > 0.0, total, 1.0)
                piece_out = mixed / safe_total[..., None]
                return jnp.where((block_request == which)[:, None, None, None], piece_out, current)
            result = lax.cond(jnp.any(block_request == which), compute, lambda current: current, result)
        return result.astype(jnp.bfloat16)
    blocks_out = lax.map(one_block, jnp.arange(0, NEW, block_rows, dtype=jnp.int32))
    attended = blocks_out.reshape(NEW, HQ * HD)
    return (attended, keys_out, values_out)
```

```python
import functools
import math

import jax
import jax.numpy as jnp
import numpy as np
from jax import lax
from jax.experimental import pallas as pl
from jax.experimental.pallas import tpu as pltpu
from jax.sharding import PartitionSpec as P

HD = 128
PAGE = 128
SHORT = 512
CTX_DEV = 120


THETA = 500000.0
NEG_FILL = -1e30
NEG_START = -1e29
LOG2E = 1.4426950408889634
VMEM_LIMIT = 32 * 1024 * 1024
SPLIT_LIMIT = 63 * 1024 * 1024
STEP_PAGES = 4


def rotate(values, positions, head_size):
    halfway = head_size // 2
    inverse = THETA ** (-(jnp.arange(halfway, dtype=jnp.float32) * 2.0) / head_size)
    angles = positions.astype(jnp.float32)[:, None] * inverse[None, :]
    cosine = jnp.cos(angles)[:, None, :]
    sine = jnp.sin(angles)[:, None, :]
    first_half = values[..., :halfway]
    second_half = values[..., halfway:]
    return jnp.concatenate(
        [first_half * cosine - second_half * sine, second_half * cosine + first_half * sine],
        axis=-1,
    )


def general_body(
    features,
    norm_gain,
    w_key,
    w_value,
    queries,
    key_pool,
    value_pool,
    cache_lens,
    page_table,
    token_request,
):
    gathered = lax.all_gather(features, "mp", axis=1, tiled=True)
    widened = gathered.astype(jnp.float32)
    mean_square = jnp.mean(widened * widened, axis=1, keepdims=True)
    normed = (widened * lax.rsqrt(mean_square + 1e-05) * norm_gain.astype(jnp.float32)).astype(
        jnp.bfloat16
    )
    tok_rows = features.shape[0]
    kv_width = w_key.shape[1]
    head_size = HD
    kv_heads = kv_width // head_size
    q_heads = queries.shape[1] // head_size
    group_size = q_heads // kv_heads
    scale = 1.0 / math.sqrt(head_size)
    pieces = (
        lax.all_gather(w_key, "dp", axis=0, tiled=True),
        lax.all_gather(w_value, "dp", axis=0, tiled=True),
    )
    key_sums = jnp.dot(normed, pieces[0], preferred_element_type=jnp.float32)
    value_sums = jnp.dot(normed, pieces[1], preferred_element_type=jnp.float32)
    total_new = token_request.shape[0]
    requests = cache_lens.shape[0]
    request_ids = jnp.arange(requests, dtype=jnp.int32)
    member = (token_request[:, None] == request_ids[None, :]).astype(jnp.int32)
    counts = jnp.sum(member, axis=0)
    starts = jnp.cumsum(counts) - counts
    token_index = jnp.arange(total_new, dtype=jnp.int32)
    token_pos = jnp.sum(member * (cache_lens - starts)[None, :], axis=1) + token_index
    dp_index = lax.axis_index("dp")
    dp_count = lax.axis_size("dp")
    first_token = dp_index * tok_rows
    my_request = lax.dynamic_slice_in_dim(token_request, first_token, tok_rows)
    my_pos = lax.dynamic_slice_in_dim(token_pos, first_token, tok_rows)
    key_heads = rotate(key_sums.reshape(tok_rows, kv_heads, head_size), my_pos, head_size)
    new_keys = key_heads.reshape(tok_rows, kv_width).astype(jnp.bfloat16)
    new_values = value_sums.astype(jnp.bfloat16)
    pages_dev = key_pool.shape[0]
    page_rows = key_pool.shape[1]
    max_pages = page_table.shape[1]
    slot_all = jnp.take(page_table.reshape(-1), token_request * max_pages + token_pos // page_rows)
    local_slot = slot_all - dp_index * pages_dev
    owned = (local_slot >= 0) & (local_slot < pages_dev)
    dest_all = jnp.where(
        owned, local_slot * page_rows + token_pos % page_rows, pages_dev * page_rows
    )
    long_pages = (CTX_DEV * dp_count + PAGE - 1) // PAGE
    old_dev = (long_pages + 2 * ((SHORT + PAGE - 1) // PAGE) + dp_count - 1) // dp_count
    old_total = old_dev * dp_count
    old_ids = jnp.arange(old_total, dtype=jnp.int32)
    old_phys = old_ids // old_dev * pages_dev + old_ids % old_dev
    matches = (page_table[None, :, :] == old_phys[:, None, None]).astype(jnp.int32)
    page_has = jnp.sum(matches, axis=(1, 2)) > 0
    page_request = jnp.sum(matches * request_ids[None, :, None], axis=(1, 2))
    page_logical = jnp.sum(
        matches * jnp.arange(max_pages, dtype=jnp.int32)[None, None, :], axis=(1, 2)
    )
    page_limit = jnp.sum(matches * cache_lens[None, :, None], axis=(1, 2))
    q_local = queries.reshape(tok_rows, kv_heads, group_size, head_size)

    def attend(att_state, keys_flat, values_flat, key_info):
        key_request, key_pos, key_ok = key_info
        visible = (
            key_ok[None, :]
            & (key_request[None, :] == my_request[:, None])
            & (key_pos[None, :] <= my_pos[:, None])
        )
        keys_shaped = keys_flat.reshape(keys_flat.shape[0], kv_heads, head_size)
        values_shaped = values_flat.reshape(values_flat.shape[0], kv_heads, head_size)
        running_max, running_sum, running_acc = att_state
        scores = (
            jnp.einsum("thgd,khd->thgk", q_local, keys_shaped, preferred_element_type=jnp.float32)
            * scale
        )
        mask_full = visible[:, None, None, :]
        masked = jnp.where(mask_full, scores, NEG_FILL)
        new_max = jnp.maximum(running_max, jnp.max(masked, axis=-1))
        factor = jnp.exp(running_max - new_max)
        soft_weights = jnp.where(mask_full, jnp.exp(masked - new_max[..., None]), 0.0)
        new_sum = running_sum * factor + jnp.sum(soft_weights, axis=-1)
        new_acc = running_acc * factor[..., None] + jnp.einsum(
            "thgk,khd->thgd",
            soft_weights.astype(jnp.bfloat16),
            values_shaped,
            preferred_element_type=jnp.float32,
        )
        return (new_max, new_sum, new_acc)

    def attend_rows(att_state, keys_flat, values_flat, key_info):
        row_count = keys_flat.shape[0]
        key_block = 2048
        if row_count > key_block and row_count % key_block == 0:
            blocks = row_count // key_block
            stacked = (
                keys_flat.reshape(blocks, key_block, kv_width),
                values_flat.reshape(blocks, key_block, kv_width),
                key_info[0].reshape(blocks, key_block),
                key_info[1].reshape(blocks, key_block),
                key_info[2].reshape(blocks, key_block),
            )

            def step_block(inner_state, slab_parts):
                return (
                    attend(
                        inner_state,
                        slab_parts[0],
                        slab_parts[1],
                        (slab_parts[2], slab_parts[3], slab_parts[4]),
                    ),
                    None,
                )

            att_state, unused = lax.scan(step_block, att_state, stacked)
            return att_state
        return attend(att_state, keys_flat, values_flat, key_info)

    start_state = (
        jnp.full((tok_rows, kv_heads, group_size), NEG_FILL, jnp.float32),
        jnp.zeros((tok_rows, kv_heads, group_size), jnp.float32),
        jnp.zeros((tok_rows, kv_heads, group_size, head_size), jnp.float32),
    )
    flat_keys = key_pool.reshape(pages_dev * page_rows, kv_width)
    flat_values = value_pool.reshape(pages_dev * page_rows, kv_width)
    old_keys = key_pool[:old_dev]
    old_values = value_pool[:old_dev]
    pieces = (
        lax.all_gather(old_keys, "dp", axis=0, tiled=True),
        lax.all_gather(old_values, "dp", axis=0, tiled=True),
    )
    page_count = pieces[0].shape[0]
    cached_keys = pieces[0].reshape(page_count * page_rows, kv_width)
    cached_values = pieces[1].reshape(page_count * page_rows, kv_width)
    row_ids = jnp.arange(page_rows, dtype=jnp.int32)[None, :]
    key_pos = page_logical[:, None] * page_rows + row_ids
    key_ok = page_has[:, None] & (key_pos < page_limit[:, None])
    key_request = jnp.broadcast_to(page_request[:, None], (page_count, page_rows))
    middle_state = attend_rows(
        start_state,
        cached_keys,
        cached_values,
        (key_request.reshape(-1), key_pos.reshape(-1), key_ok.reshape(-1)),
    )
    pieces = (
        lax.all_gather(new_keys, "dp", axis=0, tiled=True),
        lax.all_gather(new_values, "dp", axis=0, tiled=True),
    )
    att_state = middle_state
    pool_keys = flat_keys
    pool_values = flat_values
    key_request = token_request
    key_pos = token_pos
    att_state = attend_rows(
        att_state,
        pieces[0],
        pieces[1],
        (key_request, key_pos, jnp.ones((pieces[0].shape[0],), jnp.bool_)),
    )
    pool_keys, pool_values = (
        pool_keys.at[dest_all].set(pieces[0], mode="drop"),
        pool_values.at[dest_all].set(pieces[1], mode="drop"),
    )
    final_state, pool_keys, pool_values = (att_state, pool_keys, pool_values)
    final_max, final_sum, final_acc = final_state
    attended = (
        (final_acc / final_sum[..., None])
        .reshape(tok_rows, q_heads * head_size)
        .astype(jnp.bfloat16)
    )
    return (attended, pool_keys.reshape(key_pool.shape), pool_values.reshape(value_pool.shape))


def ring_chip(pos, chips):
    pos = pos % chips
    return jnp.where(pos < chips // 2, 2 * pos, 2 * chips - 1 - 2 * pos)


def ring_place(chip, chips):
    return jnp.where(chip % 2 == 0, chip // 2, (2 * chips - 1 - chip) // 2)


def ring_pairs(chips, step, swap):
    order = [2 * k if k < chips // 2 else 2 * chips - 1 - 2 * k for k in range(chips)]
    return [
        (2 * order[k] + core, 2 * order[(k + step) % chips] + (core ^ swap))
        for k in range(chips)
        for core in range(2)
    ]


def ring_offsets(chips):
    return [0] + [o for d in range(1, chips // 2) for o in (d, -d)] + [chips // 2]


def request_starts(tr_ref, requests):
    tr = tr_ref[...]
    starts = [jnp.int32(0)]
    for r in range(1, requests):
        starts.append(jnp.sum(jnp.where(tr < r, 1.0, 0.0)).astype(jnp.int32))
    starts.append(jnp.int32(tr.shape[0] * tr.shape[1]))
    return starts


def pick(cond_starts, values, tokens):
    out = jnp.zeros_like(tokens) + values[0]
    for r in range(1, len(values)):
        out = jnp.where(tokens >= cond_starts[r], values[r], out)
    return out


def chip_requests(chip, toks, starts):
    first, last = jnp.int32(0), jnp.int32(0)
    for start in starts[1:-1]:
        first = first + (chip * toks >= start).astype(jnp.int32)
        last = last + (chip * toks + toks - 1 >= start).astype(jnp.int32)
    return first, last


def split_kernel(old, f_ref, q_ref, kp_ref, vp_ref, xc_ref, xo_ref, qo_ref, kvc_ref, kvo_ref, sems):
    core = lax.axis_index("dp") % 2
    copies = []

    def copy(source, target):
        copies.append(pltpu.make_async_copy(source, target, sems.at[len(copies)]))
        copies[-1].start()

    for page_ref, first in ((kp_ref, 0), (vp_ref, old)):
        for out_ref, head in ((kvo_ref, 1 - core), (kvc_ref, core)):
            at = pl.ds(pl.multiple_of(head * HD, HD), HD)
            copy(page_ref.at[pl.ds(0, old), :, at], out_ref.at[pl.ds(first, old)])
    for out_ref, own in ((xo_ref, 1 - core), (xc_ref, core)):
        for m in range(f_ref.shape[1] // 512):
            at = pl.ds(pl.multiple_of((2 * m + own) * 256, 256), 256)
            copy(f_ref.at[:, at], out_ref.at[:, pl.ds(m * 256, 256)])
    half = q_ref.shape[1] // 2
    copy(q_ref.at[:, pl.ds(pl.multiple_of((1 - core) * half, 128), half)], qo_ref)
    for c in copies:
        c.wait()


def merge_kernel(kvm_ref, kvg_ref, q_ref, qg_ref, kv_ref, qs_ref):
    core = lax.axis_index("dp") % 2
    count = kvm_ref.shape[0]
    kv_ref[:count] = kvm_ref[...]
    kv_ref[count:] = kvg_ref[...]
    rows, group = q_ref.shape[0], qg_ref.shape[1] // HD
    for h in range(group):
        mine = pl.ds(pl.multiple_of((2 * h + core) * rows, rows), rows)
        other = pl.ds(pl.multiple_of((2 * h + 1 - core) * rows, rows), rows)
        qs_ref[mine, :] = q_ref[:, pl.ds(pl.multiple_of((core * group + h) * HD, HD), HD)]
        qs_ref[other, :] = qg_ref[:, h * HD : (h + 1) * HD]


def scale_kernel(
    chips, lens_ref, tr_ref, inv_ref, gain_ref, a_ref, b_ref, c_ref, d_ref, xs_ref, ss_ref, cos_ref, sin_ref
):
    dp = lax.axis_index("dp")
    mp = lax.axis_index("mp")
    chip, core = dp // 2, dp % 2
    rows = a_ref.shape[0]
    per_half = a_ref.shape[1] // 256
    for first, second, owner in ((a_ref, b_ref, core), (c_ref, d_ref, 1 - core)):
        at = pl.ds(pl.multiple_of(owner * rows, rows), rows)
        total = jnp.zeros((rows, 256), jnp.float32)
        for ref, half in ((first, mp), (second, 1 - mp)):
            for m in range(per_half):
                wide = ref[:, m * 256 : (m + 1) * 256].astype(jnp.float32)
                block = half * (2 * per_half) + 2 * m + core
                gain = gain_ref[:, pl.ds(pl.multiple_of(block * 256, 256), 256)].astype(jnp.float32)
                total = total + wide * wide
                xs_ref[half * per_half + m, at, :] = (wide * gain).astype(jnp.bfloat16)
        ss_ref[at, :] = jnp.broadcast_to(jnp.sum(total, axis=1, keepdims=True), (rows, 128))
    requests = lens_ref.shape[0]
    starts = request_starts(tr_ref, requests)
    tokens = chip * (2 * rows) + lax.broadcasted_iota(jnp.int32, (2 * rows, 128), 0)
    shift = pick(starts, [lens_ref[r] - starts[r] for r in range(requests)], tokens)
    angles = (tokens + shift).astype(jnp.float32) * inv_ref[...]
    lane = lax.broadcasted_iota(jnp.int32, (2 * rows, 128), 1)
    sine = jnp.sin(angles)
    cos_ref[...] = jnp.cos(angles)
    sin_ref[...] = jnp.where(lane < HD // 2, -sine, sine)


def project_kernel(chips, xs_ref, ss_ref, *refs):
    keys, values = refs[:chips], refs[chips : 2 * chips]
    send_ref, keep_ref, acc_ref = refs[2 * chips :]
    dp = lax.axis_index("dp")
    chip, core = dp // 2, dp % 2
    place = ring_place(chip, chips)
    ksum = jnp.zeros((xs_ref.shape[1], 2 * HD), jnp.float32)
    vsum = jnp.zeros((xs_ref.shape[1], 2 * HD), jnp.float32)
    for n, offset in enumerate(ring_offsets(chips)):
        x = xs_ref[ring_chip(place + offset + chips, chips)]
        ksum = ksum + jnp.dot(x, keys[n][...], preferred_element_type=jnp.float32)
        vsum = vsum + jnp.dot(x, values[n][...], preferred_element_type=jnp.float32)
    acc_ref[:, : 2 * HD] = ksum
    acc_ref[:, 2 * HD :] = vsum
    for ref, head in ((send_ref, 1 - core), (keep_ref, core)):
        ref[:, :HD] = acc_ref[:, pl.ds(pl.multiple_of(head * HD, HD), HD)]
        ref[:, HD : 2 * HD] = acc_ref[:, pl.ds(pl.multiple_of((2 + head) * HD, HD), HD)]
        ref[:, 2 * HD :] = ss_ref[...]


def rotate_kernel(width, keep_ref, got_ref, cos_ref, sin_ref, out_ref):
    total = keep_ref[...] + got_ref[...]
    inverse = lax.rsqrt(total[:, 2 * HD :] * (1.0 / width) + 1e-05)
    key = total[:, :HD] * inverse
    rolled = pltpu.roll(key, HD // 2, 1)
    out_ref[:, :HD] = (key * cos_ref[...] + rolled * sin_ref[...]).astype(jnp.bfloat16)
    out_ref[:, HD:] = (total[:, HD : 2 * HD] * inverse).astype(jnp.bfloat16)


def attend_block(qs_ref, keys, values, first, low, high, m_ref, l_ref, acc_ref):
    scores = lax.dot_general(keys, qs_ref[...], (((1,), (1,)), ((), ())), preferred_element_type=jnp.float32)
    ids = first + lax.broadcasted_iota(jnp.int32, scores.shape, 0)
    scores = jnp.where((ids >= low) & (ids < high), scores * (LOG2E / math.sqrt(HD)), NEG_FILL)
    before = m_ref[...]
    top = jnp.maximum(before, jnp.max(scores, axis=0, keepdims=True))
    shrink = jnp.exp2(before - top)
    weights = jnp.exp2(scores - top)
    m_ref[...] = top
    l_ref[...] = l_ref[...] * shrink + jnp.sum(weights, axis=0, keepdims=True)
    acc_ref[...] = acc_ref[...] * shrink + lax.dot_general(
        values,
        weights.astype(jnp.bfloat16),
        (((0,), (0,)), ((), ())),
        preferred_element_type=jnp.float32,
    )


def cached_part(
    chips, pages_dev, old, offsets, blocks, starts, reqs, lens_ref, table_ref, qs_ref, kbuf, vbuf, slot_of, state
):
    dp = lax.axis_index("dp")
    chip, core = dp // 2, dp % 2
    place = ring_place(chip, chips)
    requests = lens_ref.shape[0]
    width = qs_ref.shape[0]
    toks = starts[-1] // chips

    def clear(i, carry):
        slot_of[i] = -1
        return carry

    def held(page):
        distance = (ring_place(page // (2 * pages_dev), chips) - place + chips) % chips
        found = distance == offsets[0] % chips
        for o in offsets[1:]:
            found = found | (distance == o % chips)
        return found

    lax.fori_loop(0, slot_of.shape[0], clear, 0)
    base = jnp.int32(0)
    lows, highs = [], []
    for r in range(requests):
        length = lens_ref[r]
        pages = (length + PAGE - 1) // PAGE
        count = jnp.where((r >= reqs[0]) & (r <= reqs[1]), pages, 0)

        def put(l, at, r=r):
            page = table_ref[r, l]
            here = held(page)

            @pl.when(here)
            def _():
                slot_of[page] = at

            return at + here.astype(jnp.int32)

        end = lax.fori_loop(0, count, put, base)
        last_here = (end > base) & held(table_ref[r, pages - 1])
        lows.append(base * PAGE)
        highs.append(end * PAGE - jnp.where(last_here, pages * PAGE - length, 0))
        base = end

    for offset, block in zip(offsets, blocks):
        source = ring_chip(place + offset + chips, chips)
        for part, owner in ((0, 2 * source + core), (2 * old, 2 * source + 1 - core)):
            for s in range(old):
                slot = slot_of[owner * pages_dev + s]

                @pl.when(slot >= 0)
                def _(block=block, part=part, s=s, slot=slot):
                    at = pl.ds(pl.multiple_of(slot * PAGE, PAGE), PAGE)
                    kbuf[at, :] = block[part + s]
                    vbuf[at, :] = block[part + old + s]

    size = STEP_PAGES * PAGE
    pad = pl.ds(pl.multiple_of(base * PAGE, PAGE), size - PAGE)
    kbuf[pad, :] = jnp.zeros((size - PAGE, HD), kbuf.dtype)
    vbuf[pad, :] = jnp.zeros((size - PAGE, HD), vbuf.dtype)
    tokens = chip * toks + lax.broadcasted_iota(jnp.int32, (1, width), 1) % toks
    low = pick(starts, lows, tokens)
    high = pick(starts, highs, tokens)

    def step(i, carry):
        at = pl.ds(pl.multiple_of(i * size, size), size)
        attend_block(qs_ref, kbuf[at, :], vbuf[at, :], i * size, low, high, *state)
        return carry

    lax.fori_loop(0, (base + STEP_PAGES - 1) // STEP_PAGES, step, 0)


def cached_kernel(chips, pages_dev, old, offsets, lens_ref, table_ref, tr_ref, qs_ref, *refs):
    blocks = refs[: len(offsets)]
    m_ref, l_ref, acc_ref, kbuf, vbuf, slot_of = refs[len(offsets) :]
    chip = lax.axis_index("dp") // 2
    starts = request_starts(tr_ref, lens_ref.shape[0])
    reqs = chip_requests(chip, starts[-1] // chips, starts)
    m_ref[...] = jnp.full(m_ref.shape, NEG_START, jnp.float32)
    l_ref[...] = jnp.zeros(l_ref.shape, jnp.float32)
    acc_ref[...] = jnp.zeros(acc_ref.shape, jnp.float32)
    cached_part(
        chips,
        pages_dev,
        old,
        offsets,
        blocks,
        starts,
        reqs,
        lens_ref,
        table_ref,
        qs_ref,
        kbuf,
        vbuf,
        slot_of,
        (m_ref, l_ref, acc_ref),
    )


def fresh_kernel(
    chips, pages_dev, old, offsets, lens_ref, table_ref, tr_ref, qs_ref, m0_ref, l0_ref, acc0_ref, *refs
):
    blocks, fresh = refs[: len(offsets)], refs[len(offsets) : len(offsets) + chips]
    atto_ref, attc_ref, no_ref, nc_ref, info_ref = refs[len(offsets) + chips : len(offsets) + chips + 5]
    (kbuf, vbuf, nbuf, m_ref, l_ref, acc_ref, out_ref, slot_of, new_at, new_lo, new_hi) = refs[
        len(offsets) + chips + 5 :
    ]
    dp = lax.axis_index("dp")
    chip, core = dp // 2, dp % 2
    place = ring_place(chip, chips)
    toks = fresh[0].shape[0]
    rows = toks // 2
    requests = lens_ref.shape[0]
    width = qs_ref.shape[0]
    group = width // toks
    starts = request_starts(tr_ref, requests)
    reqs = chip_requests(chip, toks, starts)
    first_req = reqs[0]
    m_ref[...] = m0_ref[...]
    l_ref[...] = l0_ref[...]
    acc_ref[...] = acc0_ref[...]
    cached_part(
        chips,
        pages_dev,
        old,
        offsets,
        blocks,
        starts,
        reqs,
        lens_ref,
        table_ref,
        qs_ref,
        kbuf,
        vbuf,
        slot_of,
        (m_ref, l_ref, acc_ref),
    )

    def clear(i, carry):
        new_lo[i] = 0
        new_hi[i] = 0
        return carry

    lax.fori_loop(0, new_lo.shape[0], clear, 0)
    for r in range(requests):
        length = lens_ref[r]

        def place_new(l, carry, r=r, length=length):
            at = l * PAGE - length + starts[r]
            page = table_ref[r, l]
            new_at[page] = at
            new_lo[page] = jnp.maximum(starts[r] - at, 0)
            new_hi[page] = jnp.minimum(starts[r + 1] - at, PAGE)
            return carry

        end = (length + starts[r + 1] - starts[r] + PAGE - 1) // PAGE
        lax.fori_loop(length // PAGE, end, place_new, 0)

    for n, offset in enumerate(ring_offsets(chips)):
        source = ring_chip(place + offset + chips, chips)
        nbuf[pl.ds(pl.multiple_of((source + 1) * toks, toks), toks), :] = fresh[n][...]
    nbuf[:toks, :] = jnp.zeros((toks, 2 * HD), nbuf.dtype)
    nbuf[(chips + 1) * toks :, :] = jnp.zeros((toks, 2 * HD), nbuf.dtype)

    tokens = chip * toks + lax.broadcasted_iota(jnp.int32, (1, width), 1) % toks
    low = pick(starts, starts[:requests], tokens)
    first_start = starts[0]
    for r in range(1, requests):
        first_start = jnp.where(first_req == r, starts[r], first_start)

    def step(b, carry):
        at = pl.ds(pl.multiple_of((b + 1) * toks, toks), toks)
        attend_block(qs_ref, nbuf[at, :HD], nbuf[at, HD:], b * toks, low, tokens + 1, m_ref, l_ref, acc_ref)
        return carry

    lax.fori_loop(first_start // toks, chip + 1, step, 0)
    result = acc_ref[...] / l_ref[...]
    for h in range(group):
        out_ref[:, h * HD : (h + 1) * HD] = result[:, h * toks : (h + 1) * toks].T.astype(jnp.bfloat16)
    attc_ref[...] = out_ref[pl.ds(pl.multiple_of(core * rows, rows), rows), :]
    atto_ref[...] = out_ref[pl.ds(pl.multiple_of((1 - core) * rows, rows), rows), :]

    row = lax.broadcasted_iota(jnp.int32, (PAGE, 2 * toks), 0)
    column = lax.broadcasted_iota(jnp.int32, (PAGE, 2 * toks), 1)
    for ref, owner in ((no_ref, dp + 1 - 2 * core), (nc_ref, dp)):
        for s in range(pages_dev):
            page = owner * pages_dev + s
            at, low_row, high_row = new_at[page], new_lo[page], new_hi[page]

            @pl.when(high_row > low_row)
            def _(ref=ref, s=s, at=at, low_row=low_row, high_row=high_row):
                shifted = at + toks
                first = pl.multiple_of(shifted // toks * toks, toks)
                chosen = (column + first == row + shifted) & (row >= low_row) & (row < high_row)
                ref[s] = jnp.dot(
                    jnp.where(chosen, 1.0, 0.0).astype(jnp.bfloat16),
                    nbuf[pl.ds(first, 2 * toks), :],
                    preferred_element_type=jnp.float32,
                ).astype(jnp.bfloat16)

    for s in range(pages_dev):
        info_ref[2 * s] = new_lo[dp * pages_dev + s]
        info_ref[2 * s + 1] = new_hi[dp * pages_dev + s]


def join_kernel(info_ref, attc_ref, attr_ref, nc_ref, nr_ref, kp_ref, vp_ref, att_ref, ko_ref, vo_ref):
    core = lax.axis_index("dp") % 2
    half = attc_ref.shape[1]
    att_ref[:, pl.ds(pl.multiple_of(core * half, HD), half)] = attc_ref[...]
    att_ref[:, pl.ds(pl.multiple_of((1 - core) * half, HD), half)] = attr_ref[...]
    row = lax.broadcasted_iota(jnp.int32, (PAGE, HD), 0)
    for s in range(kp_ref.shape[0]):
        chosen = (row >= info_ref[2 * s]) & (row < info_ref[2 * s + 1])
        for ref, head in ((nc_ref, core), (nr_ref, 1 - core)):
            at = pl.ds(pl.multiple_of(head * HD, HD), HD)
            ko_ref[s, :, at] = jnp.where(chosen, ref[s, :, :HD], kp_ref[s, :, at])
            vo_ref[s, :, at] = jnp.where(chosen, ref[s, :, HD:], vp_ref[s, :, at])


def call(
    kernel, outs, scratch=(), ins=None, smem=(), far=(), out_smem=(), out_far=(), limit=VMEM_LIMIT, name=None
):
    vmem, sm = pl.BlockSpec(memory_space=pltpu.VMEM), pl.BlockSpec(memory_space=pltpu.SMEM)
    hbm = pl.BlockSpec(memory_space=pl.ANY)
    return pl.pallas_call(
        kernel,
        out_shape=[jax.ShapeDtypeStruct(s, d) for s, d in outs],
        in_specs=[sm if n in smem else hbm if n in far else vmem for n in range(ins)],
        out_specs=[sm if n in out_smem else hbm if n in out_far else vmem for n in range(len(outs))],
        scratch_shapes=list(scratch),
        compiler_params=pltpu.CompilerParams(vmem_limit_bytes=limit),
        name=name,
    )


def ring_send(chips, arrays, step, swap=0):
    return [lax.ppermute(a, "dp", ring_pairs(chips, step, swap * n)) for n, a in enumerate(arrays)]


def ring_body(
    dp_count,
    features,
    norm_gain,
    w_key,
    w_value,
    queries,
    key_pool,
    value_pool,
    cache_lens,
    page_table,
    token_request,
):
    bf, f32, i32 = jnp.bfloat16, jnp.float32, jnp.int32
    chips = dp_count // 2
    offsets = ring_offsets(chips)
    rows, half_width = features.shape
    width = norm_gain.shape[0]
    toks = 2 * rows
    pages_dev = key_pool.shape[0]
    long_pages = (CTX_DEV * dp_count + PAGE - 1) // PAGE
    old = (long_pages + 2 * ((SHORT + PAGE - 1) // PAGE) + dp_count - 1) // dp_count
    group = queries.shape[1] // (2 * HD)
    columns = group * toks
    core_pairs = [(i, i ^ 1) for i in range(dp_count)]
    mp_pairs = [(0, 1), (1, 0)]
    both_pairs = [(2 * i + j, 2 * (i ^ 1) + (1 - j)) for i in range(dp_count) for j in range(2)]
    requests_tile = token_request.reshape(-1, 128)

    w_got = {0: [w_key, w_value]}
    right, left = ring_send(chips, [w_key, w_value], 1), ring_send(chips, [w_key, w_value], -1)
    w_got[-1], w_got[1] = right, left
    x_mine, x_other, q_other, kv_mine, kv_other = call(
        functools.partial(split_kernel, old),
        [
            ((rows, half_width // 2), bf),
            ((rows, half_width // 2), bf),
            ((rows, group * HD), bf),
            ((2 * old, PAGE, HD), bf),
            ((2 * old, PAGE, HD), bf),
        ],
        scratch=[pltpu.SemaphoreType.DMA((4 + 2 * (half_width // 512) + 1,))],
        ins=4,
        far=(0, 1, 2, 3),
        limit=SPLIT_LIMIT,
        name="split",
    )(features, queries, key_pool, value_pool)
    x_b = lax.ppermute(x_mine, "mp", mp_pairs)
    x_c = lax.ppermute(x_other, "dp", core_pairs)
    x_d = lax.ppermute(x_other, ("dp", "mp"), both_pairs)
    q_got = lax.ppermute(q_other, "dp", core_pairs)
    kv_got = lax.ppermute(kv_other, "dp", core_pairs)
    early = (x_b, x_c, x_d, q_got, kv_got)
    for d in range(2, chips // 2):
        if d == chips // 2 - 1:
            right, left, early = lax.optimization_barrier((right, left, early))
            x_b, x_c, x_d, q_got, kv_got = early
        right, left = ring_send(chips, right, 1), ring_send(chips, left, -1)
        w_got[-d], w_got[d] = right, left

    kv, q_rows = call(
        merge_kernel,
        [((4 * old, PAGE, HD), bf), ((columns, HD), bf)],
        ins=4,
        name="merge",
    )(kv_mine, kv_got, queries, q_got)
    inverse = (THETA ** (-(np.arange(HD) % (HD // 2)) * 2.0 / HD)).astype(np.float32)[None, :]
    scaled, squares, cosine, sine = call(
        functools.partial(scale_kernel, chips),
        [((chips, toks, 256), bf), ((toks, 128), f32), ((toks, HD), f32), ((toks, HD), f32)],
        ins=8,
        smem=(0,),
        name="scale",
    )(
        cache_lens,
        requests_tile,
        jnp.asarray(inverse),
        norm_gain.reshape(1, -1),
        x_mine,
        x_b,
        x_c,
        x_d,
    )
    right, left, scaled, kv, q_rows = lax.optimization_barrier((right, left, scaled, kv, q_rows))
    w_got[chips // 2] = ring_send(chips, right[:1], 1) + ring_send(chips, left[1:], -1)
    part_send, part_keep = call(
        functools.partial(project_kernel, chips),
        [((toks, 3 * HD), f32), ((toks, 3 * HD), f32)],
        scratch=[pltpu.VMEM((toks, 4 * HD), f32)],
        ins=2 + 2 * chips,
        name="project",
    )(scaled, squares, *[w_got[o][0] for o in offsets], *[w_got[o][1] for o in offsets])
    part_got = lax.ppermute(part_send, "dp", core_pairs)

    kv_late, _ = lax.optimization_barrier((kv, part_send))
    kv_got = {0: kv}
    kv_got[-1], kv_got[1] = ring_send(chips, [kv_late], 1)[0], ring_send(chips, [kv_late], -1)[0]
    (fresh,) = call(
        functools.partial(rotate_kernel, width),
        [((toks, 2 * HD), bf)],
        ins=4,
        name="rotary",
    )(part_keep, part_got, cosine, sine)
    new = {0: fresh}
    new[-1], new[1] = ring_send(chips, [fresh], 1)[0], ring_send(chips, [fresh], -1)[0]
    for d in range(2, chips // 2):
        right, left, _ = lax.optimization_barrier((kv_got[1 - d], kv_got[d - 1], (new[1 - d], new[d - 1])))
        new[-d], new[d] = ring_send(chips, [new[1 - d]], 1)[0], ring_send(chips, [new[d - 1]], -1)[0]
        kv_got[-d], kv_got[d] = ring_send(chips, [right], 1)[0], ring_send(chips, [left], -1)[0]
    last = chips // 2
    (kv_got[last],) = ring_send(chips, [kv_got[1 - last]], 1)

    first = [o for o in offsets if abs(o) <= last - 2]
    rest = [o for o in offsets if abs(o) > last - 2]

    def buffers(count):
        slots = 2 * old * count + STEP_PAGES
        return [pltpu.VMEM((slots * PAGE, HD), bf)] * 2

    table = pltpu.SMEM((dp_count * pages_dev,), i32)
    top, total, acc = call(
        functools.partial(cached_kernel, chips, pages_dev, old, first),
        [((1, columns), f32), ((1, columns), f32), ((HD, columns), f32)],
        scratch=[*buffers(len(first)), table],
        ins=4 + len(first),
        smem=(0, 1),
        name="attend_cached",
    )(cache_lens, page_table, requests_tile, q_rows, *[kv_got[o] for o in first])
    before, top, total, acc = lax.optimization_barrier((new[last - 1], top, total, acc))
    (new[last],) = ring_send(chips, [before], -1)

    att_other, att_mine, rows_other, rows_mine, info = call(
        functools.partial(fresh_kernel, chips, pages_dev, old, rest),
        [
            ((rows, group * HD), bf),
            ((rows, group * HD), bf),
            ((pages_dev, PAGE, 2 * HD), bf),
            ((pages_dev, PAGE, 2 * HD), bf),
            ((2 * pages_dev,), i32),
        ],
        scratch=[
            *buffers(len(rest)),
            pltpu.VMEM(((chips + 2) * toks, 2 * HD), bf),
            pltpu.VMEM((1, columns), f32),
            pltpu.VMEM((1, columns), f32),
            pltpu.VMEM((HD, columns), f32),
            pltpu.VMEM((toks, group * HD), bf),
            table,
            table,
            table,
            table,
        ],
        ins=7 + len(rest) + chips,
        smem=(0, 1),
        out_smem=(4,),
        name="attend_new",
    )(
        cache_lens,
        page_table,
        requests_tile,
        q_rows,
        top,
        total,
        acc,
        *[kv_got[o] for o in rest],
        *[new[o] for o in offsets],
    )
    rows_got = lax.ppermute(rows_other, "dp", core_pairs)
    att_got = lax.ppermute(att_other, "dp", core_pairs)
    attended, keys_out, values_out = call(
        join_kernel,
        [(queries.shape, bf), (key_pool.shape, bf), (value_pool.shape, bf)],
        ins=7,
        smem=(0,),
        name="join",
    )(info, att_mine, att_got, rows_mine, rows_got, key_pool, value_pool)
    return attended, keys_out, values_out


def solution(mesh):
    in_specs = (
        P("dp", "mp"),
        P(),
        P("dp", "mp"),
        P("dp", "mp"),
        P("dp", "mp"),
        P("dp", None, "mp"),
        P("dp", None, "mp"),
        P(),
        P(),
        P(),
    )
    out_specs = (P("dp", "mp"), P("dp", None, "mp"), P("dp", None, "mp"))
    dp_count, mp_count = mesh.shape["dp"], mesh.shape["mp"]

    def body(*args):
        even = mp_count == 2 and dp_count % 8 == 0 and dp_count & (dp_count - 1) == 0
        if even and args[2].shape == (256, 2 * HD):
            return ring_body(dp_count, *args)
        return general_body(*args)

    return jax.shard_map(body, mesh=mesh, in_specs=in_specs, out_specs=out_specs, check_vma=False)
```

```python
import functools
import math

import jax
import jax.numpy as jnp
import numpy as np
from jax import lax
from jax.experimental import pallas as pl
from jax.experimental.pallas import tpu as pltpu
from jax.sharding import PartitionSpec as P

HD = 128
PAGE = 128
SHORT = 512
CTX_DEV = 120


THETA = 500000.0
NEG_FILL = -1e30
NEG_START = -1e29
LOG2E = 1.4426950408889634
VMEM_LIMIT = 32 * 1024 * 1024
SPLIT_LIMIT = 63 * 1024 * 1024
STEP_PAGES = 4


def rotate(values, positions, head_size):
    halfway = head_size // 2
    inverse = THETA ** (-(jnp.arange(halfway, dtype=jnp.float32) * 2.0) / head_size)
    angles = positions.astype(jnp.float32)[:, None] * inverse[None, :]
    cosine = jnp.cos(angles)[:, None, :]
    sine = jnp.sin(angles)[:, None, :]
    first_half = values[..., :halfway]
    second_half = values[..., halfway:]
    return jnp.concatenate(
        [first_half * cosine - second_half * sine, second_half * cosine + first_half * sine],
        axis=-1,
    )


def general_body(
    features,
    norm_gain,
    w_key,
    w_value,
    queries,
    key_pool,
    value_pool,
    cache_lens,
    page_table,
    token_request,
):
    gathered = lax.all_gather(features, "mp", axis=1, tiled=True)
    widened = gathered.astype(jnp.float32)
    mean_square = jnp.mean(widened * widened, axis=1, keepdims=True)
    normed = (widened * lax.rsqrt(mean_square + 1e-05) * norm_gain.astype(jnp.float32)).astype(
        jnp.bfloat16
    )
    tok_rows = features.shape[0]
    kv_width = w_key.shape[1]
    head_size = HD
    kv_heads = kv_width // head_size
    q_heads = queries.shape[1] // head_size
    group_size = q_heads // kv_heads
    scale = 1.0 / math.sqrt(head_size)
    pieces = (
        lax.all_gather(w_key, "dp", axis=0, tiled=True),
        lax.all_gather(w_value, "dp", axis=0, tiled=True),
    )
    key_sums = jnp.dot(normed, pieces[0], preferred_element_type=jnp.float32)
    value_sums = jnp.dot(normed, pieces[1], preferred_element_type=jnp.float32)
    total_new = token_request.shape[0]
    requests = cache_lens.shape[0]
    request_ids = jnp.arange(requests, dtype=jnp.int32)
    member = (token_request[:, None] == request_ids[None, :]).astype(jnp.int32)
    counts = jnp.sum(member, axis=0)
    starts = jnp.cumsum(counts) - counts
    token_index = jnp.arange(total_new, dtype=jnp.int32)
    token_pos = jnp.sum(member * (cache_lens - starts)[None, :], axis=1) + token_index
    dp_index = lax.axis_index("dp")
    dp_count = lax.axis_size("dp")
    first_token = dp_index * tok_rows
    my_request = lax.dynamic_slice_in_dim(token_request, first_token, tok_rows)
    my_pos = lax.dynamic_slice_in_dim(token_pos, first_token, tok_rows)
    key_heads = rotate(key_sums.reshape(tok_rows, kv_heads, head_size), my_pos, head_size)
    new_keys = key_heads.reshape(tok_rows, kv_width).astype(jnp.bfloat16)
    new_values = value_sums.astype(jnp.bfloat16)
    pages_dev = key_pool.shape[0]
    page_rows = key_pool.shape[1]
    max_pages = page_table.shape[1]
    slot_all = jnp.take(page_table.reshape(-1), token_request * max_pages + token_pos // page_rows)
    local_slot = slot_all - dp_index * pages_dev
    owned = (local_slot >= 0) & (local_slot < pages_dev)
    dest_all = jnp.where(
        owned, local_slot * page_rows + token_pos % page_rows, pages_dev * page_rows
    )
    long_pages = (CTX_DEV * dp_count + PAGE - 1) // PAGE
    old_dev = (long_pages + 2 * ((SHORT + PAGE - 1) // PAGE) + dp_count - 1) // dp_count
    old_total = old_dev * dp_count
    old_ids = jnp.arange(old_total, dtype=jnp.int32)
    old_phys = old_ids // old_dev * pages_dev + old_ids % old_dev
    matches = (page_table[None, :, :] == old_phys[:, None, None]).astype(jnp.int32)
    page_has = jnp.sum(matches, axis=(1, 2)) > 0
    page_request = jnp.sum(matches * request_ids[None, :, None], axis=(1, 2))
    page_logical = jnp.sum(
        matches * jnp.arange(max_pages, dtype=jnp.int32)[None, None, :], axis=(1, 2)
    )
    page_limit = jnp.sum(matches * cache_lens[None, :, None], axis=(1, 2))
    q_local = queries.reshape(tok_rows, kv_heads, group_size, head_size)

    def attend(att_state, keys_flat, values_flat, key_info):
        key_request, key_pos, key_ok = key_info
        visible = (
            key_ok[None, :]
            & (key_request[None, :] == my_request[:, None])
            & (key_pos[None, :] <= my_pos[:, None])
        )
        keys_shaped = keys_flat.reshape(keys_flat.shape[0], kv_heads, head_size)
        values_shaped = values_flat.reshape(values_flat.shape[0], kv_heads, head_size)
        running_max, running_sum, running_acc = att_state
        scores = (
            jnp.einsum("thgd,khd->thgk", q_local, keys_shaped, preferred_element_type=jnp.float32)
            * scale
        )
        mask_full = visible[:, None, None, :]
        masked = jnp.where(mask_full, scores, NEG_FILL)
        new_max = jnp.maximum(running_max, jnp.max(masked, axis=-1))
        factor = jnp.exp(running_max - new_max)
        soft_weights = jnp.where(mask_full, jnp.exp(masked - new_max[..., None]), 0.0)
        new_sum = running_sum * factor + jnp.sum(soft_weights, axis=-1)
        new_acc = running_acc * factor[..., None] + jnp.einsum(
            "thgk,khd->thgd",
            soft_weights.astype(jnp.bfloat16),
            values_shaped,
            preferred_element_type=jnp.float32,
        )
        return (new_max, new_sum, new_acc)

    def attend_rows(att_state, keys_flat, values_flat, key_info):
        row_count = keys_flat.shape[0]
        key_block = 2048
        if row_count > key_block and row_count % key_block == 0:
            blocks = row_count // key_block
            stacked = (
                keys_flat.reshape(blocks, key_block, kv_width),
                values_flat.reshape(blocks, key_block, kv_width),
                key_info[0].reshape(blocks, key_block),
                key_info[1].reshape(blocks, key_block),
                key_info[2].reshape(blocks, key_block),
            )

            def step_block(inner_state, slab_parts):
                return (
                    attend(
                        inner_state,
                        slab_parts[0],
                        slab_parts[1],
                        (slab_parts[2], slab_parts[3], slab_parts[4]),
                    ),
                    None,
                )

            att_state, unused = lax.scan(step_block, att_state, stacked)
            return att_state
        return attend(att_state, keys_flat, values_flat, key_info)

    start_state = (
        jnp.full((tok_rows, kv_heads, group_size), NEG_FILL, jnp.float32),
        jnp.zeros((tok_rows, kv_heads, group_size), jnp.float32),
        jnp.zeros((tok_rows, kv_heads, group_size, head_size), jnp.float32),
    )
    flat_keys = key_pool.reshape(pages_dev * page_rows, kv_width)
    flat_values = value_pool.reshape(pages_dev * page_rows, kv_width)
    old_keys = key_pool[:old_dev]
    old_values = value_pool[:old_dev]
    pieces = (
        lax.all_gather(old_keys, "dp", axis=0, tiled=True),
        lax.all_gather(old_values, "dp", axis=0, tiled=True),
    )
    page_count = pieces[0].shape[0]
    cached_keys = pieces[0].reshape(page_count * page_rows, kv_width)
    cached_values = pieces[1].reshape(page_count * page_rows, kv_width)
    row_ids = jnp.arange(page_rows, dtype=jnp.int32)[None, :]
    key_pos = page_logical[:, None] * page_rows + row_ids
    key_ok = page_has[:, None] & (key_pos < page_limit[:, None])
    key_request = jnp.broadcast_to(page_request[:, None], (page_count, page_rows))
    middle_state = attend_rows(
        start_state,
        cached_keys,
        cached_values,
        (key_request.reshape(-1), key_pos.reshape(-1), key_ok.reshape(-1)),
    )
    pieces = (
        lax.all_gather(new_keys, "dp", axis=0, tiled=True),
        lax.all_gather(new_values, "dp", axis=0, tiled=True),
    )
    att_state = middle_state
    pool_keys = flat_keys
    pool_values = flat_values
    key_request = token_request
    key_pos = token_pos
    att_state = attend_rows(
        att_state,
        pieces[0],
        pieces[1],
        (key_request, key_pos, jnp.ones((pieces[0].shape[0],), jnp.bool_)),
    )
    pool_keys, pool_values = (
        pool_keys.at[dest_all].set(pieces[0], mode="drop"),
        pool_values.at[dest_all].set(pieces[1], mode="drop"),
    )
    final_state, pool_keys, pool_values = (att_state, pool_keys, pool_values)
    final_max, final_sum, final_acc = final_state
    attended = (
        (final_acc / final_sum[..., None])
        .reshape(tok_rows, q_heads * head_size)
        .astype(jnp.bfloat16)
    )
    return (attended, pool_keys.reshape(key_pool.shape), pool_values.reshape(value_pool.shape))


def ring_chip(pos, chips):
    pos = pos % chips
    return jnp.where(pos < chips // 2, 2 * pos, 2 * chips - 1 - 2 * pos)


def ring_place(chip, chips):
    return jnp.where(chip % 2 == 0, chip // 2, (2 * chips - 1 - chip) // 2)


def ring_pairs(chips, step, swap):
    order = [2 * k if k < chips // 2 else 2 * chips - 1 - 2 * k for k in range(chips)]
    return [
        (2 * order[k] + core, 2 * order[(k + step) % chips] + (core ^ swap))
        for k in range(chips)
        for core in range(2)
    ]


def ring_offsets(chips):
    return [0] + [o for d in range(1, chips // 2) for o in (d, -d)] + [chips // 2]


def request_starts(tr_ref, requests):
    tr = tr_ref[...]
    starts = [jnp.int32(0)]
    for r in range(1, requests):
        starts.append(jnp.sum(jnp.where(tr < r, 1.0, 0.0)).astype(jnp.int32))
    starts.append(jnp.int32(tr.shape[0] * tr.shape[1]))
    return starts


def pick(cond_starts, values, tokens):
    out = jnp.zeros_like(tokens) + values[0]
    for r in range(1, len(values)):
        out = jnp.where(tokens >= cond_starts[r], values[r], out)
    return out


def chip_requests(chip, toks, starts):
    first, last = jnp.int32(0), jnp.int32(0)
    for start in starts[1:-1]:
        first = first + (chip * toks >= start).astype(jnp.int32)
        last = last + (chip * toks + toks - 1 >= start).astype(jnp.int32)
    return first, last


def split_kernel(old, f_ref, q_ref, kp_ref, vp_ref, xc_ref, xo_ref, qo_ref, kvc_ref, kvo_ref, sems):
    core = lax.axis_index("dp") % 2
    copies = []

    def copy(source, target):
        copies.append(pltpu.make_async_copy(source, target, sems.at[len(copies)]))
        copies[-1].start()

    for page_ref, first in ((kp_ref, 0), (vp_ref, old)):
        for out_ref, head in ((kvo_ref, 1 - core), (kvc_ref, core)):
            at = pl.ds(pl.multiple_of(head * HD, HD), HD)
            copy(page_ref.at[pl.ds(0, old), :, at], out_ref.at[pl.ds(first, old)])
    for out_ref, own in ((xo_ref, 1 - core), (xc_ref, core)):
        for m in range(f_ref.shape[1] // 512):
            at = pl.ds(pl.multiple_of((2 * m + own) * 256, 256), 256)
            copy(f_ref.at[:, at], out_ref.at[:, pl.ds(m * 256, 256)])
    half = q_ref.shape[1] // 2
    copy(q_ref.at[:, pl.ds(pl.multiple_of((1 - core) * half, 128), half)], qo_ref)
    for c in copies:
        c.wait()


def merge_kernel(q_ref, qg_ref, qs_ref):
    core = lax.axis_index("dp") % 2
    rows, group = q_ref.shape[0], qg_ref.shape[1] // HD
    for h in range(group):
        mine = pl.ds(pl.multiple_of((2 * h + core) * rows, rows), rows)
        other = pl.ds(pl.multiple_of((2 * h + 1 - core) * rows, rows), rows)
        qs_ref[mine, :] = q_ref[:, pl.ds(pl.multiple_of((core * group + h) * HD, HD), HD)]
        qs_ref[other, :] = qg_ref[:, h * HD : (h + 1) * HD]


def scale_kernel(
    chips, lens_ref, tr_ref, inv_ref, gain_ref, a_ref, b_ref, c_ref, d_ref, xs_ref, ss_ref, cos_ref, sin_ref
):
    dp = lax.axis_index("dp")
    mp = lax.axis_index("mp")
    chip, core = dp // 2, dp % 2
    rows = a_ref.shape[0]
    per_half = a_ref.shape[1] // 256
    for first, second, owner in ((a_ref, b_ref, core), (c_ref, d_ref, 1 - core)):
        at = pl.ds(pl.multiple_of(owner * rows, rows), rows)
        total = jnp.zeros((rows, 256), jnp.float32)
        for ref, half in ((first, mp), (second, 1 - mp)):
            for m in range(per_half):
                wide = ref[:, m * 256 : (m + 1) * 256].astype(jnp.float32)
                block = half * (2 * per_half) + 2 * m + core
                gain = gain_ref[:, pl.ds(pl.multiple_of(block * 256, 256), 256)].astype(jnp.float32)
                total = total + wide * wide
                xs_ref[half * per_half + m, at, :] = (wide * gain).astype(jnp.bfloat16)
        ss_ref[at, :] = jnp.broadcast_to(jnp.sum(total, axis=1, keepdims=True), (rows, 128))
    requests = lens_ref.shape[0]
    starts = request_starts(tr_ref, requests)
    tokens = chip * (2 * rows) + lax.broadcasted_iota(jnp.int32, (2 * rows, 128), 0)
    shift = pick(starts, [lens_ref[r] - starts[r] for r in range(requests)], tokens)
    angles = (tokens + shift).astype(jnp.float32) * inv_ref[...]
    lane = lax.broadcasted_iota(jnp.int32, (2 * rows, 128), 1)
    sine = jnp.sin(angles)
    cos_ref[...] = jnp.cos(angles)
    sin_ref[...] = jnp.where(lane < HD // 2, -sine, sine)


def project_kernel(chips, xs_ref, ss_ref, *refs):
    keys, values = refs[:chips], refs[chips : 2 * chips]
    send_ref, keep_ref, acc_ref = refs[2 * chips :]
    dp = lax.axis_index("dp")
    chip, core = dp // 2, dp % 2
    place = ring_place(chip, chips)
    ksum = jnp.zeros((xs_ref.shape[1], 2 * HD), jnp.float32)
    vsum = jnp.zeros((xs_ref.shape[1], 2 * HD), jnp.float32)
    for n, offset in enumerate(ring_offsets(chips)):
        x = xs_ref[ring_chip(place + offset + chips, chips)]
        ksum = ksum + jnp.dot(x, keys[n][...], preferred_element_type=jnp.float32)
        vsum = vsum + jnp.dot(x, values[n][...], preferred_element_type=jnp.float32)
    acc_ref[:, : 2 * HD] = ksum
    acc_ref[:, 2 * HD :] = vsum
    for ref, head in ((send_ref, 1 - core), (keep_ref, core)):
        ref[:, :HD] = acc_ref[:, pl.ds(pl.multiple_of(head * HD, HD), HD)]
        ref[:, HD : 2 * HD] = acc_ref[:, pl.ds(pl.multiple_of((2 + head) * HD, HD), HD)]
        ref[:, 2 * HD :] = ss_ref[...]


def rotate_kernel(width, keep_ref, got_ref, cos_ref, sin_ref, out_ref):
    total = keep_ref[...] + got_ref[...]
    inverse = lax.rsqrt(total[:, 2 * HD :] * (1.0 / width) + 1e-05)
    key = total[:, :HD] * inverse
    rolled = pltpu.roll(key, HD // 2, 1)
    out_ref[:, :HD] = (key * cos_ref[...] + rolled * sin_ref[...]).astype(jnp.bfloat16)
    out_ref[:, HD:] = (total[:, HD : 2 * HD] * inverse).astype(jnp.bfloat16)


def attend_block(qs_ref, keys, values, first, low, high, m_ref, l_ref, acc_ref):
    scores = lax.dot_general(keys, qs_ref[...], (((1,), (1,)), ((), ())), preferred_element_type=jnp.float32)
    ids = first + lax.broadcasted_iota(jnp.int32, scores.shape, 0)
    scores = jnp.where((ids >= low) & (ids < high), scores * (LOG2E / math.sqrt(HD)), NEG_FILL)
    before = m_ref[...]
    top = jnp.maximum(before, jnp.max(scores, axis=0, keepdims=True))
    shrink = jnp.exp2(before - top)
    weights = jnp.exp2(scores - top)
    m_ref[...] = top
    l_ref[...] = l_ref[...] * shrink + jnp.sum(weights, axis=0, keepdims=True)
    acc_ref[...] = acc_ref[...] * shrink + lax.dot_general(
        values,
        weights.astype(jnp.bfloat16),
        (((0,), (0,)), ((), ())),
        preferred_element_type=jnp.float32,
    )


def three_parts(x):
    first = x.astype(jnp.bfloat16).astype(jnp.float32)
    second = (x - first).astype(jnp.bfloat16).astype(jnp.float32)
    return jnp.concatenate([first, second, x - first - second], axis=0)


def cached_kernel(chips, pages_dev, old, away, lens_ref, table_ref, tr_ref, qs_ref, *refs):
    members = chips // 2
    near, far = refs[:members], refs[members : 2 * members]
    outs, (kbuf, vbuf, m_ref, l_ref, acc_ref, slot_of) = refs[2 * members : -6], refs[-6:]
    dp = lax.axis_index("dp")
    chip, core = dp // 2, dp % 2
    who = chip ^ away
    requests = lens_ref.shape[0]
    width = qs_ref.shape[0]
    toks = tr_ref.shape[0] * tr_ref.shape[1] // chips
    starts = request_starts(tr_ref, requests)
    first_req, last_req = chip_requests(who, toks, starts)

    def clear(i, carry):
        slot_of[i] = -1
        return carry

    lax.fori_loop(0, slot_of.shape[0], clear, 0)
    base = jnp.int32(0)
    lows, highs = [], []
    for r in range(requests):
        length = lens_ref[r]
        relevant = (r >= first_req) & (r <= last_req)
        count = jnp.where(relevant, (length + PAGE - 1) // PAGE, 0)

        def place(l, at, r=r):
            page = table_ref[r, l]
            held = page // (2 * pages_dev * members) == chip // members

            @pl.when(held)
            def _():
                slot_of[page] = at

            return at + held.astype(jnp.int32)

        end = lax.fori_loop(0, count, place, base)
        last_page = table_ref[r, (length + PAGE - 1) // PAGE - 1]
        cut = jnp.where(
            (end > base) & (last_page // (2 * pages_dev * members) == chip // members),
            (length + PAGE - 1) // PAGE * PAGE - length,
            0,
        )
        lows.append(base * PAGE)
        highs.append(end * PAGE - cut)
        base = end

    for e in range(members):
        source = chip ^ e
        for block, owner in ((near[e], 2 * source + core), (far[e], 2 * source + 1 - core)):
            for s in range(old):
                slot = slot_of[owner * pages_dev + s]

                @pl.when(slot >= 0)
                def _(block=block, s=s, slot=slot):
                    at = pl.ds(pl.multiple_of(slot * PAGE, PAGE), PAGE)
                    kbuf[at, :] = block[s]
                    vbuf[at, :] = block[old + s]

    step_pages = STEP_PAGES
    pad = pl.ds(pl.multiple_of(base * PAGE, PAGE), (step_pages - 1) * PAGE)
    kbuf[pad, :] = jnp.zeros(((step_pages - 1) * PAGE, HD), kbuf.dtype)
    vbuf[pad, :] = jnp.zeros(((step_pages - 1) * PAGE, HD), vbuf.dtype)
    tokens = who * toks + lax.broadcasted_iota(jnp.int32, (1, width), 1) % toks
    low = pick(starts, lows, tokens)
    high = pick(starts, highs, tokens)
    m_ref[...] = jnp.full(m_ref.shape, NEG_START, jnp.float32)
    l_ref[...] = jnp.zeros(l_ref.shape, jnp.float32)
    acc_ref[...] = jnp.zeros(acc_ref.shape, jnp.float32)

    def step(i, carry):
        size = step_pages * PAGE
        at = pl.ds(pl.multiple_of(i * size, size), size)
        attend_block(qs_ref, kbuf[at, :], vbuf[at, :], i * size, low, high, m_ref, l_ref, acc_ref)
        return carry

    lax.fori_loop(0, (base + step_pages - 1) // step_pages, step, 0)
    if away:
        outs[0][:HD, :] = acc_ref[...].astype(jnp.bfloat16)
        outs[0][HD:, :] = jnp.concatenate(
            [three_parts(m_ref[...]), three_parts(l_ref[...]), jnp.zeros((10, width), jnp.float32)], axis=0
        ).astype(jnp.bfloat16)
    else:
        outs[0][...], outs[1][...], outs[2][...] = m_ref[...], l_ref[...], acc_ref[...]


def fresh_kernel(
    chips, pages_dev, lens_ref, table_ref, tr_ref, qs_ref, m0_ref, l0_ref, acc0_ref, back_ref, *refs
):
    fresh = refs[:chips]
    atto_ref, attc_ref, no_ref, nc_ref, info_ref = refs[chips : chips + 5]
    nbuf, m_ref, l_ref, acc_ref, out_ref, new_at, new_lo, new_hi = refs[chips + 5 :]
    dp = lax.axis_index("dp")
    chip, core = dp // 2, dp % 2
    place = ring_place(chip, chips)
    toks = fresh[0].shape[0]
    rows = toks // 2
    requests = lens_ref.shape[0]
    width = qs_ref.shape[0]
    group = width // toks
    starts = request_starts(tr_ref, requests)
    reqs = chip_requests(chip, toks, starts)
    first_req = reqs[0]
    parts = back_ref[HD : HD + 6, :].astype(jnp.float32)
    m0, m1 = m0_ref[...], parts[0:1] + parts[1:2] + parts[2:3]
    top = jnp.maximum(m0, m1)
    f0, f1 = jnp.exp2(m0 - top), jnp.exp2(m1 - top)
    m_ref[...] = top
    l_ref[...] = l0_ref[...] * f0 + (parts[3:4] + parts[4:5] + parts[5:6]) * f1
    acc_ref[...] = acc0_ref[...] * f0 + back_ref[:HD, :].astype(jnp.float32) * f1

    def clear(i, carry):
        new_lo[i] = 0
        new_hi[i] = 0
        return carry

    lax.fori_loop(0, new_lo.shape[0], clear, 0)
    for r in range(requests):
        length = lens_ref[r]

        def place_new(l, carry, r=r, length=length):
            at = l * PAGE - length + starts[r]
            page = table_ref[r, l]
            new_at[page] = at
            new_lo[page] = jnp.maximum(starts[r] - at, 0)
            new_hi[page] = jnp.minimum(starts[r + 1] - at, PAGE)
            return carry

        end = (length + starts[r + 1] - starts[r] + PAGE - 1) // PAGE
        lax.fori_loop(length // PAGE, end, place_new, 0)

    for n, offset in enumerate(ring_offsets(chips)):
        source = ring_chip(place + offset + chips, chips)
        nbuf[pl.ds(pl.multiple_of((source + 1) * toks, toks), toks), :] = fresh[n][...]
    nbuf[:toks, :] = jnp.zeros((toks, 2 * HD), nbuf.dtype)
    nbuf[(chips + 1) * toks :, :] = jnp.zeros((toks, 2 * HD), nbuf.dtype)

    tokens = chip * toks + lax.broadcasted_iota(jnp.int32, (1, width), 1) % toks
    low = pick(starts, starts[:requests], tokens)
    first_start = starts[0]
    for r in range(1, requests):
        first_start = jnp.where(first_req == r, starts[r], first_start)

    def step(b, carry):
        at = pl.ds(pl.multiple_of((b + 1) * toks, toks), toks)
        attend_block(qs_ref, nbuf[at, :HD], nbuf[at, HD:], b * toks, low, tokens + 1, m_ref, l_ref, acc_ref)
        return carry

    lax.fori_loop(first_start // toks, chip + 1, step, 0)
    result = acc_ref[...] / l_ref[...]
    for h in range(group):
        out_ref[:, h * HD : (h + 1) * HD] = result[:, h * toks : (h + 1) * toks].T.astype(jnp.bfloat16)
    attc_ref[...] = out_ref[pl.ds(pl.multiple_of(core * rows, rows), rows), :]
    atto_ref[...] = out_ref[pl.ds(pl.multiple_of((1 - core) * rows, rows), rows), :]

    row = lax.broadcasted_iota(jnp.int32, (PAGE, 2 * toks), 0)
    column = lax.broadcasted_iota(jnp.int32, (PAGE, 2 * toks), 1)
    for ref, owner in ((no_ref, dp + 1 - 2 * core), (nc_ref, dp)):
        for s in range(pages_dev):
            page = owner * pages_dev + s
            at, low_row, high_row = new_at[page], new_lo[page], new_hi[page]

            @pl.when(high_row > low_row)
            def _(ref=ref, s=s, at=at, low_row=low_row, high_row=high_row):
                shifted = at + toks
                first = pl.multiple_of(shifted // toks * toks, toks)
                chosen = (column + first == row + shifted) & (row >= low_row) & (row < high_row)
                ref[s] = jnp.dot(
                    jnp.where(chosen, 1.0, 0.0).astype(jnp.bfloat16),
                    nbuf[pl.ds(first, 2 * toks), :],
                    preferred_element_type=jnp.float32,
                ).astype(jnp.bfloat16)

    for s in range(pages_dev):
        info_ref[2 * s] = new_lo[dp * pages_dev + s]
        info_ref[2 * s + 1] = new_hi[dp * pages_dev + s]


def join_kernel(info_ref, attc_ref, attr_ref, nc_ref, nr_ref, kp_ref, vp_ref, att_ref, ko_ref, vo_ref):
    core = lax.axis_index("dp") % 2
    half = attc_ref.shape[1]
    att_ref[:, pl.ds(pl.multiple_of(core * half, HD), half)] = attc_ref[...]
    att_ref[:, pl.ds(pl.multiple_of((1 - core) * half, HD), half)] = attr_ref[...]
    row = lax.broadcasted_iota(jnp.int32, (PAGE, HD), 0)
    for s in range(kp_ref.shape[0]):
        chosen = (row >= info_ref[2 * s]) & (row < info_ref[2 * s + 1])
        for ref, head in ((nc_ref, core), (nr_ref, 1 - core)):
            at = pl.ds(pl.multiple_of(head * HD, HD), HD)
            ko_ref[s, :, at] = jnp.where(chosen, ref[s, :, :HD], kp_ref[s, :, at])
            vo_ref[s, :, at] = jnp.where(chosen, ref[s, :, HD:], vp_ref[s, :, at])


def call(
    kernel, outs, scratch=(), ins=None, smem=(), far=(), out_smem=(), out_far=(), limit=VMEM_LIMIT, name=None
):
    vmem, sm = pl.BlockSpec(memory_space=pltpu.VMEM), pl.BlockSpec(memory_space=pltpu.SMEM)
    hbm = pl.BlockSpec(memory_space=pl.ANY)
    return pl.pallas_call(
        kernel,
        out_shape=[jax.ShapeDtypeStruct(s, d) for s, d in outs],
        in_specs=[sm if n in smem else hbm if n in far else vmem for n in range(ins)],
        out_specs=[sm if n in out_smem else hbm if n in out_far else vmem for n in range(len(outs))],
        scratch_shapes=list(scratch),
        compiler_params=pltpu.CompilerParams(vmem_limit_bytes=limit),
        name=name,
    )


def ring_send(chips, arrays, step, swap=0):
    return [lax.ppermute(a, "dp", ring_pairs(chips, step, swap * n)) for n, a in enumerate(arrays)]


def ring_body(
    dp_count,
    features,
    norm_gain,
    w_key,
    w_value,
    queries,
    key_pool,
    value_pool,
    cache_lens,
    page_table,
    token_request,
):
    bf, f32, i32 = jnp.bfloat16, jnp.float32, jnp.int32
    chips = dp_count // 2
    offsets = ring_offsets(chips)
    rows, half_width = features.shape
    width = norm_gain.shape[0]
    toks = 2 * rows
    pages_dev = key_pool.shape[0]
    long_pages = (CTX_DEV * dp_count + PAGE - 1) // PAGE
    old = (long_pages + 2 * ((SHORT + PAGE - 1) // PAGE) + dp_count - 1) // dp_count
    group = queries.shape[1] // (2 * HD)
    columns = group * toks
    core_pairs = [(i, i ^ 1) for i in range(dp_count)]
    mp_pairs = [(0, 1), (1, 0)]
    both_pairs = [(2 * i + j, 2 * (i ^ 1) + (1 - j)) for i in range(dp_count) for j in range(2)]
    requests_tile = token_request.reshape(-1, 128)

    def exchange(array, e, swap=0):
        return lax.ppermute(array, "dp", [(i, i ^ (2 * e) ^ swap) for i in range(dp_count)])

    w_got = {0: [w_key, w_value]}
    right, left = ring_send(chips, [w_key, w_value], 1), ring_send(chips, [w_key, w_value], -1)
    w_got[-1], w_got[1] = right, left
    x_mine, x_other, q_other, kv_mine, kv_other = call(
        functools.partial(split_kernel, old),
        [
            ((rows, half_width // 2), bf),
            ((rows, half_width // 2), bf),
            ((rows, group * HD), bf),
            ((2 * old, PAGE, HD), bf),
            ((2 * old, PAGE, HD), bf),
        ],
        scratch=[pltpu.SemaphoreType.DMA((4 + 2 * (half_width // 512) + 1,))],
        ins=4,
        far=(0, 1, 2, 3),
        limit=SPLIT_LIMIT,
        name="split",
    )(features, queries, key_pool, value_pool)
    x_b = lax.ppermute(x_mine, "mp", mp_pairs)
    x_c = lax.ppermute(x_other, "dp", core_pairs)
    x_d = lax.ppermute(x_other, ("dp", "mp"), both_pairs)
    q_got = lax.ppermute(q_other, "dp", core_pairs)
    kv_got = lax.ppermute(kv_other, "dp", core_pairs)
    z_near, z_far = exchange(kv_mine, 2), exchange(kv_other, 2, 1)
    y_near, y_far = exchange(kv_mine, 1), exchange(kv_other, 1, 1)
    for d in range(2, chips // 2):
        if d == chips // 2 - 1:
            w_first, z_near, z_far, y_near, y_far, q_got = lax.optimization_barrier(
                (right[0], z_near, z_far, y_near, y_far, q_got)
            )
            right = [w_first, right[1]]
        right, left = ring_send(chips, right, 1), ring_send(chips, left, -1)
        w_got[-d], w_got[d] = right, left
    near = [kv_mine, y_near, z_near, exchange(y_near, 2)]
    far = [kv_got, y_far, z_far, exchange(z_far, 1)]

    (q_rows,) = call(merge_kernel, [((columns, HD), bf)], ins=2, name="merge")(queries, q_got)
    q_away = exchange(q_rows, chips // 2)
    inverse = (THETA ** (-(np.arange(HD) % (HD // 2)) * 2.0 / HD)).astype(np.float32)[None, :]
    scaled, squares, cosine, sine = call(
        functools.partial(scale_kernel, chips),
        [((chips, toks, 256), bf), ((toks, 128), f32), ((toks, HD), f32), ((toks, HD), f32)],
        ins=8,
        smem=(0,),
        name="scale",
    )(
        cache_lens,
        requests_tile,
        jnp.asarray(inverse),
        norm_gain.reshape(1, -1),
        x_mine,
        x_b,
        x_c,
        x_d,
    )
    w_got[chips // 2] = ring_send(chips, right[:1], 1) + ring_send(chips, left[1:], -1)
    scaled, near[3], far[3], q_away = lax.optimization_barrier((scaled, near[3], far[3], q_away))
    part_send, part_keep = call(
        functools.partial(project_kernel, chips),
        [((toks, 3 * HD), f32), ((toks, 3 * HD), f32)],
        scratch=[pltpu.VMEM((toks, 4 * HD), f32)],
        ins=2 + 2 * chips,
        name="project",
    )(scaled, squares, *[w_got[o][0] for o in offsets], *[w_got[o][1] for o in offsets])
    part_got = lax.ppermute(part_send, "dp", core_pairs)

    (fresh,) = call(
        functools.partial(rotate_kernel, width),
        [((toks, 2 * HD), bf)],
        ins=4,
        name="rotary",
    )(part_keep, part_got, cosine, sine)
    new = {0: fresh}
    new[-1], new[1] = ring_send(chips, [fresh], 1)[0], ring_send(chips, [fresh], -1)[0]
    slots = dp_count // 2 * old + STEP_PAGES
    table = pltpu.SMEM((dp_count * pages_dev,), i32)

    def cached(q, away, outs, name):
        return call(
            functools.partial(cached_kernel, chips, pages_dev, old, away),
            outs,
            scratch=[
                pltpu.VMEM((slots * PAGE, HD), bf),
                pltpu.VMEM((slots * PAGE, HD), bf),
                pltpu.VMEM((1, columns), f32),
                pltpu.VMEM((1, columns), f32),
                pltpu.VMEM((HD, columns), f32),
                table,
            ],
            ins=4 + chips,
            smem=(0, 1),
            name=name,
        )(cache_lens, page_table, requests_tile, q, *near, *far)

    (away,) = cached(q_away, chips // 2, [((HD + 16, columns), bf)], "attend_cached_away")
    here = cached(
        q_rows, 0, [((1, columns), f32), ((1, columns), f32), ((HD, columns), f32)], "attend_cached_here"
    )
    beside = {2: away, 3: here}
    for d in range(2, chips // 2):
        right, left, beside[d] = lax.optimization_barrier((new[1 - d], new[d - 1], beside[d]))
        new[-d], new[d] = ring_send(chips, [right], 1)[0], ring_send(chips, [left], -1)[0]
    (new[chips // 2],) = ring_send(chips, [new[1 - chips // 2]], 1)
    back = exchange(beside[2], chips // 2)
    top, total, acc = beside[3]

    att_other, att_mine, rows_other, rows_mine, info = call(
        functools.partial(fresh_kernel, chips, pages_dev),
        [
            ((rows, group * HD), bf),
            ((rows, group * HD), bf),
            ((pages_dev, PAGE, 2 * HD), bf),
            ((pages_dev, PAGE, 2 * HD), bf),
            ((2 * pages_dev,), i32),
        ],
        scratch=[
            pltpu.VMEM(((chips + 2) * toks, 2 * HD), bf),
            pltpu.VMEM((1, columns), f32),
            pltpu.VMEM((1, columns), f32),
            pltpu.VMEM((HD, columns), f32),
            pltpu.VMEM((toks, group * HD), bf),
            table,
            table,
            table,
        ],
        ins=8 + chips,
        smem=(0, 1),
        out_smem=(4,),
        name="attend_new",
    )(
        cache_lens,
        page_table,
        requests_tile,
        q_rows,
        top,
        total,
        acc,
        back,
        *[new[o] for o in offsets],
    )
    rows_got = lax.ppermute(rows_other, "dp", core_pairs)
    att_got = lax.ppermute(att_other, "dp", core_pairs)
    attended, keys_out, values_out = call(
        join_kernel,
        [(queries.shape, bf), (key_pool.shape, bf), (value_pool.shape, bf)],
        ins=7,
        smem=(0,),
        name="join",
    )(info, att_mine, att_got, rows_mine, rows_got, key_pool, value_pool)
    return attended, keys_out, values_out


def solution(mesh):
    in_specs = (
        P("dp", "mp"),
        P(),
        P("dp", "mp"),
        P("dp", "mp"),
        P("dp", "mp"),
        P("dp", None, "mp"),
        P("dp", None, "mp"),
        P(),
        P(),
        P(),
    )
    out_specs = (P("dp", "mp"), P("dp", None, "mp"), P("dp", None, "mp"))
    dp_count, mp_count = mesh.shape["dp"], mesh.shape["mp"]

    def body(*args):
        even = mp_count == 2 and dp_count == 16
        if even and args[2].shape == (256, 2 * HD):
            return ring_body(dp_count, *args)
        return general_body(*args)

    return jax.shard_map(body, mesh=mesh, in_specs=in_specs, out_specs=out_specs, check_vma=False)
```

```python
import functools
import math

import jax
import jax.numpy as jnp
import numpy as np
from jax import lax
from jax.experimental import pallas as pl
from jax.experimental.pallas import tpu as pltpu
from jax.sharding import PartitionSpec as P

HD = 128
PAGE = 128
SHORT = 512
CTX_DEV = 120


THETA = 500000.0
NEG_FILL = -1e30
NEG_START = -1e29
LOG2E = 1.4426950408889634
VMEM_LIMIT = 32 * 1024 * 1024
SPLIT_LIMIT = 63 * 1024 * 1024
STEP_PAGES = 4


def rotate(values, positions, head_size):
    halfway = head_size // 2
    inverse = THETA ** (-(jnp.arange(halfway, dtype=jnp.float32) * 2.0) / head_size)
    angles = positions.astype(jnp.float32)[:, None] * inverse[None, :]
    cosine = jnp.cos(angles)[:, None, :]
    sine = jnp.sin(angles)[:, None, :]
    first_half = values[..., :halfway]
    second_half = values[..., halfway:]
    return jnp.concatenate(
        [first_half * cosine - second_half * sine, second_half * cosine + first_half * sine],
        axis=-1,
    )


def general_body(
    features,
    norm_gain,
    w_key,
    w_value,
    queries,
    key_pool,
    value_pool,
    cache_lens,
    page_table,
    token_request,
):
    gathered = lax.all_gather(features, "mp", axis=1, tiled=True)
    widened = gathered.astype(jnp.float32)
    mean_square = jnp.mean(widened * widened, axis=1, keepdims=True)
    normed = (widened * lax.rsqrt(mean_square + 1e-05) * norm_gain.astype(jnp.float32)).astype(
        jnp.bfloat16
    )
    tok_rows = features.shape[0]
    kv_width = w_key.shape[1]
    head_size = HD
    kv_heads = kv_width // head_size
    q_heads = queries.shape[1] // head_size
    group_size = q_heads // kv_heads
    scale = 1.0 / math.sqrt(head_size)
    pieces = (
        lax.all_gather(w_key, "dp", axis=0, tiled=True),
        lax.all_gather(w_value, "dp", axis=0, tiled=True),
    )
    key_sums = jnp.dot(normed, pieces[0], preferred_element_type=jnp.float32)
    value_sums = jnp.dot(normed, pieces[1], preferred_element_type=jnp.float32)
    total_new = token_request.shape[0]
    requests = cache_lens.shape[0]
    request_ids = jnp.arange(requests, dtype=jnp.int32)
    member = (token_request[:, None] == request_ids[None, :]).astype(jnp.int32)
    counts = jnp.sum(member, axis=0)
    starts = jnp.cumsum(counts) - counts
    token_index = jnp.arange(total_new, dtype=jnp.int32)
    token_pos = jnp.sum(member * (cache_lens - starts)[None, :], axis=1) + token_index
    dp_index = lax.axis_index("dp")
    dp_count = lax.axis_size("dp")
    first_token = dp_index * tok_rows
    my_request = lax.dynamic_slice_in_dim(token_request, first_token, tok_rows)
    my_pos = lax.dynamic_slice_in_dim(token_pos, first_token, tok_rows)
    key_heads = rotate(key_sums.reshape(tok_rows, kv_heads, head_size), my_pos, head_size)
    new_keys = key_heads.reshape(tok_rows, kv_width).astype(jnp.bfloat16)
    new_values = value_sums.astype(jnp.bfloat16)
    pages_dev = key_pool.shape[0]
    page_rows = key_pool.shape[1]
    max_pages = page_table.shape[1]
    slot_all = jnp.take(page_table.reshape(-1), token_request * max_pages + token_pos // page_rows)
    local_slot = slot_all - dp_index * pages_dev
    owned = (local_slot >= 0) & (local_slot < pages_dev)
    dest_all = jnp.where(
        owned, local_slot * page_rows + token_pos % page_rows, pages_dev * page_rows
    )
    long_pages = (CTX_DEV * dp_count + PAGE - 1) // PAGE
    old_dev = (long_pages + 2 * ((SHORT + PAGE - 1) // PAGE) + dp_count - 1) // dp_count
    old_total = old_dev * dp_count
    old_ids = jnp.arange(old_total, dtype=jnp.int32)
    old_phys = old_ids // old_dev * pages_dev + old_ids % old_dev
    matches = (page_table[None, :, :] == old_phys[:, None, None]).astype(jnp.int32)
    page_has = jnp.sum(matches, axis=(1, 2)) > 0
    page_request = jnp.sum(matches * request_ids[None, :, None], axis=(1, 2))
    page_logical = jnp.sum(
        matches * jnp.arange(max_pages, dtype=jnp.int32)[None, None, :], axis=(1, 2)
    )
    page_limit = jnp.sum(matches * cache_lens[None, :, None], axis=(1, 2))
    q_local = queries.reshape(tok_rows, kv_heads, group_size, head_size)

    def attend(att_state, keys_flat, values_flat, key_info):
        key_request, key_pos, key_ok = key_info
        visible = (
            key_ok[None, :]
            & (key_request[None, :] == my_request[:, None])
            & (key_pos[None, :] <= my_pos[:, None])
        )
        keys_shaped = keys_flat.reshape(keys_flat.shape[0], kv_heads, head_size)
        values_shaped = values_flat.reshape(values_flat.shape[0], kv_heads, head_size)
        running_max, running_sum, running_acc = att_state
        scores = (
            jnp.einsum("thgd,khd->thgk", q_local, keys_shaped, preferred_element_type=jnp.float32)
            * scale
        )
        mask_full = visible[:, None, None, :]
        masked = jnp.where(mask_full, scores, NEG_FILL)
        new_max = jnp.maximum(running_max, jnp.max(masked, axis=-1))
        factor = jnp.exp(running_max - new_max)
        soft_weights = jnp.where(mask_full, jnp.exp(masked - new_max[..., None]), 0.0)
        new_sum = running_sum * factor + jnp.sum(soft_weights, axis=-1)
        new_acc = running_acc * factor[..., None] + jnp.einsum(
            "thgk,khd->thgd",
            soft_weights.astype(jnp.bfloat16),
            values_shaped,
            preferred_element_type=jnp.float32,
        )
        return (new_max, new_sum, new_acc)

    def attend_rows(att_state, keys_flat, values_flat, key_info):
        row_count = keys_flat.shape[0]
        key_block = 2048
        if row_count > key_block and row_count % key_block == 0:
            blocks = row_count // key_block
            stacked = (
                keys_flat.reshape(blocks, key_block, kv_width),
                values_flat.reshape(blocks, key_block, kv_width),
                key_info[0].reshape(blocks, key_block),
                key_info[1].reshape(blocks, key_block),
                key_info[2].reshape(blocks, key_block),
            )

            def step_block(inner_state, slab_parts):
                return (
                    attend(
                        inner_state,
                        slab_parts[0],
                        slab_parts[1],
                        (slab_parts[2], slab_parts[3], slab_parts[4]),
                    ),
                    None,
                )

            att_state, unused = lax.scan(step_block, att_state, stacked)
            return att_state
        return attend(att_state, keys_flat, values_flat, key_info)

    start_state = (
        jnp.full((tok_rows, kv_heads, group_size), NEG_FILL, jnp.float32),
        jnp.zeros((tok_rows, kv_heads, group_size), jnp.float32),
        jnp.zeros((tok_rows, kv_heads, group_size, head_size), jnp.float32),
    )
    flat_keys = key_pool.reshape(pages_dev * page_rows, kv_width)
    flat_values = value_pool.reshape(pages_dev * page_rows, kv_width)
    old_keys = key_pool[:old_dev]
    old_values = value_pool[:old_dev]
    pieces = (
        lax.all_gather(old_keys, "dp", axis=0, tiled=True),
        lax.all_gather(old_values, "dp", axis=0, tiled=True),
    )
    page_count = pieces[0].shape[0]
    cached_keys = pieces[0].reshape(page_count * page_rows, kv_width)
    cached_values = pieces[1].reshape(page_count * page_rows, kv_width)
    row_ids = jnp.arange(page_rows, dtype=jnp.int32)[None, :]
    key_pos = page_logical[:, None] * page_rows + row_ids
    key_ok = page_has[:, None] & (key_pos < page_limit[:, None])
    key_request = jnp.broadcast_to(page_request[:, None], (page_count, page_rows))
    middle_state = attend_rows(
        start_state,
        cached_keys,
        cached_values,
        (key_request.reshape(-1), key_pos.reshape(-1), key_ok.reshape(-1)),
    )
    pieces = (
        lax.all_gather(new_keys, "dp", axis=0, tiled=True),
        lax.all_gather(new_values, "dp", axis=0, tiled=True),
    )
    att_state = middle_state
    pool_keys = flat_keys
    pool_values = flat_values
    key_request = token_request
    key_pos = token_pos
    att_state = attend_rows(
        att_state,
        pieces[0],
        pieces[1],
        (key_request, key_pos, jnp.ones((pieces[0].shape[0],), jnp.bool_)),
    )
    pool_keys, pool_values = (
        pool_keys.at[dest_all].set(pieces[0], mode="drop"),
        pool_values.at[dest_all].set(pieces[1], mode="drop"),
    )
    final_state, pool_keys, pool_values = (att_state, pool_keys, pool_values)
    final_max, final_sum, final_acc = final_state
    attended = (
        (final_acc / final_sum[..., None])
        .reshape(tok_rows, q_heads * head_size)
        .astype(jnp.bfloat16)
    )
    return (attended, pool_keys.reshape(key_pool.shape), pool_values.reshape(value_pool.shape))


def ring_chip(pos, chips):
    pos = pos % chips
    return jnp.where(pos < chips // 2, 2 * pos, 2 * chips - 1 - 2 * pos)


def ring_place(chip, chips):
    return jnp.where(chip % 2 == 0, chip // 2, (2 * chips - 1 - chip) // 2)


def ring_pairs(chips, step, swap):
    order = [2 * k if k < chips // 2 else 2 * chips - 1 - 2 * k for k in range(chips)]
    return [
        (2 * order[k] + core, 2 * order[(k + step) % chips] + (core ^ swap))
        for k in range(chips)
        for core in range(2)
    ]


def ring_offsets(chips):
    return [0] + [o for d in range(1, chips // 2) for o in (d, -d)] + [chips // 2]


def request_starts(tr_ref, requests):
    tr = tr_ref[...]
    starts = [jnp.int32(0)]
    for r in range(1, requests):
        starts.append(jnp.sum(jnp.where(tr < r, 1.0, 0.0)).astype(jnp.int32))
    starts.append(jnp.int32(tr.shape[0] * tr.shape[1]))
    return starts


def pick(cond_starts, values, tokens):
    out = jnp.zeros_like(tokens) + values[0]
    for r in range(1, len(values)):
        out = jnp.where(tokens >= cond_starts[r], values[r], out)
    return out


def chip_requests(chip, toks, starts):
    first, last = jnp.int32(0), jnp.int32(0)
    for start in starts[1:-1]:
        first = first + (chip * toks >= start).astype(jnp.int32)
        last = last + (chip * toks + toks - 1 >= start).astype(jnp.int32)
    return first, last


def split_kernel(old, f_ref, q_ref, kp_ref, vp_ref, xm_ref, kvm_ref, out_ref, sems):
    core = lax.axis_index("dp") % 2
    copies = []

    def copy(source, target):
        copies.append(pltpu.make_async_copy(source, target, sems.at[len(copies)]))
        copies[-1].start()

    rows, pieces = f_ref.shape[0], f_ref.shape[1] // 256
    half = q_ref.shape[1] // 2
    mine = pl.ds(pl.multiple_of(core * HD, HD), HD)
    other = pl.ds(pl.multiple_of((1 - core) * HD, HD), HD)
    at = 0
    for k in range(pieces):
        for ref, own in ((out_ref, 1 - core), (xm_ref, core)):
            lane = pl.multiple_of((k // 2 * 2 + own) * 256 + k % 2 * HD, HD)
            copy(f_ref.at[:, pl.ds(lane, HD)], ref.at[pl.ds(k * rows, rows), :])
    at = pieces * rows
    for h in range(half // HD):
        lane = pl.multiple_of((1 - core) * half + h * HD, HD)
        copy(q_ref.at[:, pl.ds(lane, HD)], out_ref.at[pl.ds(at, rows), :])
        at += rows
    for n, ref in enumerate((kp_ref, vp_ref)):
        copy(ref.at[pl.ds(0, old), :, mine], kvm_ref.at[pl.ds(n * old, old)])
        for p in range(old):
            copy(ref.at[p, :, other], out_ref.at[pl.ds(at, PAGE), :])
            at += PAGE
    for c in copies:
        c.wait()


def stack_kernel(wk_ref, wv_ref, out_ref, sems):
    rows = wk_ref.shape[0]
    copies = [
        pltpu.make_async_copy(ref, out_ref.at[pl.ds(n * rows, rows), :], sems.at[n])
        for n, ref in enumerate((wk_ref, wv_ref))
    ]
    for c in copies:
        c.start()
    for c in copies:
        c.wait()


def merge_kernel(xm_ref, kvm_ref, got_ref, q_ref, x_ref, kv_ref, qs_ref):
    core = lax.axis_index("dp") % 2
    size, count = xm_ref.shape[0], kvm_ref.shape[0]
    x_ref[:size, :] = xm_ref[...]
    x_ref[size:, :] = got_ref[:size, :]
    rows, group = q_ref.shape[0], q_ref.shape[1] // (2 * HD)
    for h in range(group):
        mine = pl.ds(pl.multiple_of((2 * h + core) * rows, rows), rows)
        other = pl.ds(pl.multiple_of((2 * h + 1 - core) * rows, rows), rows)
        qs_ref[mine, :] = q_ref[:, pl.ds(pl.multiple_of((core * group + h) * HD, HD), HD)]
        qs_ref[other, :] = got_ref[size + h * rows : size + (h + 1) * rows, :]
    kv_ref[:count] = kvm_ref[...]
    first = size + group * rows
    for n in range(count):
        kv_ref[count + n] = got_ref[first + n * PAGE : first + (n + 1) * PAGE, :]


def scale_kernel(chips, lens_ref, tr_ref, inv_ref, gain_ref, x_ref, got_ref, xs_ref, ss_ref, cos_ref, sin_ref):
    dp = lax.axis_index("dp")
    mp = lax.axis_index("mp")
    chip, core = dp // 2, dp % 2
    rows = xs_ref.shape[1] // 2
    pieces = x_ref.shape[0] // (2 * rows)
    for n, owner in enumerate((core, 1 - core)):
        at = pl.ds(pl.multiple_of(owner * rows, rows), rows)
        total = jnp.zeros((rows, HD), jnp.float32)
        for ref, half in ((x_ref, mp), (got_ref, 1 - mp)):
            for k in range(pieces):
                first = (n * pieces + k) * rows
                wide = ref[first : first + rows, :].astype(jnp.float32)
                lane = (half * pieces + k // 2 * 2 + core) * 256 + k % 2 * HD
                gain = gain_ref[:, pl.ds(pl.multiple_of(lane, HD), HD)].astype(jnp.float32)
                total = total + wide * wide
                xs_ref[half * (pieces // 2) + k // 2, at, k % 2 * HD : (k % 2 + 1) * HD] = (
                    wide * gain
                ).astype(jnp.bfloat16)
        ss_ref[at, :] = jnp.broadcast_to(jnp.sum(total, axis=1, keepdims=True), (rows, HD))
    requests = lens_ref.shape[0]
    starts = request_starts(tr_ref, requests)
    tokens = chip * (2 * rows) + lax.broadcasted_iota(jnp.int32, (2 * rows, 128), 0)
    shift = pick(starts, [lens_ref[r] - starts[r] for r in range(requests)], tokens)
    angles = (tokens + shift).astype(jnp.float32) * inv_ref[...]
    lane = lax.broadcasted_iota(jnp.int32, (2 * rows, 128), 1)
    sine = jnp.sin(angles)
    cos_ref[...] = jnp.cos(angles)
    sin_ref[...] = jnp.where(lane < HD // 2, -sine, sine)


def project_kernel(chips, xs_ref, ss_ref, *refs):
    rows = xs_ref.shape[2]
    keys = [ref.at[pl.ds(0, rows), :] for ref in refs[: chips - 1]] + [refs[chips - 1]]
    values = [ref.at[pl.ds(rows, rows), :] for ref in refs[: chips - 1]] + [refs[chips]]
    send_ref, keep_ref, acc_ref = refs[chips + 1 :]
    dp = lax.axis_index("dp")
    chip, core = dp // 2, dp % 2
    place = ring_place(chip, chips)
    ksum = jnp.zeros((xs_ref.shape[1], 2 * HD), jnp.float32)
    vsum = jnp.zeros((xs_ref.shape[1], 2 * HD), jnp.float32)
    for n, offset in enumerate(ring_offsets(chips)):
        x = xs_ref[ring_chip(place + offset + chips, chips)]
        ksum = ksum + jnp.dot(x, keys[n][...], preferred_element_type=jnp.float32)
        vsum = vsum + jnp.dot(x, values[n][...], preferred_element_type=jnp.float32)
    acc_ref[:, : 2 * HD] = ksum
    acc_ref[:, 2 * HD :] = vsum
    for ref, head in ((send_ref, 1 - core), (keep_ref, core)):
        ref[:, :HD] = acc_ref[:, pl.ds(pl.multiple_of(head * HD, HD), HD)]
        ref[:, HD : 2 * HD] = acc_ref[:, pl.ds(pl.multiple_of((2 + head) * HD, HD), HD)]
        ref[:, 2 * HD :] = ss_ref[...]


def rotate_kernel(width, keep_ref, got_ref, cos_ref, sin_ref, out_ref):
    total = keep_ref[...] + got_ref[...]
    inverse = lax.rsqrt(total[:, 2 * HD :] * (1.0 / width) + 1e-05)
    key = total[:, :HD] * inverse
    rolled = pltpu.roll(key, HD // 2, 1)
    out_ref[:, :HD] = (key * cos_ref[...] + rolled * sin_ref[...]).astype(jnp.bfloat16)
    out_ref[:, HD:] = (total[:, HD : 2 * HD] * inverse).astype(jnp.bfloat16)


def attend_block(qs_ref, keys, values, first, low, high, m_ref, l_ref, acc_ref):
    scores = lax.dot_general(keys, qs_ref[...], (((1,), (1,)), ((), ())), preferred_element_type=jnp.float32)
    ids = first + lax.broadcasted_iota(jnp.int32, scores.shape, 0)
    scores = jnp.where((ids >= low) & (ids < high), scores * (LOG2E / math.sqrt(HD)), NEG_FILL)
    before = m_ref[...]
    top = jnp.maximum(before, jnp.max(scores, axis=0, keepdims=True))
    shrink = jnp.exp2(before - top)
    weights = jnp.exp2(scores - top)
    m_ref[...] = top
    l_ref[...] = l_ref[...] * shrink + jnp.sum(weights, axis=0, keepdims=True)
    acc_ref[...] = acc_ref[...] * shrink + lax.dot_general(
        values,
        weights.astype(jnp.bfloat16),
        (((0,), (0,)), ((), ())),
        preferred_element_type=jnp.float32,
    )


def three_parts(x):
    first = x.astype(jnp.bfloat16).astype(jnp.float32)
    second = (x - first).astype(jnp.bfloat16).astype(jnp.float32)
    return jnp.concatenate([first, second, x - first - second], axis=0)


def cached_kernel(chips, pages_dev, old, away, lens_ref, table_ref, tr_ref, qs_ref, *refs):
    members = chips // 2
    blocks = refs[:members]
    outs, (kbuf, vbuf, m_ref, l_ref, acc_ref, slot_of) = refs[members:-6], refs[-6:]
    dp = lax.axis_index("dp")
    chip, core = dp // 2, dp % 2
    who = chip ^ away
    requests = lens_ref.shape[0]
    width = qs_ref.shape[0]
    toks = tr_ref.shape[0] * tr_ref.shape[1] // chips
    starts = request_starts(tr_ref, requests)
    first_req, last_req = chip_requests(who, toks, starts)

    def clear(i, carry):
        slot_of[i] = -1
        return carry

    lax.fori_loop(0, slot_of.shape[0], clear, 0)
    base = jnp.int32(0)
    lows, highs = [], []
    for r in range(requests):
        length = lens_ref[r]
        relevant = (r >= first_req) & (r <= last_req)
        count = jnp.where(relevant, (length + PAGE - 1) // PAGE, 0)

        def place(l, at, r=r):
            page = table_ref[r, l]
            held = page // (2 * pages_dev * members) == chip // members

            @pl.when(held)
            def _():
                slot_of[page] = at

            return at + held.astype(jnp.int32)

        end = lax.fori_loop(0, count, place, base)
        last_page = table_ref[r, (length + PAGE - 1) // PAGE - 1]
        cut = jnp.where(
            (end > base) & (last_page // (2 * pages_dev * members) == chip // members),
            (length + PAGE - 1) // PAGE * PAGE - length,
            0,
        )
        lows.append(base * PAGE)
        highs.append(end * PAGE - cut)
        base = end

    for e in range(members):
        source = chip ^ e
        for part, owner in ((0, 2 * source + core), (2 * old, 2 * source + 1 - core)):
            for s in range(old):
                slot = slot_of[owner * pages_dev + s]

                @pl.when(slot >= 0)
                def _(e=e, part=part, s=s, slot=slot):
                    at = pl.ds(pl.multiple_of(slot * PAGE, PAGE), PAGE)
                    kbuf[at, :] = blocks[e][part + s]
                    vbuf[at, :] = blocks[e][part + old + s]

    step_pages = STEP_PAGES
    pad = pl.ds(pl.multiple_of(base * PAGE, PAGE), (step_pages - 1) * PAGE)
    kbuf[pad, :] = jnp.zeros(((step_pages - 1) * PAGE, HD), kbuf.dtype)
    vbuf[pad, :] = jnp.zeros(((step_pages - 1) * PAGE, HD), vbuf.dtype)
    tokens = who * toks + lax.broadcasted_iota(jnp.int32, (1, width), 1) % toks
    low = pick(starts, lows, tokens)
    high = pick(starts, highs, tokens)
    m_ref[...] = jnp.full(m_ref.shape, NEG_START, jnp.float32)
    l_ref[...] = jnp.zeros(l_ref.shape, jnp.float32)
    acc_ref[...] = jnp.zeros(acc_ref.shape, jnp.float32)

    def step(i, carry):
        size = step_pages * PAGE
        at = pl.ds(pl.multiple_of(i * size, size), size)
        attend_block(qs_ref, kbuf[at, :], vbuf[at, :], i * size, low, high, m_ref, l_ref, acc_ref)
        return carry

    lax.fori_loop(0, (base + step_pages - 1) // step_pages, step, 0)
    if away:
        outs[0][:HD, :] = acc_ref[...].astype(jnp.bfloat16)
        outs[0][HD:, :] = jnp.concatenate(
            [three_parts(m_ref[...]), three_parts(l_ref[...]), jnp.zeros((10, width), jnp.float32)], axis=0
        ).astype(jnp.bfloat16)
    else:
        outs[0][...], outs[1][...], outs[2][...] = m_ref[...], l_ref[...], acc_ref[...]


def fresh_kernel(
    chips, pages_dev, lens_ref, table_ref, tr_ref, qs_ref, m0_ref, l0_ref, acc0_ref, back_ref, *refs
):
    fresh = refs[:chips]
    send_ref, attc_ref, nc_ref, info_ref = refs[chips : chips + 4]
    nbuf, m_ref, l_ref, acc_ref, out_ref, new_at, new_lo, new_hi = refs[chips + 4 :]
    dp = lax.axis_index("dp")
    chip, core = dp // 2, dp % 2
    place = ring_place(chip, chips)
    toks = fresh[0].shape[0]
    rows = toks // 2
    requests = lens_ref.shape[0]
    width = qs_ref.shape[0]
    group = width // toks
    starts = request_starts(tr_ref, requests)
    reqs = chip_requests(chip, toks, starts)
    first_req = reqs[0]
    parts = back_ref[HD : HD + 6, :].astype(jnp.float32)
    m0, m1 = m0_ref[...], parts[0:1] + parts[1:2] + parts[2:3]
    top = jnp.maximum(m0, m1)
    f0, f1 = jnp.exp2(m0 - top), jnp.exp2(m1 - top)
    m_ref[...] = top
    l_ref[...] = l0_ref[...] * f0 + (parts[3:4] + parts[4:5] + parts[5:6]) * f1
    acc_ref[...] = acc0_ref[...] * f0 + back_ref[:HD, :].astype(jnp.float32) * f1

    def clear(i, carry):
        new_lo[i] = 0
        new_hi[i] = 0
        return carry

    lax.fori_loop(0, new_lo.shape[0], clear, 0)
    for r in range(requests):
        length = lens_ref[r]

        def place_new(l, carry, r=r, length=length):
            at = l * PAGE - length + starts[r]
            page = table_ref[r, l]
            new_at[page] = at
            new_lo[page] = jnp.maximum(starts[r] - at, 0)
            new_hi[page] = jnp.minimum(starts[r + 1] - at, PAGE)
            return carry

        end = (length + starts[r + 1] - starts[r] + PAGE - 1) // PAGE
        lax.fori_loop(length // PAGE, end, place_new, 0)

    for n, offset in enumerate(ring_offsets(chips)):
        source = ring_chip(place + offset + chips, chips)
        nbuf[pl.ds(pl.multiple_of((source + 1) * toks, toks), toks), :] = fresh[n][...]
    nbuf[:toks, :] = jnp.zeros((toks, 2 * HD), nbuf.dtype)
    nbuf[(chips + 1) * toks :, :] = jnp.zeros((toks, 2 * HD), nbuf.dtype)

    tokens = chip * toks + lax.broadcasted_iota(jnp.int32, (1, width), 1) % toks
    low = pick(starts, starts[:requests], tokens)
    first_start = starts[0]
    for r in range(1, requests):
        first_start = jnp.where(first_req == r, starts[r], first_start)

    def step(b, carry):
        at = pl.ds(pl.multiple_of((b + 1) * toks, toks), toks)
        attend_block(qs_ref, nbuf[at, :HD], nbuf[at, HD:], b * toks, low, tokens + 1, m_ref, l_ref, acc_ref)
        return carry

    lax.fori_loop(first_start // toks, chip + 1, step, 0)
    result = acc_ref[...] / l_ref[...]
    for h in range(group):
        out_ref[:, h * HD : (h + 1) * HD] = result[:, h * toks : (h + 1) * toks].T.astype(jnp.bfloat16)
    attc_ref[...] = out_ref[pl.ds(pl.multiple_of(core * rows, rows), rows), :]
    other = pl.ds(pl.multiple_of((1 - core) * rows, rows), rows)
    for h in range(group):
        first = 2 * pages_dev * PAGE + h * rows
        send_ref[first : first + rows, :] = out_ref[other, h * HD : (h + 1) * HD]

    row = lax.broadcasted_iota(jnp.int32, (PAGE, 2 * toks), 0)
    column = lax.broadcasted_iota(jnp.int32, (PAGE, 2 * toks), 1)
    for ref, owner in ((send_ref, dp + 1 - 2 * core), (nc_ref, dp)):
        for s in range(pages_dev):
            page = owner * pages_dev + s
            at, low_row, high_row = new_at[page], new_lo[page], new_hi[page]

            @pl.when(high_row > low_row)
            def _(ref=ref, s=s, at=at, low_row=low_row, high_row=high_row):
                shifted = at + toks
                first = pl.multiple_of(shifted // toks * toks, toks)
                chosen = (column + first == row + shifted) & (row >= low_row) & (row < high_row)
                found = jnp.dot(
                    jnp.where(chosen, 1.0, 0.0).astype(jnp.bfloat16),
                    nbuf[pl.ds(first, 2 * toks), :],
                    preferred_element_type=jnp.float32,
                ).astype(jnp.bfloat16)
                ref[2 * s * PAGE : (2 * s + 1) * PAGE, :] = found[:, :HD]
                ref[(2 * s + 1) * PAGE : (2 * s + 2) * PAGE, :] = found[:, HD:]

    for s in range(pages_dev):
        info_ref[2 * s] = new_lo[dp * pages_dev + s]
        info_ref[2 * s + 1] = new_hi[dp * pages_dev + s]


def join_kernel(info_ref, attc_ref, nc_ref, got_ref, kp_ref, vp_ref, att_ref, ko_ref, vo_ref):
    core = lax.axis_index("dp") % 2
    rows, half = attc_ref.shape
    pages = kp_ref.shape[0]
    att_ref[:, pl.ds(pl.multiple_of(core * half, HD), half)] = attc_ref[...]
    for h in range(half // HD):
        first = 2 * pages * PAGE + h * rows
        lane = pl.multiple_of((1 - core) * half + h * HD, HD)
        att_ref[:, pl.ds(lane, HD)] = got_ref[first : first + rows, :]
    row = lax.broadcasted_iota(jnp.int32, (PAGE, HD), 0)
    for s in range(pages):
        chosen = (row >= info_ref[2 * s]) & (row < info_ref[2 * s + 1])
        for ref, head in ((nc_ref, core), (got_ref, 1 - core)):
            at = pl.ds(pl.multiple_of(head * HD, HD), HD)
            first = 2 * s * PAGE
            ko_ref[s, :, at] = jnp.where(chosen, ref[first : first + PAGE, :], kp_ref[s, :, at])
            vo_ref[s, :, at] = jnp.where(chosen, ref[first + PAGE : first + 2 * PAGE, :], vp_ref[s, :, at])


def call(
    kernel, outs, scratch=(), ins=None, smem=(), far=(), out_smem=(), out_far=(), limit=VMEM_LIMIT, name=None
):
    vmem, sm = pl.BlockSpec(memory_space=pltpu.VMEM), pl.BlockSpec(memory_space=pltpu.SMEM)
    hbm = pl.BlockSpec(memory_space=pl.ANY)
    return pl.pallas_call(
        kernel,
        out_shape=[jax.ShapeDtypeStruct(s, d) for s, d in outs],
        in_specs=[sm if n in smem else hbm if n in far else vmem for n in range(ins)],
        out_specs=[sm if n in out_smem else hbm if n in out_far else vmem for n in range(len(outs))],
        scratch_shapes=list(scratch),
        compiler_params=pltpu.CompilerParams(vmem_limit_bytes=limit),
        name=name,
    )


def ring_send(chips, arrays, step, swap=0):
    return [lax.ppermute(a, "dp", ring_pairs(chips, step, swap * n)) for n, a in enumerate(arrays)]


def ring_body(
    dp_count,
    features,
    norm_gain,
    w_key,
    w_value,
    queries,
    key_pool,
    value_pool,
    cache_lens,
    page_table,
    token_request,
):
    bf, f32, i32 = jnp.bfloat16, jnp.float32, jnp.int32
    chips = dp_count // 2
    offsets = ring_offsets(chips)
    rows, half_width = features.shape
    width = norm_gain.shape[0]
    toks = 2 * rows
    pages_dev = key_pool.shape[0]
    long_pages = (CTX_DEV * dp_count + PAGE - 1) // PAGE
    old = (long_pages + 2 * ((SHORT + PAGE - 1) // PAGE) + dp_count - 1) // dp_count
    group = queries.shape[1] // (2 * HD)
    columns = group * toks
    core_pairs = [(i, i ^ 1) for i in range(dp_count)]
    mp_pairs = [(0, 1), (1, 0)]
    requests_tile = token_request.reshape(-1, 128)

    def exchange(array, e, swap=0):
        return lax.ppermute(array, "dp", [(i, i ^ (2 * e) ^ swap) for i in range(dp_count)])

    last = chips // 2
    w_rows = w_key.shape[0]
    (w_both,) = call(
        stack_kernel,
        [((2 * w_rows, w_key.shape[1]), bf)],
        scratch=[pltpu.SemaphoreType.DMA((2,))],
        ins=2,
        far=(0, 1),
        limit=SPLIT_LIMIT,
        name="stack",
    )(w_key, w_value)

    def hop(array, step):
        return ring_send(chips, [array], step)[0]

    w_got = {0: w_both, -1: hop(w_both, 1), 1: hop(w_both, -1)}
    pieces = half_width // 256
    bundle = (pieces + group) * rows + 2 * old * PAGE
    x_mine, kv_mine, core_send = call(
        functools.partial(split_kernel, old),
        [((pieces * rows, HD), bf), ((2 * old, PAGE, HD), bf), ((bundle, HD), bf)],
        scratch=[pltpu.SemaphoreType.DMA((2 * pieces + group + 2 + 2 * old,))],
        ins=4,
        far=(0, 1, 2, 3),
        limit=SPLIT_LIMIT,
        name="split",
    )(features, queries, key_pool, value_pool)
    core_got = lax.ppermute(core_send, "dp", core_pairs)
    x_here, kv, q_rows = call(
        merge_kernel,
        [((2 * pieces * rows, HD), bf), ((4 * old, PAGE, HD), bf), ((columns, HD), bf)],
        ins=4,
        name="merge",
    )(x_mine, kv_mine, core_got, queries)
    x_there = lax.ppermute(x_here, "mp", mp_pairs)
    q_away = exchange(q_rows, last)
    kv_z, kv_y = exchange(kv, 2), exchange(kv, 1)

    right, x_here = lax.optimization_barrier((w_got[-1], x_here))
    w_got[-2], w_got[2] = hop(right, 1), hop(w_got[1], -1)
    right, x_there, kv_y = lax.optimization_barrier((w_got[-2], x_there, kv_y))
    w_got[-3], w_got[3] = hop(right, 1), hop(w_got[2], -1)
    kv_d = exchange(kv_y, 2)
    inverse = (THETA ** (-(np.arange(HD) % (HD // 2)) * 2.0 / HD)).astype(np.float32)[None, :]
    scaled, squares, cosine, sine = call(
        functools.partial(scale_kernel, chips),
        [((chips, toks, w_rows), bf), ((toks, HD), f32), ((toks, HD), f32), ((toks, HD), f32)],
        ins=6,
        smem=(0,),
        name="scale",
    )(cache_lens, requests_tile, jnp.asarray(inverse), norm_gain.reshape(1, -1), x_here, x_there)
    right, kv_z, q_away = lax.optimization_barrier((w_got[-3], kv_z, q_away))
    w_last = [hop(right[:w_rows], 1), hop(w_got[3][w_rows:], -1)]
    scaled, kv_d = lax.optimization_barrier((scaled, kv_d))
    part_send, part_keep = call(
        functools.partial(project_kernel, chips),
        [((toks, 3 * HD), f32), ((toks, 3 * HD), f32)],
        scratch=[pltpu.VMEM((toks, 4 * HD), f32)],
        ins=2 + chips + 1,
        name="project",
    )(scaled, squares, *[w_got[o] for o in offsets[:-1]], *w_last)
    part_got = lax.ppermute(part_send, "dp", core_pairs)

    (fresh,) = call(
        functools.partial(rotate_kernel, width),
        [((toks, 2 * HD), bf)],
        ins=4,
        name="rotary",
    )(part_keep, part_got, cosine, sine)
    new = {0: fresh}
    new[-1], new[1] = ring_send(chips, [fresh], 1)[0], ring_send(chips, [fresh], -1)[0]
    slots = dp_count // 2 * old + STEP_PAGES
    table = pltpu.SMEM((dp_count * pages_dev,), i32)

    def cached(q, away, outs, name):
        return call(
            functools.partial(cached_kernel, chips, pages_dev, old, away),
            outs,
            scratch=[
                pltpu.VMEM((slots * PAGE, HD), bf),
                pltpu.VMEM((slots * PAGE, HD), bf),
                pltpu.VMEM((1, columns), f32),
                pltpu.VMEM((1, columns), f32),
                pltpu.VMEM((HD, columns), f32),
                table,
            ],
            ins=4 + chips // 2,
            smem=(0, 1),
            name=name,
        )(cache_lens, page_table, requests_tile, q, kv, kv_y, kv_z, kv_d)

    (away,) = cached(q_away, chips // 2, [((HD + 16, columns), bf)], "attend_cached_away")
    here = cached(
        q_rows, 0, [((1, columns), f32), ((1, columns), f32), ((HD, columns), f32)], "attend_cached_here"
    )
    beside = {2: away, 3: here}
    for d in range(2, chips // 2):
        right, left, beside[d] = lax.optimization_barrier((new[1 - d], new[d - 1], beside[d]))
        new[-d], new[d] = ring_send(chips, [right], 1)[0], ring_send(chips, [left], -1)[0]
    (new[chips // 2],) = ring_send(chips, [new[1 - chips // 2]], 1)
    back = exchange(beside[2], chips // 2)
    top, total, acc = beside[3]

    rows_bundle = 2 * pages_dev * PAGE
    last_send, att_mine, rows_mine, info = call(
        functools.partial(fresh_kernel, chips, pages_dev),
        [
            ((rows_bundle + group * rows, HD), bf),
            ((rows, group * HD), bf),
            ((rows_bundle, HD), bf),
            ((2 * pages_dev,), i32),
        ],
        scratch=[
            pltpu.VMEM(((chips + 2) * toks, 2 * HD), bf),
            pltpu.VMEM((1, columns), f32),
            pltpu.VMEM((1, columns), f32),
            pltpu.VMEM((HD, columns), f32),
            pltpu.VMEM((toks, group * HD), bf),
            table,
            table,
            table,
        ],
        ins=8 + chips,
        smem=(0, 1),
        out_smem=(3,),
        name="attend_new",
    )(
        cache_lens,
        page_table,
        requests_tile,
        q_rows,
        top,
        total,
        acc,
        back,
        *[new[o] for o in offsets],
    )
    last_got = lax.ppermute(last_send, "dp", core_pairs)
    attended, keys_out, values_out = call(
        join_kernel,
        [(queries.shape, bf), (key_pool.shape, bf), (value_pool.shape, bf)],
        ins=6,
        smem=(0,),
        name="join",
    )(info, att_mine, rows_mine, last_got, key_pool, value_pool)
    return attended, keys_out, values_out


def solution(mesh):
    in_specs = (
        P("dp", "mp"),
        P(),
        P("dp", "mp"),
        P("dp", "mp"),
        P("dp", "mp"),
        P("dp", None, "mp"),
        P("dp", None, "mp"),
        P(),
        P(),
        P(),
    )
    out_specs = (P("dp", "mp"), P("dp", None, "mp"), P("dp", None, "mp"))
    dp_count, mp_count = mesh.shape["dp"], mesh.shape["mp"]

    def body(*args):
        even = mp_count == 2 and dp_count == 16
        if even and args[2].shape == (256, 2 * HD):
            return ring_body(dp_count, *args)
        return general_body(*args)

    return jax.shard_map(body, mesh=mesh, in_specs=in_specs, out_specs=out_specs, check_vma=False)
```

```python
import functools
import math

import jax
import jax.numpy as jnp
import numpy as np
from jax import lax
from jax.experimental import pallas as pl
from jax.experimental.pallas import tpu as pltpu
from jax.sharding import PartitionSpec as P

HD = 128
PAGE = 128
SHORT = 512
CTX_DEV = 120


THETA = 500000.0
NEG_FILL = -1e30
NEG_START = -1e29
LOG2E = 1.4426950408889634
VMEM_LIMIT = 32 * 1024 * 1024
SPLIT_LIMIT = 63 * 1024 * 1024
STEP_PAGES = 4


def rotate(values, positions, head_size):
    halfway = head_size // 2
    inverse = THETA ** (-(jnp.arange(halfway, dtype=jnp.float32) * 2.0) / head_size)
    angles = positions.astype(jnp.float32)[:, None] * inverse[None, :]
    cosine = jnp.cos(angles)[:, None, :]
    sine = jnp.sin(angles)[:, None, :]
    first_half = values[..., :halfway]
    second_half = values[..., halfway:]
    return jnp.concatenate(
        [first_half * cosine - second_half * sine, second_half * cosine + first_half * sine],
        axis=-1,
    )


def general_body(
    features,
    norm_gain,
    w_key,
    w_value,
    queries,
    key_pool,
    value_pool,
    cache_lens,
    page_table,
    token_request,
):
    gathered = lax.all_gather(features, "mp", axis=1, tiled=True)
    widened = gathered.astype(jnp.float32)
    mean_square = jnp.mean(widened * widened, axis=1, keepdims=True)
    normed = (widened * lax.rsqrt(mean_square + 1e-05) * norm_gain.astype(jnp.float32)).astype(
        jnp.bfloat16
    )
    tok_rows = features.shape[0]
    kv_width = w_key.shape[1]
    head_size = HD
    kv_heads = kv_width // head_size
    q_heads = queries.shape[1] // head_size
    group_size = q_heads // kv_heads
    scale = 1.0 / math.sqrt(head_size)
    pieces = (
        lax.all_gather(w_key, "dp", axis=0, tiled=True),
        lax.all_gather(w_value, "dp", axis=0, tiled=True),
    )
    key_sums = jnp.dot(normed, pieces[0], preferred_element_type=jnp.float32)
    value_sums = jnp.dot(normed, pieces[1], preferred_element_type=jnp.float32)
    total_new = token_request.shape[0]
    requests = cache_lens.shape[0]
    request_ids = jnp.arange(requests, dtype=jnp.int32)
    member = (token_request[:, None] == request_ids[None, :]).astype(jnp.int32)
    counts = jnp.sum(member, axis=0)
    starts = jnp.cumsum(counts) - counts
    token_index = jnp.arange(total_new, dtype=jnp.int32)
    token_pos = jnp.sum(member * (cache_lens - starts)[None, :], axis=1) + token_index
    dp_index = lax.axis_index("dp")
    dp_count = lax.axis_size("dp")
    first_token = dp_index * tok_rows
    my_request = lax.dynamic_slice_in_dim(token_request, first_token, tok_rows)
    my_pos = lax.dynamic_slice_in_dim(token_pos, first_token, tok_rows)
    key_heads = rotate(key_sums.reshape(tok_rows, kv_heads, head_size), my_pos, head_size)
    new_keys = key_heads.reshape(tok_rows, kv_width).astype(jnp.bfloat16)
    new_values = value_sums.astype(jnp.bfloat16)
    pages_dev = key_pool.shape[0]
    page_rows = key_pool.shape[1]
    max_pages = page_table.shape[1]
    slot_all = jnp.take(page_table.reshape(-1), token_request * max_pages + token_pos // page_rows)
    local_slot = slot_all - dp_index * pages_dev
    owned = (local_slot >= 0) & (local_slot < pages_dev)
    dest_all = jnp.where(
        owned, local_slot * page_rows + token_pos % page_rows, pages_dev * page_rows
    )
    long_pages = (CTX_DEV * dp_count + PAGE - 1) // PAGE
    old_dev = (long_pages + 2 * ((SHORT + PAGE - 1) // PAGE) + dp_count - 1) // dp_count
    old_total = old_dev * dp_count
    old_ids = jnp.arange(old_total, dtype=jnp.int32)
    old_phys = old_ids // old_dev * pages_dev + old_ids % old_dev
    matches = (page_table[None, :, :] == old_phys[:, None, None]).astype(jnp.int32)
    page_has = jnp.sum(matches, axis=(1, 2)) > 0
    page_request = jnp.sum(matches * request_ids[None, :, None], axis=(1, 2))
    page_logical = jnp.sum(
        matches * jnp.arange(max_pages, dtype=jnp.int32)[None, None, :], axis=(1, 2)
    )
    page_limit = jnp.sum(matches * cache_lens[None, :, None], axis=(1, 2))
    q_local = queries.reshape(tok_rows, kv_heads, group_size, head_size)

    def attend(att_state, keys_flat, values_flat, key_info):
        key_request, key_pos, key_ok = key_info
        visible = (
            key_ok[None, :]
            & (key_request[None, :] == my_request[:, None])
            & (key_pos[None, :] <= my_pos[:, None])
        )
        keys_shaped = keys_flat.reshape(keys_flat.shape[0], kv_heads, head_size)
        values_shaped = values_flat.reshape(values_flat.shape[0], kv_heads, head_size)
        running_max, running_sum, running_acc = att_state
        scores = (
            jnp.einsum("thgd,khd->thgk", q_local, keys_shaped, preferred_element_type=jnp.float32)
            * scale
        )
        mask_full = visible[:, None, None, :]
        masked = jnp.where(mask_full, scores, NEG_FILL)
        new_max = jnp.maximum(running_max, jnp.max(masked, axis=-1))
        factor = jnp.exp(running_max - new_max)
        soft_weights = jnp.where(mask_full, jnp.exp(masked - new_max[..., None]), 0.0)
        new_sum = running_sum * factor + jnp.sum(soft_weights, axis=-1)
        new_acc = running_acc * factor[..., None] + jnp.einsum(
            "thgk,khd->thgd",
            soft_weights.astype(jnp.bfloat16),
            values_shaped,
            preferred_element_type=jnp.float32,
        )
        return (new_max, new_sum, new_acc)

    def attend_rows(att_state, keys_flat, values_flat, key_info):
        row_count = keys_flat.shape[0]
        key_block = 2048
        if row_count > key_block and row_count % key_block == 0:
            blocks = row_count // key_block
            stacked = (
                keys_flat.reshape(blocks, key_block, kv_width),
                values_flat.reshape(blocks, key_block, kv_width),
                key_info[0].reshape(blocks, key_block),
                key_info[1].reshape(blocks, key_block),
                key_info[2].reshape(blocks, key_block),
            )

            def step_block(inner_state, slab_parts):
                return (
                    attend(
                        inner_state,
                        slab_parts[0],
                        slab_parts[1],
                        (slab_parts[2], slab_parts[3], slab_parts[4]),
                    ),
                    None,
                )

            att_state, unused = lax.scan(step_block, att_state, stacked)
            return att_state
        return attend(att_state, keys_flat, values_flat, key_info)

    start_state = (
        jnp.full((tok_rows, kv_heads, group_size), NEG_FILL, jnp.float32),
        jnp.zeros((tok_rows, kv_heads, group_size), jnp.float32),
        jnp.zeros((tok_rows, kv_heads, group_size, head_size), jnp.float32),
    )
    flat_keys = key_pool.reshape(pages_dev * page_rows, kv_width)
    flat_values = value_pool.reshape(pages_dev * page_rows, kv_width)
    old_keys = key_pool[:old_dev]
    old_values = value_pool[:old_dev]
    pieces = (
        lax.all_gather(old_keys, "dp", axis=0, tiled=True),
        lax.all_gather(old_values, "dp", axis=0, tiled=True),
    )
    page_count = pieces[0].shape[0]
    cached_keys = pieces[0].reshape(page_count * page_rows, kv_width)
    cached_values = pieces[1].reshape(page_count * page_rows, kv_width)
    row_ids = jnp.arange(page_rows, dtype=jnp.int32)[None, :]
    key_pos = page_logical[:, None] * page_rows + row_ids
    key_ok = page_has[:, None] & (key_pos < page_limit[:, None])
    key_request = jnp.broadcast_to(page_request[:, None], (page_count, page_rows))
    middle_state = attend_rows(
        start_state,
        cached_keys,
        cached_values,
        (key_request.reshape(-1), key_pos.reshape(-1), key_ok.reshape(-1)),
    )
    pieces = (
        lax.all_gather(new_keys, "dp", axis=0, tiled=True),
        lax.all_gather(new_values, "dp", axis=0, tiled=True),
    )
    att_state = middle_state
    pool_keys = flat_keys
    pool_values = flat_values
    key_request = token_request
    key_pos = token_pos
    att_state = attend_rows(
        att_state,
        pieces[0],
        pieces[1],
        (key_request, key_pos, jnp.ones((pieces[0].shape[0],), jnp.bool_)),
    )
    pool_keys, pool_values = (
        pool_keys.at[dest_all].set(pieces[0], mode="drop"),
        pool_values.at[dest_all].set(pieces[1], mode="drop"),
    )
    final_state, pool_keys, pool_values = (att_state, pool_keys, pool_values)
    final_max, final_sum, final_acc = final_state
    attended = (
        (final_acc / final_sum[..., None])
        .reshape(tok_rows, q_heads * head_size)
        .astype(jnp.bfloat16)
    )
    return (attended, pool_keys.reshape(key_pool.shape), pool_values.reshape(value_pool.shape))


def ring_chip(pos, chips):
    pos = pos % chips
    return jnp.where(pos < chips // 2, 2 * pos, 2 * chips - 1 - 2 * pos)


def ring_place(chip, chips):
    return jnp.where(chip % 2 == 0, chip // 2, (2 * chips - 1 - chip) // 2)


def ring_pairs(chips, step, swap):
    order = [2 * k if k < chips // 2 else 2 * chips - 1 - 2 * k for k in range(chips)]
    return [
        (2 * order[k] + core, 2 * order[(k + step) % chips] + (core ^ swap))
        for k in range(chips)
        for core in range(2)
    ]


def ring_offsets(chips):
    return [0] + [o for d in range(1, chips // 2) for o in (d, -d)] + [chips // 2]


def request_starts(tr_ref, requests):
    tr = tr_ref[...]
    starts = [jnp.int32(0)]
    for r in range(1, requests):
        starts.append(jnp.sum(jnp.where(tr < r, 1.0, 0.0)).astype(jnp.int32))
    starts.append(jnp.int32(tr.shape[0] * tr.shape[1]))
    return starts


def pick(cond_starts, values, tokens):
    out = jnp.zeros_like(tokens) + values[0]
    for r in range(1, len(values)):
        out = jnp.where(tokens >= cond_starts[r], values[r], out)
    return out


def chip_requests(chip, toks, starts):
    first, last = jnp.int32(0), jnp.int32(0)
    for start in starts[1:-1]:
        first = first + (chip * toks >= start).astype(jnp.int32)
        last = last + (chip * toks + toks - 1 >= start).astype(jnp.int32)
    return first, last


def split_kernel(old, f_ref, q_ref, kp_ref, vp_ref, xc_ref, xo_ref, kvc_ref, out_ref, sems):
    core = lax.axis_index("dp") % 2
    copies = []

    def copy(source, target):
        copies.append(pltpu.make_async_copy(source, target, sems.at[len(copies)]))
        copies[-1].start()

    rows = f_ref.shape[0]
    half = q_ref.shape[1] // 2
    mine = pl.ds(pl.multiple_of(core * HD, HD), HD)
    other = pl.ds(pl.multiple_of((1 - core) * HD, HD), HD)
    for out, own in ((xo_ref, 1 - core), (xc_ref, core)):
        for m in range(f_ref.shape[1] // 512):
            at = pl.ds(pl.multiple_of((2 * m + own) * 256, 256), 256)
            copy(f_ref.at[:, at], out.at[:, pl.ds(m * 256, 256)])
    at = 0
    for n, ref in enumerate((kp_ref, vp_ref)):
        copy(ref.at[pl.ds(0, old), :, mine], kvc_ref.at[pl.ds(n * old, old)])
        for p in range(old):
            copy(ref.at[p, :, other], out_ref.at[pl.ds(at, PAGE), :])
            at += PAGE
    for h in range(half // HD):
        lane = pl.multiple_of((1 - core) * half + h * HD, HD)
        copy(q_ref.at[:, pl.ds(lane, HD)], out_ref.at[pl.ds(at, rows), :])
        at += rows
    for c in copies:
        c.wait()


def merge_kernel(q_ref, got_ref, qs_ref, kv_ref):
    core = lax.axis_index("dp") % 2
    count = kv_ref.shape[0]
    rows, group = q_ref.shape[0], q_ref.shape[1] // (2 * HD)
    for n in range(count):
        kv_ref[n] = got_ref[n * PAGE : (n + 1) * PAGE, :]
    for h in range(group):
        mine = pl.ds(pl.multiple_of((2 * h + core) * rows, rows), rows)
        other = pl.ds(pl.multiple_of((2 * h + 1 - core) * rows, rows), rows)
        qs_ref[mine, :] = q_ref[:, pl.ds(pl.multiple_of((core * group + h) * HD, HD), HD)]
        first = count * PAGE + h * rows
        qs_ref[other, :] = got_ref[first : first + rows, :]


def scale_kernel(
    chips, lens_ref, tr_ref, inv_ref, gain_ref, a_ref, b_ref, c_ref, d_ref, xs_ref, ss_ref, cos_ref, sin_ref
):
    dp = lax.axis_index("dp")
    mp = lax.axis_index("mp")
    chip, core = dp // 2, dp % 2
    rows = a_ref.shape[0]
    per_half = a_ref.shape[1] // 256
    for first, second, owner in ((a_ref, b_ref, core), (c_ref, d_ref, 1 - core)):
        at = pl.ds(pl.multiple_of(owner * rows, rows), rows)
        total = jnp.zeros((rows, 256), jnp.float32)
        for ref, half in ((first, mp), (second, 1 - mp)):
            for m in range(per_half):
                wide = ref[:, m * 256 : (m + 1) * 256].astype(jnp.float32)
                block = half * (2 * per_half) + 2 * m + core
                gain = gain_ref[:, pl.ds(pl.multiple_of(block * 256, 256), 256)].astype(jnp.float32)
                total = total + wide * wide
                xs_ref[half * per_half + m, at, :] = (wide * gain).astype(jnp.bfloat16)
        ss_ref[at, :] = jnp.broadcast_to(jnp.sum(total, axis=1, keepdims=True), (rows, 128))
    requests = lens_ref.shape[0]
    starts = request_starts(tr_ref, requests)
    tokens = chip * (2 * rows) + lax.broadcasted_iota(jnp.int32, (2 * rows, 128), 0)
    shift = pick(starts, [lens_ref[r] - starts[r] for r in range(requests)], tokens)
    angles = (tokens + shift).astype(jnp.float32) * inv_ref[...]
    lane = lax.broadcasted_iota(jnp.int32, (2 * rows, 128), 1)
    sine = jnp.sin(angles)
    cos_ref[...] = jnp.cos(angles)
    sin_ref[...] = jnp.where(lane < HD // 2, -sine, sine)


def project_kernel(chips, xs_ref, ss_ref, *refs):
    keys, values = refs[:chips], refs[chips : 2 * chips]
    send_ref, keep_ref, acc_ref = refs[2 * chips :]
    dp = lax.axis_index("dp")
    chip, core = dp // 2, dp % 2
    place = ring_place(chip, chips)
    ksum = jnp.zeros((xs_ref.shape[1], 2 * HD), jnp.float32)
    vsum = jnp.zeros((xs_ref.shape[1], 2 * HD), jnp.float32)
    for n, offset in enumerate(ring_offsets(chips)):
        x = xs_ref[ring_chip(place + offset + chips, chips)]
        ksum = ksum + jnp.dot(x, keys[n][...], preferred_element_type=jnp.float32)
        vsum = vsum + jnp.dot(x, values[n][...], preferred_element_type=jnp.float32)
    acc_ref[:, : 2 * HD] = ksum
    acc_ref[:, 2 * HD :] = vsum
    for ref, head in ((send_ref, 1 - core), (keep_ref, core)):
        ref[:, :HD] = acc_ref[:, pl.ds(pl.multiple_of(head * HD, HD), HD)]
        ref[:, HD : 2 * HD] = acc_ref[:, pl.ds(pl.multiple_of((2 + head) * HD, HD), HD)]
        ref[:, 2 * HD :] = ss_ref[...]


def rotate_kernel(width, keep_ref, got_ref, cos_ref, sin_ref, out_ref):
    total = keep_ref[...] + got_ref[...]
    inverse = lax.rsqrt(total[:, 2 * HD :] * (1.0 / width) + 1e-05)
    key = total[:, :HD] * inverse
    rolled = pltpu.roll(key, HD // 2, 1)
    out_ref[:, :HD] = (key * cos_ref[...] + rolled * sin_ref[...]).astype(jnp.bfloat16)
    out_ref[:, HD:] = (total[:, HD : 2 * HD] * inverse).astype(jnp.bfloat16)


def attend_block(qs_ref, keys, values, first, low, high, m_ref, l_ref, acc_ref):
    scores = lax.dot_general(keys, qs_ref[...], (((1,), (1,)), ((), ())), preferred_element_type=jnp.float32)
    ids = first + lax.broadcasted_iota(jnp.int32, scores.shape, 0)
    scores = jnp.where((ids >= low) & (ids < high), scores * (LOG2E / math.sqrt(HD)), NEG_FILL)
    before = m_ref[...]
    top = jnp.maximum(before, jnp.max(scores, axis=0, keepdims=True))
    shrink = jnp.exp2(before - top)
    weights = jnp.exp2(scores - top)
    m_ref[...] = top
    l_ref[...] = l_ref[...] * shrink + jnp.sum(weights, axis=0, keepdims=True)
    acc_ref[...] = acc_ref[...] * shrink + lax.dot_general(
        values,
        weights.astype(jnp.bfloat16),
        (((0,), (0,)), ((), ())),
        preferred_element_type=jnp.float32,
    )


def three_parts(x):
    first = x.astype(jnp.bfloat16).astype(jnp.float32)
    second = (x - first).astype(jnp.bfloat16).astype(jnp.float32)
    return jnp.concatenate([first, second, x - first - second], axis=0)


def cached_kernel(chips, pages_dev, old, away, lens_ref, table_ref, tr_ref, qs_ref, *refs):
    members = chips // 2
    near, far = refs[:members], refs[members : 2 * members]
    outs, (kbuf, vbuf, m_ref, l_ref, acc_ref, slot_of) = refs[2 * members : -6], refs[-6:]
    dp = lax.axis_index("dp")
    chip, core = dp // 2, dp % 2
    who = chip ^ away
    requests = lens_ref.shape[0]
    width = qs_ref.shape[0]
    toks = tr_ref.shape[0] * tr_ref.shape[1] // chips
    starts = request_starts(tr_ref, requests)
    first_req, last_req = chip_requests(who, toks, starts)

    def clear(i, carry):
        slot_of[i] = -1
        return carry

    lax.fori_loop(0, slot_of.shape[0], clear, 0)
    base = jnp.int32(0)
    lows, highs = [], []
    for r in range(requests):
        length = lens_ref[r]
        relevant = (r >= first_req) & (r <= last_req)
        count = jnp.where(relevant, (length + PAGE - 1) // PAGE, 0)

        def place(l, at, r=r):
            page = table_ref[r, l]
            held = page // (2 * pages_dev * members) == chip // members

            @pl.when(held)
            def _():
                slot_of[page] = at

            return at + held.astype(jnp.int32)

        end = lax.fori_loop(0, count, place, base)
        last_page = table_ref[r, (length + PAGE - 1) // PAGE - 1]
        cut = jnp.where(
            (end > base) & (last_page // (2 * pages_dev * members) == chip // members),
            (length + PAGE - 1) // PAGE * PAGE - length,
            0,
        )
        lows.append(base * PAGE)
        highs.append(end * PAGE - cut)
        base = end

    for e in range(members):
        source = chip ^ e
        for block, owner in ((near[e], 2 * source + core), (far[e], 2 * source + 1 - core)):
            for s in range(old):
                slot = slot_of[owner * pages_dev + s]

                @pl.when(slot >= 0)
                def _(block=block, s=s, slot=slot):
                    at = pl.ds(pl.multiple_of(slot * PAGE, PAGE), PAGE)
                    kbuf[at, :] = block[s]
                    vbuf[at, :] = block[old + s]

    step_pages = STEP_PAGES
    pad = pl.ds(pl.multiple_of(base * PAGE, PAGE), (step_pages - 1) * PAGE)
    kbuf[pad, :] = jnp.zeros(((step_pages - 1) * PAGE, HD), kbuf.dtype)
    vbuf[pad, :] = jnp.zeros(((step_pages - 1) * PAGE, HD), vbuf.dtype)
    tokens = who * toks + lax.broadcasted_iota(jnp.int32, (1, width), 1) % toks
    low = pick(starts, lows, tokens)
    high = pick(starts, highs, tokens)
    m_ref[...] = jnp.full(m_ref.shape, NEG_START, jnp.float32)
    l_ref[...] = jnp.zeros(l_ref.shape, jnp.float32)
    acc_ref[...] = jnp.zeros(acc_ref.shape, jnp.float32)

    def step(i, carry):
        size = step_pages * PAGE
        at = pl.ds(pl.multiple_of(i * size, size), size)
        attend_block(qs_ref, kbuf[at, :], vbuf[at, :], i * size, low, high, m_ref, l_ref, acc_ref)
        return carry

    lax.fori_loop(0, (base + step_pages - 1) // step_pages, step, 0)
    if away:
        outs[0][:HD, :] = acc_ref[...].astype(jnp.bfloat16)
        outs[0][HD:, :] = jnp.concatenate(
            [three_parts(m_ref[...]), three_parts(l_ref[...]), jnp.zeros((10, width), jnp.float32)], axis=0
        ).astype(jnp.bfloat16)
    else:
        outs[0][...], outs[1][...], outs[2][...] = m_ref[...], l_ref[...], acc_ref[...]


def fresh_kernel(
    chips, pages_dev, lens_ref, table_ref, tr_ref, qs_ref, m0_ref, l0_ref, acc0_ref, back_ref, *refs
):
    fresh = refs[:chips]
    atto_ref, attc_ref, no_ref, nc_ref, info_ref = refs[chips : chips + 5]
    nbuf, m_ref, l_ref, acc_ref, out_ref, new_at, new_lo, new_hi = refs[chips + 5 :]
    dp = lax.axis_index("dp")
    chip, core = dp // 2, dp % 2
    place = ring_place(chip, chips)
    toks = fresh[0].shape[0]
    rows = toks // 2
    requests = lens_ref.shape[0]
    width = qs_ref.shape[0]
    group = width // toks
    starts = request_starts(tr_ref, requests)
    reqs = chip_requests(chip, toks, starts)
    first_req = reqs[0]
    parts = back_ref[HD : HD + 6, :].astype(jnp.float32)
    m0, m1 = m0_ref[...], parts[0:1] + parts[1:2] + parts[2:3]
    top = jnp.maximum(m0, m1)
    f0, f1 = jnp.exp2(m0 - top), jnp.exp2(m1 - top)
    m_ref[...] = top
    l_ref[...] = l0_ref[...] * f0 + (parts[3:4] + parts[4:5] + parts[5:6]) * f1
    acc_ref[...] = acc0_ref[...] * f0 + back_ref[:HD, :].astype(jnp.float32) * f1

    def clear(i, carry):
        new_lo[i] = 0
        new_hi[i] = 0
        return carry

    lax.fori_loop(0, new_lo.shape[0], clear, 0)
    for r in range(requests):
        length = lens_ref[r]

        def place_new(l, carry, r=r, length=length):
            at = l * PAGE - length + starts[r]
            page = table_ref[r, l]
            new_at[page] = at
            new_lo[page] = jnp.maximum(starts[r] - at, 0)
            new_hi[page] = jnp.minimum(starts[r + 1] - at, PAGE)
            return carry

        end = (length + starts[r + 1] - starts[r] + PAGE - 1) // PAGE
        lax.fori_loop(length // PAGE, end, place_new, 0)

    for n, offset in enumerate(ring_offsets(chips)):
        source = ring_chip(place + offset + chips, chips)
        nbuf[pl.ds(pl.multiple_of((source + 1) * toks, toks), toks), :] = fresh[n][...]
    nbuf[:toks, :] = jnp.zeros((toks, 2 * HD), nbuf.dtype)
    nbuf[(chips + 1) * toks :, :] = jnp.zeros((toks, 2 * HD), nbuf.dtype)

    tokens = chip * toks + lax.broadcasted_iota(jnp.int32, (1, width), 1) % toks
    low = pick(starts, starts[:requests], tokens)
    first_start = starts[0]
    for r in range(1, requests):
        first_start = jnp.where(first_req == r, starts[r], first_start)

    def step(b, carry):
        at = pl.ds(pl.multiple_of((b + 1) * toks, toks), toks)
        attend_block(qs_ref, nbuf[at, :HD], nbuf[at, HD:], b * toks, low, tokens + 1, m_ref, l_ref, acc_ref)
        return carry

    lax.fori_loop(first_start // toks, chip + 1, step, 0)
    result = acc_ref[...] / l_ref[...]
    for h in range(group):
        out_ref[:, h * HD : (h + 1) * HD] = result[:, h * toks : (h + 1) * toks].T.astype(jnp.bfloat16)
    attc_ref[...] = out_ref[pl.ds(pl.multiple_of(core * rows, rows), rows), :]
    atto_ref[...] = out_ref[pl.ds(pl.multiple_of((1 - core) * rows, rows), rows), :]

    row = lax.broadcasted_iota(jnp.int32, (PAGE, 2 * toks), 0)
    column = lax.broadcasted_iota(jnp.int32, (PAGE, 2 * toks), 1)
    for ref, owner in ((no_ref, dp + 1 - 2 * core), (nc_ref, dp)):
        for s in range(pages_dev):
            page = owner * pages_dev + s
            at, low_row, high_row = new_at[page], new_lo[page], new_hi[page]

            @pl.when(high_row > low_row)
            def _(ref=ref, s=s, at=at, low_row=low_row, high_row=high_row):
                shifted = at + toks
                first = pl.multiple_of(shifted // toks * toks, toks)
                chosen = (column + first == row + shifted) & (row >= low_row) & (row < high_row)
                ref[s] = jnp.dot(
                    jnp.where(chosen, 1.0, 0.0).astype(jnp.bfloat16),
                    nbuf[pl.ds(first, 2 * toks), :],
                    preferred_element_type=jnp.float32,
                ).astype(jnp.bfloat16)

    for s in range(pages_dev):
        info_ref[2 * s] = new_lo[dp * pages_dev + s]
        info_ref[2 * s + 1] = new_hi[dp * pages_dev + s]


def join_kernel(info_ref, attc_ref, attr_ref, nc_ref, nr_ref, kp_ref, vp_ref, att_ref, ko_ref, vo_ref):
    core = lax.axis_index("dp") % 2
    half = attc_ref.shape[1]
    att_ref[:, pl.ds(pl.multiple_of(core * half, HD), half)] = attc_ref[...]
    att_ref[:, pl.ds(pl.multiple_of((1 - core) * half, HD), half)] = attr_ref[...]
    row = lax.broadcasted_iota(jnp.int32, (PAGE, HD), 0)
    for s in range(kp_ref.shape[0]):
        chosen = (row >= info_ref[2 * s]) & (row < info_ref[2 * s + 1])
        for ref, head in ((nc_ref, core), (nr_ref, 1 - core)):
            at = pl.ds(pl.multiple_of(head * HD, HD), HD)
            ko_ref[s, :, at] = jnp.where(chosen, ref[s, :, :HD], kp_ref[s, :, at])
            vo_ref[s, :, at] = jnp.where(chosen, ref[s, :, HD:], vp_ref[s, :, at])


def call(
    kernel, outs, scratch=(), ins=None, smem=(), far=(), out_smem=(), out_far=(), limit=VMEM_LIMIT, name=None
):
    vmem, sm = pl.BlockSpec(memory_space=pltpu.VMEM), pl.BlockSpec(memory_space=pltpu.SMEM)
    hbm = pl.BlockSpec(memory_space=pl.ANY)
    return pl.pallas_call(
        kernel,
        out_shape=[jax.ShapeDtypeStruct(s, d) for s, d in outs],
        in_specs=[sm if n in smem else hbm if n in far else vmem for n in range(ins)],
        out_specs=[sm if n in out_smem else hbm if n in out_far else vmem for n in range(len(outs))],
        scratch_shapes=list(scratch),
        compiler_params=pltpu.CompilerParams(vmem_limit_bytes=limit),
        name=name,
    )


def ring_send(chips, arrays, step, swap=0):
    return [lax.ppermute(a, "dp", ring_pairs(chips, step, swap * n)) for n, a in enumerate(arrays)]


def ring_body(
    dp_count,
    features,
    norm_gain,
    w_key,
    w_value,
    queries,
    key_pool,
    value_pool,
    cache_lens,
    page_table,
    token_request,
):
    bf, f32, i32 = jnp.bfloat16, jnp.float32, jnp.int32
    chips = dp_count // 2
    offsets = ring_offsets(chips)
    rows, half_width = features.shape
    width = norm_gain.shape[0]
    toks = 2 * rows
    pages_dev = key_pool.shape[0]
    long_pages = (CTX_DEV * dp_count + PAGE - 1) // PAGE
    old = (long_pages + 2 * ((SHORT + PAGE - 1) // PAGE) + dp_count - 1) // dp_count
    group = queries.shape[1] // (2 * HD)
    columns = group * toks
    core_pairs = [(i, i ^ 1) for i in range(dp_count)]
    mp_pairs = [(0, 1), (1, 0)]
    both_pairs = [(2 * i + j, 2 * (i ^ 1) + (1 - j)) for i in range(dp_count) for j in range(2)]
    requests_tile = token_request.reshape(-1, 128)

    def exchange(array, e, swap=0):
        return lax.ppermute(array, "dp", [(i, i ^ (2 * e) ^ swap) for i in range(dp_count)])

    w_got = {0: [w_key, w_value]}
    right, left = ring_send(chips, [w_key, w_value], 1), ring_send(chips, [w_key, w_value], -1)
    w_got[-1], w_got[1] = right, left
    bundle = 2 * old * PAGE + group * rows
    x_mine, x_other, kv_mine, core_send = call(
        functools.partial(split_kernel, old),
        [
            ((rows, half_width // 2), bf),
            ((rows, half_width // 2), bf),
            ((2 * old, PAGE, HD), bf),
            ((bundle, HD), bf),
        ],
        scratch=[pltpu.SemaphoreType.DMA((2 * (half_width // 512) + 2 + 2 * old + group,))],
        ins=4,
        far=(0, 1, 2, 3),
        limit=SPLIT_LIMIT,
        name="split",
    )(features, queries, key_pool, value_pool)
    core_got = lax.ppermute(core_send, "dp", core_pairs)
    x_b = lax.ppermute(x_mine, "mp", mp_pairs)
    x_c = lax.ppermute(x_other, "dp", core_pairs)
    x_d = lax.ppermute(x_other, ("dp", "mp"), both_pairs)
    q_rows, kv_other = call(
        merge_kernel,
        [((columns, HD), bf), ((2 * old, PAGE, HD), bf)],
        ins=2,
        name="merge",
    )(queries, core_got)
    q_away = exchange(q_rows, chips // 2)
    z_near, z_far = exchange(kv_mine, 2), exchange(kv_other, 2)
    y_near, y_far = exchange(kv_mine, 1), exchange(kv_other, 1)
    for d in range(2, chips // 2):
        if d == chips // 2 - 1:
            (w_first, w_second), z_near, z_far, y_near, y_far = lax.optimization_barrier(
                (right, z_near, z_far, y_near, y_far)
            )
            right = [w_first, w_second]
        right, left = ring_send(chips, right, 1), ring_send(chips, left, -1)
        w_got[-d], w_got[d] = right, left
    near = [kv_mine, y_near, z_near, exchange(y_near, 2)]
    far = [kv_other, y_far, z_far, exchange(z_far, 1)]

    inverse = (THETA ** (-(np.arange(HD) % (HD // 2)) * 2.0 / HD)).astype(np.float32)[None, :]
    scaled, squares, cosine, sine = call(
        functools.partial(scale_kernel, chips),
        [((chips, toks, 256), bf), ((toks, 128), f32), ((toks, HD), f32), ((toks, HD), f32)],
        ins=8,
        smem=(0,),
        name="scale",
    )(
        cache_lens,
        requests_tile,
        jnp.asarray(inverse),
        norm_gain.reshape(1, -1),
        x_mine,
        x_b,
        x_c,
        x_d,
    )
    w_got[chips // 2] = ring_send(chips, right[:1], 1) + ring_send(chips, left[1:], -1)
    scaled, q_away = lax.optimization_barrier((scaled, q_away))
    part_send, part_keep = call(
        functools.partial(project_kernel, chips),
        [((toks, 3 * HD), f32), ((toks, 3 * HD), f32)],
        scratch=[pltpu.VMEM((toks, 4 * HD), f32)],
        ins=2 + 2 * chips,
        name="project",
    )(scaled, squares, *[w_got[o][0] for o in offsets], *[w_got[o][1] for o in offsets])
    part_got = lax.ppermute(part_send, "dp", core_pairs)

    (fresh,) = call(
        functools.partial(rotate_kernel, width),
        [((toks, 2 * HD), bf)],
        ins=4,
        name="rotary",
    )(part_keep, part_got, cosine, sine)
    new = {0: fresh}
    new[-1], new[1] = ring_send(chips, [fresh], 1)[0], ring_send(chips, [fresh], -1)[0]
    slots = dp_count // 2 * old + STEP_PAGES
    table = pltpu.SMEM((dp_count * pages_dev,), i32)

    def cached(q, away, outs, name):
        return call(
            functools.partial(cached_kernel, chips, pages_dev, old, away),
            outs,
            scratch=[
                pltpu.VMEM((slots * PAGE, HD), bf),
                pltpu.VMEM((slots * PAGE, HD), bf),
                pltpu.VMEM((1, columns), f32),
                pltpu.VMEM((1, columns), f32),
                pltpu.VMEM((HD, columns), f32),
                table,
            ],
            ins=4 + chips,
            smem=(0, 1),
            name=name,
        )(cache_lens, page_table, requests_tile, q, *near, *far)

    (away,) = cached(q_away, chips // 2, [((HD + 16, columns), bf)], "attend_cached_away")
    here = cached(
        q_rows, 0, [((1, columns), f32), ((1, columns), f32), ((HD, columns), f32)], "attend_cached_here"
    )
    beside = {2: away, 3: here}
    for d in range(2, chips // 2):
        right, beside[d] = lax.optimization_barrier((new[1 - d], beside[d]))
        new[-d], new[d] = ring_send(chips, [right], 1)[0], ring_send(chips, [new[d - 1]], -1)[0]
    (new[chips // 2],) = ring_send(chips, [new[1 - chips // 2]], 1)
    back = exchange(beside[2], chips // 2)
    top, total, acc = beside[3]

    att_other, att_mine, rows_other, rows_mine, info = call(
        functools.partial(fresh_kernel, chips, pages_dev),
        [
            ((rows, group * HD), bf),
            ((rows, group * HD), bf),
            ((pages_dev, PAGE, 2 * HD), bf),
            ((pages_dev, PAGE, 2 * HD), bf),
            ((2 * pages_dev,), i32),
        ],
        scratch=[
            pltpu.VMEM(((chips + 2) * toks, 2 * HD), bf),
            pltpu.VMEM((1, columns), f32),
            pltpu.VMEM((1, columns), f32),
            pltpu.VMEM((HD, columns), f32),
            pltpu.VMEM((toks, group * HD), bf),
            table,
            table,
            table,
        ],
        ins=8 + chips,
        smem=(0, 1),
        out_smem=(4,),
        name="attend_new",
    )(
        cache_lens,
        page_table,
        requests_tile,
        q_rows,
        top,
        total,
        acc,
        back,
        *[new[o] for o in offsets],
    )
    rows_got = lax.ppermute(rows_other, "dp", core_pairs)
    att_got = lax.ppermute(att_other, "dp", core_pairs)
    attended, keys_out, values_out = call(
        join_kernel,
        [(queries.shape, bf), (key_pool.shape, bf), (value_pool.shape, bf)],
        ins=7,
        smem=(0,),
        name="join",
    )(info, att_mine, att_got, rows_mine, rows_got, key_pool, value_pool)
    return attended, keys_out, values_out


def solution(mesh):
    in_specs = (
        P("dp", "mp"),
        P(),
        P("dp", "mp"),
        P("dp", "mp"),
        P("dp", "mp"),
        P("dp", None, "mp"),
        P("dp", None, "mp"),
        P(),
        P(),
        P(),
    )
    out_specs = (P("dp", "mp"), P("dp", None, "mp"), P("dp", None, "mp"))
    dp_count, mp_count = mesh.shape["dp"], mesh.shape["mp"]

    def body(*args):
        even = mp_count == 2 and dp_count == 16
        if even and args[2].shape == (256, 2 * HD):
            return ring_body(dp_count, *args)
        return general_body(*args)

    return jax.shard_map(body, mesh=mesh, in_specs=in_specs, out_specs=out_specs, check_vma=False)
```

```python
import functools
import math

import jax
import jax.numpy as jnp
import numpy as np
from jax import lax
from jax.experimental import pallas as pl
from jax.experimental.pallas import tpu as pltpu
from jax.sharding import PartitionSpec as P

HD = 128
PAGE = 128
SHORT = 512
CTX_DEV = 120


THETA = 500000.0
NEG_FILL = -1e30
NEG_START = -1e29
LOG2E = 1.4426950408889634
VMEM_LIMIT = 32 * 1024 * 1024
SPLIT_LIMIT = 63 * 1024 * 1024
STEP_PAGES = 4


def rotate(values, positions, head_size):
    halfway = head_size // 2
    inverse = THETA ** (-(jnp.arange(halfway, dtype=jnp.float32) * 2.0) / head_size)
    angles = positions.astype(jnp.float32)[:, None] * inverse[None, :]
    cosine = jnp.cos(angles)[:, None, :]
    sine = jnp.sin(angles)[:, None, :]
    first_half = values[..., :halfway]
    second_half = values[..., halfway:]
    return jnp.concatenate(
        [first_half * cosine - second_half * sine, second_half * cosine + first_half * sine],
        axis=-1,
    )


def general_body(
    features,
    norm_gain,
    w_key,
    w_value,
    queries,
    key_pool,
    value_pool,
    cache_lens,
    page_table,
    token_request,
):
    gathered = lax.all_gather(features, "mp", axis=1, tiled=True)
    widened = gathered.astype(jnp.float32)
    mean_square = jnp.mean(widened * widened, axis=1, keepdims=True)
    normed = (widened * lax.rsqrt(mean_square + 1e-05) * norm_gain.astype(jnp.float32)).astype(
        jnp.bfloat16
    )
    tok_rows = features.shape[0]
    kv_width = w_key.shape[1]
    head_size = HD
    kv_heads = kv_width // head_size
    q_heads = queries.shape[1] // head_size
    group_size = q_heads // kv_heads
    scale = 1.0 / math.sqrt(head_size)
    pieces = (
        lax.all_gather(w_key, "dp", axis=0, tiled=True),
        lax.all_gather(w_value, "dp", axis=0, tiled=True),
    )
    key_sums = jnp.dot(normed, pieces[0], preferred_element_type=jnp.float32)
    value_sums = jnp.dot(normed, pieces[1], preferred_element_type=jnp.float32)
    total_new = token_request.shape[0]
    requests = cache_lens.shape[0]
    request_ids = jnp.arange(requests, dtype=jnp.int32)
    member = (token_request[:, None] == request_ids[None, :]).astype(jnp.int32)
    counts = jnp.sum(member, axis=0)
    starts = jnp.cumsum(counts) - counts
    token_index = jnp.arange(total_new, dtype=jnp.int32)
    token_pos = jnp.sum(member * (cache_lens - starts)[None, :], axis=1) + token_index
    dp_index = lax.axis_index("dp")
    dp_count = lax.axis_size("dp")
    first_token = dp_index * tok_rows
    my_request = lax.dynamic_slice_in_dim(token_request, first_token, tok_rows)
    my_pos = lax.dynamic_slice_in_dim(token_pos, first_token, tok_rows)
    key_heads = rotate(key_sums.reshape(tok_rows, kv_heads, head_size), my_pos, head_size)
    new_keys = key_heads.reshape(tok_rows, kv_width).astype(jnp.bfloat16)
    new_values = value_sums.astype(jnp.bfloat16)
    pages_dev = key_pool.shape[0]
    page_rows = key_pool.shape[1]
    max_pages = page_table.shape[1]
    slot_all = jnp.take(page_table.reshape(-1), token_request * max_pages + token_pos // page_rows)
    local_slot = slot_all - dp_index * pages_dev
    owned = (local_slot >= 0) & (local_slot < pages_dev)
    dest_all = jnp.where(
        owned, local_slot * page_rows + token_pos % page_rows, pages_dev * page_rows
    )
    long_pages = (CTX_DEV * dp_count + PAGE - 1) // PAGE
    old_dev = (long_pages + 2 * ((SHORT + PAGE - 1) // PAGE) + dp_count - 1) // dp_count
    old_total = old_dev * dp_count
    old_ids = jnp.arange(old_total, dtype=jnp.int32)
    old_phys = old_ids // old_dev * pages_dev + old_ids % old_dev
    matches = (page_table[None, :, :] == old_phys[:, None, None]).astype(jnp.int32)
    page_has = jnp.sum(matches, axis=(1, 2)) > 0
    page_request = jnp.sum(matches * request_ids[None, :, None], axis=(1, 2))
    page_logical = jnp.sum(
        matches * jnp.arange(max_pages, dtype=jnp.int32)[None, None, :], axis=(1, 2)
    )
    page_limit = jnp.sum(matches * cache_lens[None, :, None], axis=(1, 2))
    q_local = queries.reshape(tok_rows, kv_heads, group_size, head_size)

    def attend(att_state, keys_flat, values_flat, key_info):
        key_request, key_pos, key_ok = key_info
        visible = (
            key_ok[None, :]
            & (key_request[None, :] == my_request[:, None])
            & (key_pos[None, :] <= my_pos[:, None])
        )
        keys_shaped = keys_flat.reshape(keys_flat.shape[0], kv_heads, head_size)
        values_shaped = values_flat.reshape(values_flat.shape[0], kv_heads, head_size)
        running_max, running_sum, running_acc = att_state
        scores = (
            jnp.einsum("thgd,khd->thgk", q_local, keys_shaped, preferred_element_type=jnp.float32)
            * scale
        )
        mask_full = visible[:, None, None, :]
        masked = jnp.where(mask_full, scores, NEG_FILL)
        new_max = jnp.maximum(running_max, jnp.max(masked, axis=-1))
        factor = jnp.exp(running_max - new_max)
        soft_weights = jnp.where(mask_full, jnp.exp(masked - new_max[..., None]), 0.0)
        new_sum = running_sum * factor + jnp.sum(soft_weights, axis=-1)
        new_acc = running_acc * factor[..., None] + jnp.einsum(
            "thgk,khd->thgd",
            soft_weights.astype(jnp.bfloat16),
            values_shaped,
            preferred_element_type=jnp.float32,
        )
        return (new_max, new_sum, new_acc)

    def attend_rows(att_state, keys_flat, values_flat, key_info):
        row_count = keys_flat.shape[0]
        key_block = 2048
        if row_count > key_block and row_count % key_block == 0:
            blocks = row_count // key_block
            stacked = (
                keys_flat.reshape(blocks, key_block, kv_width),
                values_flat.reshape(blocks, key_block, kv_width),
                key_info[0].reshape(blocks, key_block),
                key_info[1].reshape(blocks, key_block),
                key_info[2].reshape(blocks, key_block),
            )

            def step_block(inner_state, slab_parts):
                return (
                    attend(
                        inner_state,
                        slab_parts[0],
                        slab_parts[1],
                        (slab_parts[2], slab_parts[3], slab_parts[4]),
                    ),
                    None,
                )

            att_state, unused = lax.scan(step_block, att_state, stacked)
            return att_state
        return attend(att_state, keys_flat, values_flat, key_info)

    start_state = (
        jnp.full((tok_rows, kv_heads, group_size), NEG_FILL, jnp.float32),
        jnp.zeros((tok_rows, kv_heads, group_size), jnp.float32),
        jnp.zeros((tok_rows, kv_heads, group_size, head_size), jnp.float32),
    )
    flat_keys = key_pool.reshape(pages_dev * page_rows, kv_width)
    flat_values = value_pool.reshape(pages_dev * page_rows, kv_width)
    old_keys = key_pool[:old_dev]
    old_values = value_pool[:old_dev]
    pieces = (
        lax.all_gather(old_keys, "dp", axis=0, tiled=True),
        lax.all_gather(old_values, "dp", axis=0, tiled=True),
    )
    page_count = pieces[0].shape[0]
    cached_keys = pieces[0].reshape(page_count * page_rows, kv_width)
    cached_values = pieces[1].reshape(page_count * page_rows, kv_width)
    row_ids = jnp.arange(page_rows, dtype=jnp.int32)[None, :]
    key_pos = page_logical[:, None] * page_rows + row_ids
    key_ok = page_has[:, None] & (key_pos < page_limit[:, None])
    key_request = jnp.broadcast_to(page_request[:, None], (page_count, page_rows))
    middle_state = attend_rows(
        start_state,
        cached_keys,
        cached_values,
        (key_request.reshape(-1), key_pos.reshape(-1), key_ok.reshape(-1)),
    )
    pieces = (
        lax.all_gather(new_keys, "dp", axis=0, tiled=True),
        lax.all_gather(new_values, "dp", axis=0, tiled=True),
    )
    att_state = middle_state
    pool_keys = flat_keys
    pool_values = flat_values
    key_request = token_request
    key_pos = token_pos
    att_state = attend_rows(
        att_state,
        pieces[0],
        pieces[1],
        (key_request, key_pos, jnp.ones((pieces[0].shape[0],), jnp.bool_)),
    )
    pool_keys, pool_values = (
        pool_keys.at[dest_all].set(pieces[0], mode="drop"),
        pool_values.at[dest_all].set(pieces[1], mode="drop"),
    )
    final_state, pool_keys, pool_values = (att_state, pool_keys, pool_values)
    final_max, final_sum, final_acc = final_state
    attended = (
        (final_acc / final_sum[..., None])
        .reshape(tok_rows, q_heads * head_size)
        .astype(jnp.bfloat16)
    )
    return (attended, pool_keys.reshape(key_pool.shape), pool_values.reshape(value_pool.shape))


def ring_chip(pos, chips):
    pos = pos % chips
    return jnp.where(pos < chips // 2, 2 * pos, 2 * chips - 1 - 2 * pos)


def ring_place(chip, chips):
    return jnp.where(chip % 2 == 0, chip // 2, (2 * chips - 1 - chip) // 2)


def ring_pairs(chips, step, swap):
    order = [2 * k if k < chips // 2 else 2 * chips - 1 - 2 * k for k in range(chips)]
    return [
        (2 * order[k] + core, 2 * order[(k + step) % chips] + (core ^ swap))
        for k in range(chips)
        for core in range(2)
    ]


def ring_offsets(chips):
    return [0] + [o for d in range(1, chips // 2) for o in (d, -d)] + [chips // 2]


def request_starts(tr_ref, requests):
    tr = tr_ref[...]
    starts = [jnp.int32(0)]
    for r in range(1, requests):
        starts.append(jnp.sum(jnp.where(tr < r, 1.0, 0.0)).astype(jnp.int32))
    starts.append(jnp.int32(tr.shape[0] * tr.shape[1]))
    return starts


def pick(cond_starts, values, tokens):
    out = jnp.zeros_like(tokens) + values[0]
    for r in range(1, len(values)):
        out = jnp.where(tokens >= cond_starts[r], values[r], out)
    return out


def chip_requests(chip, toks, starts):
    first, last = jnp.int32(0), jnp.int32(0)
    for start in starts[1:-1]:
        first = first + (chip * toks >= start).astype(jnp.int32)
        last = last + (chip * toks + toks - 1 >= start).astype(jnp.int32)
    return first, last


def split_kernel(old, f_ref, q_ref, kp_ref, vp_ref, xc_ref, xo_ref, kvc_ref, out_ref, sems):
    core = lax.axis_index("dp") % 2
    copies = []

    def copy(source, target):
        copies.append(pltpu.make_async_copy(source, target, sems.at[len(copies)]))
        copies[-1].start()

    rows = f_ref.shape[0]
    half = q_ref.shape[1] // 2
    mine = pl.ds(pl.multiple_of(core * HD, HD), HD)
    other = pl.ds(pl.multiple_of((1 - core) * HD, HD), HD)
    for out, own in ((xo_ref, 1 - core), (xc_ref, core)):
        for m in range(f_ref.shape[1] // 512):
            at = pl.ds(pl.multiple_of((2 * m + own) * 256, 256), 256)
            copy(f_ref.at[:, at], out.at[:, pl.ds(m * 256, 256)])
    at = 0
    for n, ref in enumerate((kp_ref, vp_ref)):
        copy(ref.at[pl.ds(0, old), :, mine], kvc_ref.at[pl.ds(n * old, old)])
        for p in range(old):
            copy(ref.at[p, :, other], out_ref.at[pl.ds(at, PAGE), :])
            at += PAGE
    for h in range(half // HD):
        lane = pl.multiple_of((1 - core) * half + h * HD, HD)
        copy(q_ref.at[:, pl.ds(lane, HD)], out_ref.at[pl.ds(at, rows), :])
        at += rows
    for c in copies:
        c.wait()


def merge_kernel(q_ref, got_ref, qs_ref, kv_ref):
    core = lax.axis_index("dp") % 2
    count = kv_ref.shape[0]
    rows, group = q_ref.shape[0], q_ref.shape[1] // (2 * HD)
    for n in range(count):
        kv_ref[n] = got_ref[n * PAGE : (n + 1) * PAGE, :]
    for h in range(group):
        mine = pl.ds(pl.multiple_of((2 * h + core) * rows, rows), rows)
        other = pl.ds(pl.multiple_of((2 * h + 1 - core) * rows, rows), rows)
        qs_ref[mine, :] = q_ref[:, pl.ds(pl.multiple_of((core * group + h) * HD, HD), HD)]
        first = count * PAGE + h * rows
        qs_ref[other, :] = got_ref[first : first + rows, :]


def scale_kernel(
    chips, lens_ref, tr_ref, inv_ref, gain_ref, a_ref, b_ref, c_ref, d_ref, xs_ref, ss_ref, cos_ref, sin_ref
):
    dp = lax.axis_index("dp")
    mp = lax.axis_index("mp")
    chip, core = dp // 2, dp % 2
    rows = a_ref.shape[0]
    per_half = a_ref.shape[1] // 256
    for first, second, owner in ((a_ref, b_ref, core), (c_ref, d_ref, 1 - core)):
        at = pl.ds(pl.multiple_of(owner * rows, rows), rows)
        total = jnp.zeros((rows, 256), jnp.float32)
        for ref, half in ((first, mp), (second, 1 - mp)):
            for m in range(per_half):
                wide = ref[:, m * 256 : (m + 1) * 256].astype(jnp.float32)
                block = half * (2 * per_half) + 2 * m + core
                gain = gain_ref[:, pl.ds(pl.multiple_of(block * 256, 256), 256)].astype(jnp.float32)
                total = total + wide * wide
                xs_ref[half * per_half + m, at, :] = (wide * gain).astype(jnp.bfloat16)
        ss_ref[at, :] = jnp.broadcast_to(jnp.sum(total, axis=1, keepdims=True), (rows, 128))
    requests = lens_ref.shape[0]
    starts = request_starts(tr_ref, requests)
    tokens = chip * (2 * rows) + lax.broadcasted_iota(jnp.int32, (2 * rows, 128), 0)
    shift = pick(starts, [lens_ref[r] - starts[r] for r in range(requests)], tokens)
    angles = (tokens + shift).astype(jnp.float32) * inv_ref[...]
    lane = lax.broadcasted_iota(jnp.int32, (2 * rows, 128), 1)
    sine = jnp.sin(angles)
    cos_ref[...] = jnp.cos(angles)
    sin_ref[...] = jnp.where(lane < HD // 2, -sine, sine)


def project_kernel(chips, xs_ref, ss_ref, *refs):
    keys, values = refs[:chips], refs[chips : 2 * chips]
    send_ref, keep_ref, acc_ref = refs[2 * chips :]
    dp = lax.axis_index("dp")
    chip, core = dp // 2, dp % 2
    place = ring_place(chip, chips)
    ksum = jnp.zeros((xs_ref.shape[1], 2 * HD), jnp.float32)
    vsum = jnp.zeros((xs_ref.shape[1], 2 * HD), jnp.float32)
    for n, offset in enumerate(ring_offsets(chips)):
        x = xs_ref[ring_chip(place + offset + chips, chips)]
        ksum = ksum + jnp.dot(x, keys[n][...], preferred_element_type=jnp.float32)
        vsum = vsum + jnp.dot(x, values[n][...], preferred_element_type=jnp.float32)
    acc_ref[:, : 2 * HD] = ksum
    acc_ref[:, 2 * HD :] = vsum
    for ref, head in ((send_ref, 1 - core), (keep_ref, core)):
        ref[:, :HD] = acc_ref[:, pl.ds(pl.multiple_of(head * HD, HD), HD)]
        ref[:, HD : 2 * HD] = acc_ref[:, pl.ds(pl.multiple_of((2 + head) * HD, HD), HD)]
        ref[:, 2 * HD :] = ss_ref[...]


def rotate_kernel(width, keep_ref, got_ref, cos_ref, sin_ref, out_ref):
    total = keep_ref[...] + got_ref[...]
    inverse = lax.rsqrt(total[:, 2 * HD :] * (1.0 / width) + 1e-05)
    key = total[:, :HD] * inverse
    rolled = pltpu.roll(key, HD // 2, 1)
    out_ref[:, :HD] = (key * cos_ref[...] + rolled * sin_ref[...]).astype(jnp.bfloat16)
    out_ref[:, HD:] = (total[:, HD : 2 * HD] * inverse).astype(jnp.bfloat16)


def attend_block(qs_ref, keys, values, first, low, high, m_ref, l_ref, acc_ref):
    scores = lax.dot_general(keys, qs_ref[...], (((1,), (1,)), ((), ())), preferred_element_type=jnp.float32)
    ids = first + lax.broadcasted_iota(jnp.int32, scores.shape, 0)
    scores = jnp.where((ids >= low) & (ids < high), scores * (LOG2E / math.sqrt(HD)), NEG_FILL)
    before = m_ref[...]
    top = jnp.maximum(before, jnp.max(scores, axis=0, keepdims=True))
    shrink = jnp.exp2(before - top)
    weights = jnp.exp2(scores - top)
    m_ref[...] = top
    l_ref[...] = l_ref[...] * shrink + jnp.sum(weights, axis=0, keepdims=True)
    acc_ref[...] = acc_ref[...] * shrink + lax.dot_general(
        values,
        weights.astype(jnp.bfloat16),
        (((0,), (0,)), ((), ())),
        preferred_element_type=jnp.float32,
    )


def three_parts(x):
    first = x.astype(jnp.bfloat16).astype(jnp.float32)
    second = (x - first).astype(jnp.bfloat16).astype(jnp.float32)
    return jnp.concatenate([first, second, x - first - second], axis=0)


def cached_kernel(chips, pages_dev, old, away, lens_ref, table_ref, tr_ref, qs_ref, *refs):
    members = chips // 2
    near, far = refs[:members], refs[members : 2 * members]
    outs, (kbuf, vbuf, m_ref, l_ref, acc_ref, slot_of) = refs[2 * members : -6], refs[-6:]
    dp = lax.axis_index("dp")
    chip, core = dp // 2, dp % 2
    who = chip ^ away
    requests = lens_ref.shape[0]
    width = qs_ref.shape[0]
    toks = tr_ref.shape[0] * tr_ref.shape[1] // chips
    starts = request_starts(tr_ref, requests)
    first_req, last_req = chip_requests(who, toks, starts)

    def clear(i, carry):
        slot_of[i] = -1
        return carry

    lax.fori_loop(0, slot_of.shape[0], clear, 0)
    base = jnp.int32(0)
    lows, highs = [], []
    for r in range(requests):
        length = lens_ref[r]
        relevant = (r >= first_req) & (r <= last_req)
        count = jnp.where(relevant, (length + PAGE - 1) // PAGE, 0)

        def place(l, at, r=r):
            page = table_ref[r, l]
            held = page // (2 * pages_dev * members) == chip // members

            @pl.when(held)
            def _():
                slot_of[page] = at

            return at + held.astype(jnp.int32)

        end = lax.fori_loop(0, count, place, base)
        last_page = table_ref[r, (length + PAGE - 1) // PAGE - 1]
        cut = jnp.where(
            (end > base) & (last_page // (2 * pages_dev * members) == chip // members),
            (length + PAGE - 1) // PAGE * PAGE - length,
            0,
        )
        lows.append(base * PAGE)
        highs.append(end * PAGE - cut)
        base = end

    for e in range(members):
        source = chip ^ e
        for block, owner in ((near[e], 2 * source + core), (far[e], 2 * source + 1 - core)):
            for s in range(old):
                slot = slot_of[owner * pages_dev + s]

                @pl.when(slot >= 0)
                def _(block=block, s=s, slot=slot):
                    at = pl.ds(pl.multiple_of(slot * PAGE, PAGE), PAGE)
                    kbuf[at, :] = block[s]
                    vbuf[at, :] = block[old + s]

    step_pages = STEP_PAGES
    pad = pl.ds(pl.multiple_of(base * PAGE, PAGE), (step_pages - 1) * PAGE)
    kbuf[pad, :] = jnp.zeros(((step_pages - 1) * PAGE, HD), kbuf.dtype)
    vbuf[pad, :] = jnp.zeros(((step_pages - 1) * PAGE, HD), vbuf.dtype)
    tokens = who * toks + lax.broadcasted_iota(jnp.int32, (1, width), 1) % toks
    low = pick(starts, lows, tokens)
    high = pick(starts, highs, tokens)
    m_ref[...] = jnp.full(m_ref.shape, NEG_START, jnp.float32)
    l_ref[...] = jnp.zeros(l_ref.shape, jnp.float32)
    acc_ref[...] = jnp.zeros(acc_ref.shape, jnp.float32)

    def step(i, carry):
        size = step_pages * PAGE
        at = pl.ds(pl.multiple_of(i * size, size), size)
        attend_block(qs_ref, kbuf[at, :], vbuf[at, :], i * size, low, high, m_ref, l_ref, acc_ref)
        return carry

    lax.fori_loop(0, (base + step_pages - 1) // step_pages, step, 0)
    if away:
        outs[0][:HD, :] = acc_ref[...].astype(jnp.bfloat16)
        outs[0][HD:, :] = jnp.concatenate(
            [three_parts(m_ref[...]), three_parts(l_ref[...]), jnp.zeros((10, width), jnp.float32)], axis=0
        ).astype(jnp.bfloat16)
    else:
        outs[0][...], outs[1][...], outs[2][...] = m_ref[...], l_ref[...], acc_ref[...]


def fresh_kernel(
    chips, pages_dev, lens_ref, table_ref, tr_ref, qs_ref, m0_ref, l0_ref, acc0_ref, back_ref, *refs
):
    fresh = refs[:chips]
    atto_ref, attc_ref, no_ref, nc_ref, info_ref = refs[chips : chips + 5]
    nbuf, m_ref, l_ref, acc_ref, out_ref, new_at, new_lo, new_hi = refs[chips + 5 :]
    dp = lax.axis_index("dp")
    chip, core = dp // 2, dp % 2
    place = ring_place(chip, chips)
    toks = fresh[0].shape[0]
    rows = toks // 2
    requests = lens_ref.shape[0]
    width = qs_ref.shape[0]
    group = width // toks
    starts = request_starts(tr_ref, requests)
    reqs = chip_requests(chip, toks, starts)
    first_req = reqs[0]
    parts = back_ref[HD : HD + 6, :].astype(jnp.float32)
    m0, m1 = m0_ref[...], parts[0:1] + parts[1:2] + parts[2:3]
    top = jnp.maximum(m0, m1)
    f0, f1 = jnp.exp2(m0 - top), jnp.exp2(m1 - top)
    m_ref[...] = top
    l_ref[...] = l0_ref[...] * f0 + (parts[3:4] + parts[4:5] + parts[5:6]) * f1
    acc_ref[...] = acc0_ref[...] * f0 + back_ref[:HD, :].astype(jnp.float32) * f1

    def clear(i, carry):
        new_lo[i] = 0
        new_hi[i] = 0
        return carry

    lax.fori_loop(0, new_lo.shape[0], clear, 0)
    for r in range(requests):
        length = lens_ref[r]

        def place_new(l, carry, r=r, length=length):
            at = l * PAGE - length + starts[r]
            page = table_ref[r, l]
            new_at[page] = at
            new_lo[page] = jnp.maximum(starts[r] - at, 0)
            new_hi[page] = jnp.minimum(starts[r + 1] - at, PAGE)
            return carry

        end = (length + starts[r + 1] - starts[r] + PAGE - 1) // PAGE
        lax.fori_loop(length // PAGE, end, place_new, 0)

    for n, offset in enumerate(ring_offsets(chips)):
        source = ring_chip(place + offset + chips, chips)
        nbuf[pl.ds(pl.multiple_of((source + 1) * toks, toks), toks), :] = fresh[n][...]
    nbuf[:toks, :] = jnp.zeros((toks, 2 * HD), nbuf.dtype)
    nbuf[(chips + 1) * toks :, :] = jnp.zeros((toks, 2 * HD), nbuf.dtype)

    tokens = chip * toks + lax.broadcasted_iota(jnp.int32, (1, width), 1) % toks
    low = pick(starts, starts[:requests], tokens)
    first_start = starts[0]
    for r in range(1, requests):
        first_start = jnp.where(first_req == r, starts[r], first_start)

    def step(b, carry):
        at = pl.ds(pl.multiple_of((b + 1) * toks, toks), toks)
        attend_block(qs_ref, nbuf[at, :HD], nbuf[at, HD:], b * toks, low, tokens + 1, m_ref, l_ref, acc_ref)
        return carry

    lax.fori_loop(first_start // toks, chip + 1, step, 0)
    result = acc_ref[...] / l_ref[...]
    for h in range(group):
        out_ref[:, h * HD : (h + 1) * HD] = result[:, h * toks : (h + 1) * toks].T.astype(jnp.bfloat16)
    attc_ref[...] = out_ref[pl.ds(pl.multiple_of(core * rows, rows), rows), :]
    atto_ref[...] = out_ref[pl.ds(pl.multiple_of((1 - core) * rows, rows), rows), :]

    row = lax.broadcasted_iota(jnp.int32, (PAGE, 2 * toks), 0)
    column = lax.broadcasted_iota(jnp.int32, (PAGE, 2 * toks), 1)
    for ref, owner in ((no_ref, dp + 1 - 2 * core), (nc_ref, dp)):
        for s in range(pages_dev):
            page = owner * pages_dev + s
            at, low_row, high_row = new_at[page], new_lo[page], new_hi[page]

            @pl.when(high_row > low_row)
            def _(ref=ref, s=s, at=at, low_row=low_row, high_row=high_row):
                shifted = at + toks
                first = pl.multiple_of(shifted // toks * toks, toks)
                chosen = (column + first == row + shifted) & (row >= low_row) & (row < high_row)
                ref[s] = jnp.dot(
                    jnp.where(chosen, 1.0, 0.0).astype(jnp.bfloat16),
                    nbuf[pl.ds(first, 2 * toks), :],
                    preferred_element_type=jnp.float32,
                ).astype(jnp.bfloat16)

    for s in range(pages_dev):
        info_ref[2 * s] = new_lo[dp * pages_dev + s]
        info_ref[2 * s + 1] = new_hi[dp * pages_dev + s]


def join_kernel(info_ref, attc_ref, attr_ref, nc_ref, nr_ref, kp_ref, vp_ref, att_ref, ko_ref, vo_ref):
    core = lax.axis_index("dp") % 2
    half = attc_ref.shape[1]
    att_ref[:, pl.ds(pl.multiple_of(core * half, HD), half)] = attc_ref[...]
    att_ref[:, pl.ds(pl.multiple_of((1 - core) * half, HD), half)] = attr_ref[...]
    row = lax.broadcasted_iota(jnp.int32, (PAGE, HD), 0)
    for s in range(kp_ref.shape[0]):
        chosen = (row >= info_ref[2 * s]) & (row < info_ref[2 * s + 1])
        for ref, head in ((nc_ref, core), (nr_ref, 1 - core)):
            at = pl.ds(pl.multiple_of(head * HD, HD), HD)
            ko_ref[s, :, at] = jnp.where(chosen, ref[s, :, :HD], kp_ref[s, :, at])
            vo_ref[s, :, at] = jnp.where(chosen, ref[s, :, HD:], vp_ref[s, :, at])


def call(
    kernel, outs, scratch=(), ins=None, smem=(), far=(), out_smem=(), out_far=(), limit=VMEM_LIMIT, name=None
):
    vmem, sm = pl.BlockSpec(memory_space=pltpu.VMEM), pl.BlockSpec(memory_space=pltpu.SMEM)
    hbm = pl.BlockSpec(memory_space=pl.ANY)
    return pl.pallas_call(
        kernel,
        out_shape=[jax.ShapeDtypeStruct(s, d) for s, d in outs],
        in_specs=[sm if n in smem else hbm if n in far else vmem for n in range(ins)],
        out_specs=[sm if n in out_smem else hbm if n in out_far else vmem for n in range(len(outs))],
        scratch_shapes=list(scratch),
        compiler_params=pltpu.CompilerParams(vmem_limit_bytes=limit),
        name=name,
    )


def ring_send(chips, arrays, step, swap=0):
    return [lax.ppermute(a, "dp", ring_pairs(chips, step, swap * n)) for n, a in enumerate(arrays)]


def ring_body(
    dp_count,
    features,
    norm_gain,
    w_key,
    w_value,
    queries,
    key_pool,
    value_pool,
    cache_lens,
    page_table,
    token_request,
):
    bf, f32, i32 = jnp.bfloat16, jnp.float32, jnp.int32
    chips = dp_count // 2
    offsets = ring_offsets(chips)
    rows, half_width = features.shape
    width = norm_gain.shape[0]
    toks = 2 * rows
    pages_dev = key_pool.shape[0]
    long_pages = (CTX_DEV * dp_count + PAGE - 1) // PAGE
    old = (long_pages + 2 * ((SHORT + PAGE - 1) // PAGE) + dp_count - 1) // dp_count
    group = queries.shape[1] // (2 * HD)
    columns = group * toks
    core_pairs = [(i, i ^ 1) for i in range(dp_count)]
    mp_pairs = [(0, 1), (1, 0)]
    both_pairs = [(2 * i + j, 2 * (i ^ 1) + (1 - j)) for i in range(dp_count) for j in range(2)]
    requests_tile = token_request.reshape(-1, 128)

    def exchange(array, e, swap=0):
        return lax.ppermute(array, "dp", [(i, i ^ (2 * e) ^ swap) for i in range(dp_count)])

    w_got = {0: [w_key, w_value]}
    right, left = ring_send(chips, [w_key, w_value], 1), ring_send(chips, [w_key, w_value], -1)
    w_got[-1], w_got[1] = right, left
    bundle = 2 * old * PAGE + group * rows
    x_mine, x_other, kv_mine, core_send = call(
        functools.partial(split_kernel, old),
        [
            ((rows, half_width // 2), bf),
            ((rows, half_width // 2), bf),
            ((2 * old, PAGE, HD), bf),
            ((bundle, HD), bf),
        ],
        scratch=[pltpu.SemaphoreType.DMA((2 * (half_width // 512) + 2 + 2 * old + group,))],
        ins=4,
        far=(0, 1, 2, 3),
        limit=SPLIT_LIMIT,
        name="split",
    )(features, queries, key_pool, value_pool)
    core_got = lax.ppermute(core_send, "dp", core_pairs)
    x_b = lax.ppermute(x_mine, "mp", mp_pairs)
    x_c = lax.ppermute(x_other, "dp", core_pairs)
    x_d = lax.ppermute(x_other, ("dp", "mp"), both_pairs)
    q_rows, kv_other = call(
        merge_kernel,
        [((columns, HD), bf), ((2 * old, PAGE, HD), bf)],
        ins=2,
        name="merge",
    )(queries, core_got)
    for d in range(2, chips // 2):
        right, left = ring_send(chips, right, 1), ring_send(chips, left, -1)
        w_got[-d], w_got[d] = right, left
    inverse = (THETA ** (-(np.arange(HD) % (HD // 2)) * 2.0 / HD)).astype(np.float32)[None, :]
    scaled, squares, cosine, sine = call(
        functools.partial(scale_kernel, chips),
        [((chips, toks, 256), bf), ((toks, 128), f32), ((toks, HD), f32), ((toks, HD), f32)],
        ins=8,
        smem=(0,),
        name="scale",
    )(
        cache_lens,
        requests_tile,
        jnp.asarray(inverse),
        norm_gain.reshape(1, -1),
        x_mine,
        x_b,
        x_c,
        x_d,
    )
    w_got[chips // 2] = ring_send(chips, right[:1], 1) + ring_send(chips, left[1:], -1)
    scaled, q_rows, kv_other = lax.optimization_barrier((scaled, q_rows, kv_other))
    part_send, part_keep = call(
        functools.partial(project_kernel, chips),
        [((toks, 3 * HD), f32), ((toks, 3 * HD), f32)],
        scratch=[pltpu.VMEM((toks, 4 * HD), f32)],
        ins=2 + 2 * chips,
        name="project",
    )(scaled, squares, *[w_got[o][0] for o in offsets], *[w_got[o][1] for o in offsets])
    part_got = lax.ppermute(part_send, "dp", core_pairs)

    first_near, first_far, _ = lax.optimization_barrier((kv_mine, kv_other, part_send))
    z_near, z_far = exchange(first_near, 2), exchange(first_far, 2)
    y_near, y_far = exchange(first_near, 1), exchange(first_far, 1)
    (fresh,) = call(
        functools.partial(rotate_kernel, width),
        [((toks, 2 * HD), bf)],
        ins=4,
        name="rotary",
    )(part_keep, part_got, cosine, sine)
    new = {0: fresh}
    new[-1], new[1] = ring_send(chips, [fresh], 1)[0], ring_send(chips, [fresh], -1)[0]
    late_y, late_z, late_q, _ = lax.optimization_barrier((y_near, z_far, q_rows, fresh))
    q_away = exchange(late_q, chips // 2)
    near = [kv_mine, y_near, z_near, exchange(late_y, 2)]
    far = [kv_other, y_far, z_far, exchange(late_z, 1)]
    slots = dp_count // 2 * old + STEP_PAGES
    table = pltpu.SMEM((dp_count * pages_dev,), i32)

    def cached(q, away, outs, name):
        return call(
            functools.partial(cached_kernel, chips, pages_dev, old, away),
            outs,
            scratch=[
                pltpu.VMEM((slots * PAGE, HD), bf),
                pltpu.VMEM((slots * PAGE, HD), bf),
                pltpu.VMEM((1, columns), f32),
                pltpu.VMEM((1, columns), f32),
                pltpu.VMEM((HD, columns), f32),
                table,
            ],
            ins=4 + chips,
            smem=(0, 1),
            name=name,
        )(cache_lens, page_table, requests_tile, q, *near, *far)

    (away,) = cached(q_away, chips // 2, [((HD + 16, columns), bf)], "attend_cached_away")
    here = cached(
        q_rows, 0, [((1, columns), f32), ((1, columns), f32), ((HD, columns), f32)], "attend_cached_here"
    )
    beside = {2: away, 3: here}
    for d in range(2, chips // 2):
        right, left, beside[d] = lax.optimization_barrier((new[1 - d], new[d - 1], beside[d]))
        new[-d], new[d] = ring_send(chips, [right], 1)[0], ring_send(chips, [left], -1)[0]
    (new[chips // 2],) = ring_send(chips, [new[1 - chips // 2]], 1)
    back = exchange(beside[2], chips // 2)
    top, total, acc = beside[3]

    att_other, att_mine, rows_other, rows_mine, info = call(
        functools.partial(fresh_kernel, chips, pages_dev),
        [
            ((rows, group * HD), bf),
            ((rows, group * HD), bf),
            ((pages_dev, PAGE, 2 * HD), bf),
            ((pages_dev, PAGE, 2 * HD), bf),
            ((2 * pages_dev,), i32),
        ],
        scratch=[
            pltpu.VMEM(((chips + 2) * toks, 2 * HD), bf),
            pltpu.VMEM((1, columns), f32),
            pltpu.VMEM((1, columns), f32),
            pltpu.VMEM((HD, columns), f32),
            pltpu.VMEM((toks, group * HD), bf),
            table,
            table,
            table,
        ],
        ins=8 + chips,
        smem=(0, 1),
        out_smem=(4,),
        name="attend_new",
    )(
        cache_lens,
        page_table,
        requests_tile,
        q_rows,
        top,
        total,
        acc,
        back,
        *[new[o] for o in offsets],
    )
    rows_got = lax.ppermute(rows_other, "dp", core_pairs)
    att_got = lax.ppermute(att_other, "dp", core_pairs)
    attended, keys_out, values_out = call(
        join_kernel,
        [(queries.shape, bf), (key_pool.shape, bf), (value_pool.shape, bf)],
        ins=7,
        smem=(0,),
        name="join",
    )(info, att_mine, att_got, rows_mine, rows_got, key_pool, value_pool)
    return attended, keys_out, values_out


def solution(mesh):
    in_specs = (
        P("dp", "mp"),
        P(),
        P("dp", "mp"),
        P("dp", "mp"),
        P("dp", "mp"),
        P("dp", None, "mp"),
        P("dp", None, "mp"),
        P(),
        P(),
        P(),
    )
    out_specs = (P("dp", "mp"), P("dp", None, "mp"), P("dp", None, "mp"))
    dp_count, mp_count = mesh.shape["dp"], mesh.shape["mp"]

    def body(*args):
        even = mp_count == 2 and dp_count == 16
        if even and args[2].shape == (256, 2 * HD):
            return ring_body(dp_count, *args)
        return general_body(*args)

    return jax.shard_map(body, mesh=mesh, in_specs=in_specs, out_specs=out_specs, check_vma=False)
```

```python
import functools
import math

import jax
import jax.numpy as jnp
import numpy as np
from jax import lax
from jax.experimental import pallas as pl
from jax.experimental.pallas import tpu as pltpu
from jax.sharding import PartitionSpec as P

HD = 128
PAGE = 128
SHORT = 512
CTX_DEV = 120


THETA = 500000.0
NEG_FILL = -1e30
NEG_START = -1e29
LOG2E = 1.4426950408889634
VMEM_LIMIT = 32 * 1024 * 1024
SPLIT_LIMIT = 63 * 1024 * 1024
STEP_PAGES = 4


def rotate(values, positions, head_size):
    halfway = head_size // 2
    inverse = THETA ** (-(jnp.arange(halfway, dtype=jnp.float32) * 2.0) / head_size)
    angles = positions.astype(jnp.float32)[:, None] * inverse[None, :]
    cosine = jnp.cos(angles)[:, None, :]
    sine = jnp.sin(angles)[:, None, :]
    first_half = values[..., :halfway]
    second_half = values[..., halfway:]
    return jnp.concatenate(
        [first_half * cosine - second_half * sine, second_half * cosine + first_half * sine],
        axis=-1,
    )


def general_body(
    features,
    norm_gain,
    w_key,
    w_value,
    queries,
    key_pool,
    value_pool,
    cache_lens,
    page_table,
    token_request,
):
    gathered = lax.all_gather(features, "mp", axis=1, tiled=True)
    widened = gathered.astype(jnp.float32)
    mean_square = jnp.mean(widened * widened, axis=1, keepdims=True)
    normed = (widened * lax.rsqrt(mean_square + 1e-05) * norm_gain.astype(jnp.float32)).astype(
        jnp.bfloat16
    )
    tok_rows = features.shape[0]
    kv_width = w_key.shape[1]
    head_size = HD
    kv_heads = kv_width // head_size
    q_heads = queries.shape[1] // head_size
    group_size = q_heads // kv_heads
    scale = 1.0 / math.sqrt(head_size)
    pieces = (
        lax.all_gather(w_key, "dp", axis=0, tiled=True),
        lax.all_gather(w_value, "dp", axis=0, tiled=True),
    )
    key_sums = jnp.dot(normed, pieces[0], preferred_element_type=jnp.float32)
    value_sums = jnp.dot(normed, pieces[1], preferred_element_type=jnp.float32)
    total_new = token_request.shape[0]
    requests = cache_lens.shape[0]
    request_ids = jnp.arange(requests, dtype=jnp.int32)
    member = (token_request[:, None] == request_ids[None, :]).astype(jnp.int32)
    counts = jnp.sum(member, axis=0)
    starts = jnp.cumsum(counts) - counts
    token_index = jnp.arange(total_new, dtype=jnp.int32)
    token_pos = jnp.sum(member * (cache_lens - starts)[None, :], axis=1) + token_index
    dp_index = lax.axis_index("dp")
    dp_count = lax.axis_size("dp")
    first_token = dp_index * tok_rows
    my_request = lax.dynamic_slice_in_dim(token_request, first_token, tok_rows)
    my_pos = lax.dynamic_slice_in_dim(token_pos, first_token, tok_rows)
    key_heads = rotate(key_sums.reshape(tok_rows, kv_heads, head_size), my_pos, head_size)
    new_keys = key_heads.reshape(tok_rows, kv_width).astype(jnp.bfloat16)
    new_values = value_sums.astype(jnp.bfloat16)
    pages_dev = key_pool.shape[0]
    page_rows = key_pool.shape[1]
    max_pages = page_table.shape[1]
    slot_all = jnp.take(page_table.reshape(-1), token_request * max_pages + token_pos // page_rows)
    local_slot = slot_all - dp_index * pages_dev
    owned = (local_slot >= 0) & (local_slot < pages_dev)
    dest_all = jnp.where(
        owned, local_slot * page_rows + token_pos % page_rows, pages_dev * page_rows
    )
    long_pages = (CTX_DEV * dp_count + PAGE - 1) // PAGE
    old_dev = (long_pages + 2 * ((SHORT + PAGE - 1) // PAGE) + dp_count - 1) // dp_count
    old_total = old_dev * dp_count
    old_ids = jnp.arange(old_total, dtype=jnp.int32)
    old_phys = old_ids // old_dev * pages_dev + old_ids % old_dev
    matches = (page_table[None, :, :] == old_phys[:, None, None]).astype(jnp.int32)
    page_has = jnp.sum(matches, axis=(1, 2)) > 0
    page_request = jnp.sum(matches * request_ids[None, :, None], axis=(1, 2))
    page_logical = jnp.sum(
        matches * jnp.arange(max_pages, dtype=jnp.int32)[None, None, :], axis=(1, 2)
    )
    page_limit = jnp.sum(matches * cache_lens[None, :, None], axis=(1, 2))
    q_local = queries.reshape(tok_rows, kv_heads, group_size, head_size)

    def attend(att_state, keys_flat, values_flat, key_info):
        key_request, key_pos, key_ok = key_info
        visible = (
            key_ok[None, :]
            & (key_request[None, :] == my_request[:, None])
            & (key_pos[None, :] <= my_pos[:, None])
        )
        keys_shaped = keys_flat.reshape(keys_flat.shape[0], kv_heads, head_size)
        values_shaped = values_flat.reshape(values_flat.shape[0], kv_heads, head_size)
        running_max, running_sum, running_acc = att_state
        scores = (
            jnp.einsum("thgd,khd->thgk", q_local, keys_shaped, preferred_element_type=jnp.float32)
            * scale
        )
        mask_full = visible[:, None, None, :]
        masked = jnp.where(mask_full, scores, NEG_FILL)
        new_max = jnp.maximum(running_max, jnp.max(masked, axis=-1))
        factor = jnp.exp(running_max - new_max)
        soft_weights = jnp.where(mask_full, jnp.exp(masked - new_max[..., None]), 0.0)
        new_sum = running_sum * factor + jnp.sum(soft_weights, axis=-1)
        new_acc = running_acc * factor[..., None] + jnp.einsum(
            "thgk,khd->thgd",
            soft_weights.astype(jnp.bfloat16),
            values_shaped,
            preferred_element_type=jnp.float32,
        )
        return (new_max, new_sum, new_acc)

    def attend_rows(att_state, keys_flat, values_flat, key_info):
        row_count = keys_flat.shape[0]
        key_block = 2048
        if row_count > key_block and row_count % key_block == 0:
            blocks = row_count // key_block
            stacked = (
                keys_flat.reshape(blocks, key_block, kv_width),
                values_flat.reshape(blocks, key_block, kv_width),
                key_info[0].reshape(blocks, key_block),
                key_info[1].reshape(blocks, key_block),
                key_info[2].reshape(blocks, key_block),
            )

            def step_block(inner_state, slab_parts):
                return (
                    attend(
                        inner_state,
                        slab_parts[0],
                        slab_parts[1],
                        (slab_parts[2], slab_parts[3], slab_parts[4]),
                    ),
                    None,
                )

            att_state, unused = lax.scan(step_block, att_state, stacked)
            return att_state
        return attend(att_state, keys_flat, values_flat, key_info)

    start_state = (
        jnp.full((tok_rows, kv_heads, group_size), NEG_FILL, jnp.float32),
        jnp.zeros((tok_rows, kv_heads, group_size), jnp.float32),
        jnp.zeros((tok_rows, kv_heads, group_size, head_size), jnp.float32),
    )
    flat_keys = key_pool.reshape(pages_dev * page_rows, kv_width)
    flat_values = value_pool.reshape(pages_dev * page_rows, kv_width)
    old_keys = key_pool[:old_dev]
    old_values = value_pool[:old_dev]
    pieces = (
        lax.all_gather(old_keys, "dp", axis=0, tiled=True),
        lax.all_gather(old_values, "dp", axis=0, tiled=True),
    )
    page_count = pieces[0].shape[0]
    cached_keys = pieces[0].reshape(page_count * page_rows, kv_width)
    cached_values = pieces[1].reshape(page_count * page_rows, kv_width)
    row_ids = jnp.arange(page_rows, dtype=jnp.int32)[None, :]
    key_pos = page_logical[:, None] * page_rows + row_ids
    key_ok = page_has[:, None] & (key_pos < page_limit[:, None])
    key_request = jnp.broadcast_to(page_request[:, None], (page_count, page_rows))
    middle_state = attend_rows(
        start_state,
        cached_keys,
        cached_values,
        (key_request.reshape(-1), key_pos.reshape(-1), key_ok.reshape(-1)),
    )
    pieces = (
        lax.all_gather(new_keys, "dp", axis=0, tiled=True),
        lax.all_gather(new_values, "dp", axis=0, tiled=True),
    )
    att_state = middle_state
    pool_keys = flat_keys
    pool_values = flat_values
    key_request = token_request
    key_pos = token_pos
    att_state = attend_rows(
        att_state,
        pieces[0],
        pieces[1],
        (key_request, key_pos, jnp.ones((pieces[0].shape[0],), jnp.bool_)),
    )
    pool_keys, pool_values = (
        pool_keys.at[dest_all].set(pieces[0], mode="drop"),
        pool_values.at[dest_all].set(pieces[1], mode="drop"),
    )
    final_state, pool_keys, pool_values = (att_state, pool_keys, pool_values)
    final_max, final_sum, final_acc = final_state
    attended = (
        (final_acc / final_sum[..., None])
        .reshape(tok_rows, q_heads * head_size)
        .astype(jnp.bfloat16)
    )
    return (attended, pool_keys.reshape(key_pool.shape), pool_values.reshape(value_pool.shape))


def ring_chip(pos, chips):
    pos = pos % chips
    return jnp.where(pos < chips // 2, 2 * pos, 2 * chips - 1 - 2 * pos)


def ring_place(chip, chips):
    return jnp.where(chip % 2 == 0, chip // 2, (2 * chips - 1 - chip) // 2)


def ring_pairs(chips, step, swap):
    order = [2 * k if k < chips // 2 else 2 * chips - 1 - 2 * k for k in range(chips)]
    return [
        (2 * order[k] + core, 2 * order[(k + step) % chips] + (core ^ swap))
        for k in range(chips)
        for core in range(2)
    ]


def ring_offsets(chips):
    return [0] + [o for d in range(1, chips // 2) for o in (d, -d)] + [chips // 2]


def request_starts(tr_ref, requests):
    tr = tr_ref[...]
    starts = [jnp.int32(0)]
    for r in range(1, requests):
        starts.append(jnp.sum(jnp.where(tr < r, 1.0, 0.0)).astype(jnp.int32))
    starts.append(jnp.int32(tr.shape[0] * tr.shape[1]))
    return starts


def pick(cond_starts, values, tokens):
    out = jnp.zeros_like(tokens) + values[0]
    for r in range(1, len(values)):
        out = jnp.where(tokens >= cond_starts[r], values[r], out)
    return out


def chip_requests(chip, toks, starts):
    first, last = jnp.int32(0), jnp.int32(0)
    for start in starts[1:-1]:
        first = first + (chip * toks >= start).astype(jnp.int32)
        last = last + (chip * toks + toks - 1 >= start).astype(jnp.int32)
    return first, last


def split_kernel(old, f_ref, q_ref, kp_ref, vp_ref, xc_ref, xo_ref, kvc_ref, out_ref, sems):
    core = lax.axis_index("dp") % 2
    copies = []

    def copy(source, target):
        copies.append(pltpu.make_async_copy(source, target, sems.at[len(copies)]))
        copies[-1].start()

    rows = f_ref.shape[0]
    half = q_ref.shape[1] // 2
    mine = pl.ds(pl.multiple_of(core * HD, HD), HD)
    other = pl.ds(pl.multiple_of((1 - core) * HD, HD), HD)
    for out, own in ((xo_ref, 1 - core), (xc_ref, core)):
        for m in range(f_ref.shape[1] // 512):
            at = pl.ds(pl.multiple_of((2 * m + own) * 256, 256), 256)
            copy(f_ref.at[:, at], out.at[:, pl.ds(m * 256, 256)])
    at = 0
    for n, ref in enumerate((kp_ref, vp_ref)):
        copy(ref.at[pl.ds(0, old), :, mine], kvc_ref.at[pl.ds(n * old, old)])
        for p in range(old):
            copy(ref.at[p, :, other], out_ref.at[pl.ds(at, PAGE), :])
            at += PAGE
    for h in range(half // HD):
        lane = pl.multiple_of((1 - core) * half + h * HD, HD)
        copy(q_ref.at[:, pl.ds(lane, HD)], out_ref.at[pl.ds(at, rows), :])
        at += rows
    for c in copies:
        c.wait()


def merge_kernel(q_ref, got_ref, qs_ref, kv_ref):
    core = lax.axis_index("dp") % 2
    count = kv_ref.shape[0]
    rows, group = q_ref.shape[0], q_ref.shape[1] // (2 * HD)
    for n in range(count):
        kv_ref[n] = got_ref[n * PAGE : (n + 1) * PAGE, :]
    for h in range(group):
        mine = pl.ds(pl.multiple_of((2 * h + core) * rows, rows), rows)
        other = pl.ds(pl.multiple_of((2 * h + 1 - core) * rows, rows), rows)
        qs_ref[mine, :] = q_ref[:, pl.ds(pl.multiple_of((core * group + h) * HD, HD), HD)]
        first = count * PAGE + h * rows
        qs_ref[other, :] = got_ref[first : first + rows, :]


def scale_kernel(
    chips, lens_ref, tr_ref, inv_ref, gain_ref, a_ref, b_ref, c_ref, d_ref, xs_ref, ss_ref, cos_ref, sin_ref
):
    dp = lax.axis_index("dp")
    mp = lax.axis_index("mp")
    chip, core = dp // 2, dp % 2
    rows = a_ref.shape[0]
    per_half = a_ref.shape[1] // 256
    for first, second, owner in ((a_ref, b_ref, core), (c_ref, d_ref, 1 - core)):
        at = pl.ds(pl.multiple_of(owner * rows, rows), rows)
        total = jnp.zeros((rows, 256), jnp.float32)
        for ref, half in ((first, mp), (second, 1 - mp)):
            for m in range(per_half):
                wide = ref[:, m * 256 : (m + 1) * 256].astype(jnp.float32)
                block = half * (2 * per_half) + 2 * m + core
                gain = gain_ref[:, pl.ds(pl.multiple_of(block * 256, 256), 256)].astype(jnp.float32)
                total = total + wide * wide
                xs_ref[half * per_half + m, at, :] = (wide * gain).astype(jnp.bfloat16)
        ss_ref[at, :] = jnp.broadcast_to(jnp.sum(total, axis=1, keepdims=True), (rows, 128))
    requests = lens_ref.shape[0]
    starts = request_starts(tr_ref, requests)
    tokens = chip * (2 * rows) + lax.broadcasted_iota(jnp.int32, (2 * rows, 128), 0)
    shift = pick(starts, [lens_ref[r] - starts[r] for r in range(requests)], tokens)
    angles = (tokens + shift).astype(jnp.float32) * inv_ref[...]
    lane = lax.broadcasted_iota(jnp.int32, (2 * rows, 128), 1)
    sine = jnp.sin(angles)
    cos_ref[...] = jnp.cos(angles)
    sin_ref[...] = jnp.where(lane < HD // 2, -sine, sine)


def project_kernel(chips, xs_ref, ss_ref, *refs):
    keys, values = refs[:chips], refs[chips : 2 * chips]
    send_ref, keep_ref, acc_ref = refs[2 * chips :]
    dp = lax.axis_index("dp")
    chip, core = dp // 2, dp % 2
    place = ring_place(chip, chips)
    ksum = jnp.zeros((xs_ref.shape[1], 2 * HD), jnp.float32)
    vsum = jnp.zeros((xs_ref.shape[1], 2 * HD), jnp.float32)
    for n, offset in enumerate(ring_offsets(chips)):
        x = xs_ref[ring_chip(place + offset + chips, chips)]
        ksum = ksum + jnp.dot(x, keys[n][...], preferred_element_type=jnp.float32)
        vsum = vsum + jnp.dot(x, values[n][...], preferred_element_type=jnp.float32)
    acc_ref[:, : 2 * HD] = ksum
    acc_ref[:, 2 * HD :] = vsum
    for ref, head in ((send_ref, 1 - core), (keep_ref, core)):
        ref[:, :HD] = acc_ref[:, pl.ds(pl.multiple_of(head * HD, HD), HD)]
        ref[:, HD : 2 * HD] = acc_ref[:, pl.ds(pl.multiple_of((2 + head) * HD, HD), HD)]
        ref[:, 2 * HD :] = ss_ref[...]


def rotate_kernel(width, keep_ref, got_ref, cos_ref, sin_ref, out_ref):
    total = keep_ref[...] + got_ref[...]
    inverse = lax.rsqrt(total[:, 2 * HD :] * (1.0 / width) + 1e-05)
    key = total[:, :HD] * inverse
    rolled = pltpu.roll(key, HD // 2, 1)
    out_ref[:, :HD] = (key * cos_ref[...] + rolled * sin_ref[...]).astype(jnp.bfloat16)
    out_ref[:, HD:] = (total[:, HD : 2 * HD] * inverse).astype(jnp.bfloat16)


def attend_block(qs_ref, keys, values, first, low, high, m_ref, l_ref, acc_ref):
    scores = lax.dot_general(keys, qs_ref[...], (((1,), (1,)), ((), ())), preferred_element_type=jnp.float32)
    ids = first + lax.broadcasted_iota(jnp.int32, scores.shape, 0)
    scores = jnp.where((ids >= low) & (ids < high), scores * (LOG2E / math.sqrt(HD)), NEG_FILL)
    before = m_ref[...]
    top = jnp.maximum(before, jnp.max(scores, axis=0, keepdims=True))
    shrink = jnp.exp2(before - top)
    weights = jnp.exp2(scores - top)
    m_ref[...] = top
    l_ref[...] = l_ref[...] * shrink + jnp.sum(weights, axis=0, keepdims=True)
    acc_ref[...] = acc_ref[...] * shrink + lax.dot_general(
        values,
        weights.astype(jnp.bfloat16),
        (((0,), (0,)), ((), ())),
        preferred_element_type=jnp.float32,
    )


def three_parts(x):
    first = x.astype(jnp.bfloat16).astype(jnp.float32)
    second = (x - first).astype(jnp.bfloat16).astype(jnp.float32)
    return jnp.concatenate([first, second, x - first - second], axis=0)


def cached_kernel(chips, pages_dev, old, away, lens_ref, table_ref, tr_ref, qs_ref, *refs):
    members = chips // 2
    near, far = refs[:members], refs[members : 2 * members]
    outs, (kbuf, vbuf, m_ref, l_ref, acc_ref, slot_of) = refs[2 * members : -6], refs[-6:]
    dp = lax.axis_index("dp")
    chip, core = dp // 2, dp % 2
    who = chip ^ away
    requests = lens_ref.shape[0]
    width = qs_ref.shape[0]
    toks = tr_ref.shape[0] * tr_ref.shape[1] // chips
    starts = request_starts(tr_ref, requests)
    first_req, last_req = chip_requests(who, toks, starts)

    def clear(i, carry):
        slot_of[i] = -1
        return carry

    lax.fori_loop(0, slot_of.shape[0], clear, 0)
    base = jnp.int32(0)
    lows, highs = [], []
    for r in range(requests):
        length = lens_ref[r]
        relevant = (r >= first_req) & (r <= last_req)
        count = jnp.where(relevant, (length + PAGE - 1) // PAGE, 0)

        def place(l, at, r=r):
            page = table_ref[r, l]
            held = page // (2 * pages_dev * members) == chip // members

            @pl.when(held)
            def _():
                slot_of[page] = at

            return at + held.astype(jnp.int32)

        end = lax.fori_loop(0, count, place, base)
        last_page = table_ref[r, (length + PAGE - 1) // PAGE - 1]
        cut = jnp.where(
            (end > base) & (last_page // (2 * pages_dev * members) == chip // members),
            (length + PAGE - 1) // PAGE * PAGE - length,
            0,
        )
        lows.append(base * PAGE)
        highs.append(end * PAGE - cut)
        base = end

    for e in range(members):
        source = chip ^ e
        for block, owner in ((near[e], 2 * source + core), (far[e], 2 * source + 1 - core)):
            for s in range(old):
                slot = slot_of[owner * pages_dev + s]

                @pl.when(slot >= 0)
                def _(block=block, s=s, slot=slot):
                    at = pl.ds(pl.multiple_of(slot * PAGE, PAGE), PAGE)
                    kbuf[at, :] = block[s]
                    vbuf[at, :] = block[old + s]

    step_pages = STEP_PAGES
    pad = pl.ds(pl.multiple_of(base * PAGE, PAGE), (step_pages - 1) * PAGE)
    kbuf[pad, :] = jnp.zeros(((step_pages - 1) * PAGE, HD), kbuf.dtype)
    vbuf[pad, :] = jnp.zeros(((step_pages - 1) * PAGE, HD), vbuf.dtype)
    tokens = who * toks + lax.broadcasted_iota(jnp.int32, (1, width), 1) % toks
    low = pick(starts, lows, tokens)
    high = pick(starts, highs, tokens)
    m_ref[...] = jnp.full(m_ref.shape, NEG_START, jnp.float32)
    l_ref[...] = jnp.zeros(l_ref.shape, jnp.float32)
    acc_ref[...] = jnp.zeros(acc_ref.shape, jnp.float32)

    def step(i, carry):
        size = step_pages * PAGE
        at = pl.ds(pl.multiple_of(i * size, size), size)
        attend_block(qs_ref, kbuf[at, :], vbuf[at, :], i * size, low, high, m_ref, l_ref, acc_ref)
        return carry

    lax.fori_loop(0, (base + step_pages - 1) // step_pages, step, 0)
    if away:
        outs[0][:HD, :] = acc_ref[...].astype(jnp.bfloat16)
        outs[0][HD:, :] = jnp.concatenate(
            [three_parts(m_ref[...]), three_parts(l_ref[...]), jnp.zeros((10, width), jnp.float32)], axis=0
        ).astype(jnp.bfloat16)
    else:
        outs[0][...], outs[1][...], outs[2][...] = m_ref[...], l_ref[...], acc_ref[...]


def fresh_kernel(
    chips, pages_dev, lens_ref, table_ref, tr_ref, qs_ref, m0_ref, l0_ref, acc0_ref, back_ref, *refs
):
    fresh = refs[:chips]
    atto_ref, attc_ref, no_ref, nc_ref, info_ref = refs[chips : chips + 5]
    nbuf, m_ref, l_ref, acc_ref, out_ref, new_at, new_lo, new_hi = refs[chips + 5 :]
    dp = lax.axis_index("dp")
    chip, core = dp // 2, dp % 2
    place = ring_place(chip, chips)
    toks = fresh[0].shape[0]
    rows = toks // 2
    requests = lens_ref.shape[0]
    width = qs_ref.shape[0]
    group = width // toks
    starts = request_starts(tr_ref, requests)
    reqs = chip_requests(chip, toks, starts)
    first_req = reqs[0]
    parts = back_ref[HD : HD + 6, :].astype(jnp.float32)
    m0, m1 = m0_ref[...], parts[0:1] + parts[1:2] + parts[2:3]
    top = jnp.maximum(m0, m1)
    f0, f1 = jnp.exp2(m0 - top), jnp.exp2(m1 - top)
    m_ref[...] = top
    l_ref[...] = l0_ref[...] * f0 + (parts[3:4] + parts[4:5] + parts[5:6]) * f1
    acc_ref[...] = acc0_ref[...] * f0 + back_ref[:HD, :].astype(jnp.float32) * f1

    def clear(i, carry):
        new_lo[i] = 0
        new_hi[i] = 0
        return carry

    lax.fori_loop(0, new_lo.shape[0], clear, 0)
    for r in range(requests):
        length = lens_ref[r]

        def place_new(l, carry, r=r, length=length):
            at = l * PAGE - length + starts[r]
            page = table_ref[r, l]
            new_at[page] = at
            new_lo[page] = jnp.maximum(starts[r] - at, 0)
            new_hi[page] = jnp.minimum(starts[r + 1] - at, PAGE)
            return carry

        end = (length + starts[r + 1] - starts[r] + PAGE - 1) // PAGE
        lax.fori_loop(length // PAGE, end, place_new, 0)

    for n, offset in enumerate(ring_offsets(chips)):
        source = ring_chip(place + offset + chips, chips)
        nbuf[pl.ds(pl.multiple_of((source + 1) * toks, toks), toks), :] = fresh[n][...]
    nbuf[:toks, :] = jnp.zeros((toks, 2 * HD), nbuf.dtype)
    nbuf[(chips + 1) * toks :, :] = jnp.zeros((toks, 2 * HD), nbuf.dtype)

    tokens = chip * toks + lax.broadcasted_iota(jnp.int32, (1, width), 1) % toks
    low = pick(starts, starts[:requests], tokens)
    first_start = starts[0]
    for r in range(1, requests):
        first_start = jnp.where(first_req == r, starts[r], first_start)

    def step(b, carry):
        at = pl.ds(pl.multiple_of((b + 1) * toks, toks), toks)
        attend_block(qs_ref, nbuf[at, :HD], nbuf[at, HD:], b * toks, low, tokens + 1, m_ref, l_ref, acc_ref)
        return carry

    lax.fori_loop(first_start // toks, chip + 1, step, 0)
    result = acc_ref[...] / l_ref[...]
    for h in range(group):
        out_ref[:, h * HD : (h + 1) * HD] = result[:, h * toks : (h + 1) * toks].T.astype(jnp.bfloat16)
    attc_ref[...] = out_ref[pl.ds(pl.multiple_of(core * rows, rows), rows), :]
    atto_ref[...] = out_ref[pl.ds(pl.multiple_of((1 - core) * rows, rows), rows), :]

    row = lax.broadcasted_iota(jnp.int32, (PAGE, 2 * toks), 0)
    column = lax.broadcasted_iota(jnp.int32, (PAGE, 2 * toks), 1)
    for ref, owner in ((no_ref, dp + 1 - 2 * core), (nc_ref, dp)):
        for s in range(pages_dev):
            page = owner * pages_dev + s
            at, low_row, high_row = new_at[page], new_lo[page], new_hi[page]

            @pl.when(high_row > low_row)
            def _(ref=ref, s=s, at=at, low_row=low_row, high_row=high_row):
                shifted = at + toks
                first = pl.multiple_of(shifted // toks * toks, toks)
                chosen = (column + first == row + shifted) & (row >= low_row) & (row < high_row)
                ref[s] = jnp.dot(
                    jnp.where(chosen, 1.0, 0.0).astype(jnp.bfloat16),
                    nbuf[pl.ds(first, 2 * toks), :],
                    preferred_element_type=jnp.float32,
                ).astype(jnp.bfloat16)

    for s in range(pages_dev):
        info_ref[2 * s] = new_lo[dp * pages_dev + s]
        info_ref[2 * s + 1] = new_hi[dp * pages_dev + s]


def join_kernel(info_ref, attc_ref, attr_ref, nc_ref, nr_ref, kp_ref, vp_ref, att_ref, ko_ref, vo_ref):
    core = lax.axis_index("dp") % 2
    half = attc_ref.shape[1]
    att_ref[:, pl.ds(pl.multiple_of(core * half, HD), half)] = attc_ref[...]
    att_ref[:, pl.ds(pl.multiple_of((1 - core) * half, HD), half)] = attr_ref[...]
    row = lax.broadcasted_iota(jnp.int32, (PAGE, HD), 0)
    for s in range(kp_ref.shape[0]):
        chosen = (row >= info_ref[2 * s]) & (row < info_ref[2 * s + 1])
        for ref, head in ((nc_ref, core), (nr_ref, 1 - core)):
            at = pl.ds(pl.multiple_of(head * HD, HD), HD)
            ko_ref[s, :, at] = jnp.where(chosen, ref[s, :, :HD], kp_ref[s, :, at])
            vo_ref[s, :, at] = jnp.where(chosen, ref[s, :, HD:], vp_ref[s, :, at])


def call(
    kernel, outs, scratch=(), ins=None, smem=(), far=(), out_smem=(), out_far=(), limit=VMEM_LIMIT, name=None
):
    vmem, sm = pl.BlockSpec(memory_space=pltpu.VMEM), pl.BlockSpec(memory_space=pltpu.SMEM)
    hbm = pl.BlockSpec(memory_space=pl.ANY)
    return pl.pallas_call(
        kernel,
        out_shape=[jax.ShapeDtypeStruct(s, d) for s, d in outs],
        in_specs=[sm if n in smem else hbm if n in far else vmem for n in range(ins)],
        out_specs=[sm if n in out_smem else hbm if n in out_far else vmem for n in range(len(outs))],
        scratch_shapes=list(scratch),
        compiler_params=pltpu.CompilerParams(vmem_limit_bytes=limit),
        name=name,
    )


def ring_send(chips, arrays, step, swap=0):
    return [lax.ppermute(a, "dp", ring_pairs(chips, step, swap * n)) for n, a in enumerate(arrays)]


def ring_body(
    dp_count,
    features,
    norm_gain,
    w_key,
    w_value,
    queries,
    key_pool,
    value_pool,
    cache_lens,
    page_table,
    token_request,
):
    bf, f32, i32 = jnp.bfloat16, jnp.float32, jnp.int32
    chips = dp_count // 2
    offsets = ring_offsets(chips)
    rows, half_width = features.shape
    width = norm_gain.shape[0]
    toks = 2 * rows
    pages_dev = key_pool.shape[0]
    long_pages = (CTX_DEV * dp_count + PAGE - 1) // PAGE
    old = (long_pages + 2 * ((SHORT + PAGE - 1) // PAGE) + dp_count - 1) // dp_count
    group = queries.shape[1] // (2 * HD)
    columns = group * toks
    core_pairs = [(i, i ^ 1) for i in range(dp_count)]
    mp_pairs = [(0, 1), (1, 0)]
    both_pairs = [(2 * i + j, 2 * (i ^ 1) + (1 - j)) for i in range(dp_count) for j in range(2)]
    requests_tile = token_request.reshape(-1, 128)

    def exchange(array, e, swap=0):
        return lax.ppermute(array, "dp", [(i, i ^ (2 * e) ^ swap) for i in range(dp_count)])

    w_got = {0: [w_key, w_value]}
    right, left = ring_send(chips, [w_key, w_value], 1), ring_send(chips, [w_key, w_value], -1)
    w_got[-1], w_got[1] = right, left
    bundle = 2 * old * PAGE + group * rows
    x_mine, x_other, kv_mine, core_send = call(
        functools.partial(split_kernel, old),
        [
            ((rows, half_width // 2), bf),
            ((rows, half_width // 2), bf),
            ((2 * old, PAGE, HD), bf),
            ((bundle, HD), bf),
        ],
        scratch=[pltpu.SemaphoreType.DMA((2 * (half_width // 512) + 2 + 2 * old + group,))],
        ins=4,
        far=(0, 1, 2, 3),
        limit=SPLIT_LIMIT,
        name="split",
    )(features, queries, key_pool, value_pool)
    core_send, _ = lax.optimization_barrier((core_send, w_got[-1]))
    core_got = lax.ppermute(core_send, "dp", core_pairs)
    x_b = lax.ppermute(x_mine, "mp", mp_pairs)
    x_c = lax.ppermute(x_other, "dp", core_pairs)
    x_d = lax.ppermute(x_other, ("dp", "mp"), both_pairs)
    q_rows, kv_other = call(
        merge_kernel,
        [((columns, HD), bf), ((2 * old, PAGE, HD), bf)],
        ins=2,
        name="merge",
    )(queries, core_got)
    for d in range(2, chips // 2):
        right, left = ring_send(chips, right, 1), ring_send(chips, left, -1)
        w_got[-d], w_got[d] = right, left
    inverse = (THETA ** (-(np.arange(HD) % (HD // 2)) * 2.0 / HD)).astype(np.float32)[None, :]
    scaled, squares, cosine, sine = call(
        functools.partial(scale_kernel, chips),
        [((chips, toks, 256), bf), ((toks, 128), f32), ((toks, HD), f32), ((toks, HD), f32)],
        ins=8,
        smem=(0,),
        name="scale",
    )(
        cache_lens,
        requests_tile,
        jnp.asarray(inverse),
        norm_gain.reshape(1, -1),
        x_mine,
        x_b,
        x_c,
        x_d,
    )
    w_got[chips // 2] = ring_send(chips, right[:1], 1) + ring_send(chips, left[1:], -1)
    scaled, q_rows, kv_other = lax.optimization_barrier((scaled, q_rows, kv_other))
    part_send, part_keep = call(
        functools.partial(project_kernel, chips),
        [((toks, 3 * HD), f32), ((toks, 3 * HD), f32)],
        scratch=[pltpu.VMEM((toks, 4 * HD), f32)],
        ins=2 + 2 * chips,
        name="project",
    )(scaled, squares, *[w_got[o][0] for o in offsets], *[w_got[o][1] for o in offsets])
    part_got = lax.ppermute(part_send, "dp", core_pairs)

    first_near, first_far, _ = lax.optimization_barrier((kv_mine, kv_other, part_send))
    z_near, z_far = exchange(first_near, 2), exchange(first_far, 2)
    y_near, y_far = exchange(first_near, 1), exchange(first_far, 1)
    (fresh,) = call(
        functools.partial(rotate_kernel, width),
        [((toks, 2 * HD), bf)],
        ins=4,
        name="rotary",
    )(part_keep, part_got, cosine, sine)
    new = {0: fresh}
    new[-1], new[1] = ring_send(chips, [fresh], 1)[0], ring_send(chips, [fresh], -1)[0]
    late_y, late_z, late_q, _ = lax.optimization_barrier((y_near, z_far, q_rows, (new[-1], new[1])))
    q_away = exchange(late_q, chips // 2)
    near = [kv_mine, y_near, z_near, exchange(late_y, 2)]
    far = [kv_other, y_far, z_far, exchange(late_z, 1)]
    slots = dp_count // 2 * old + STEP_PAGES
    table = pltpu.SMEM((dp_count * pages_dev,), i32)

    def cached(q, away, outs, name):
        return call(
            functools.partial(cached_kernel, chips, pages_dev, old, away),
            outs,
            scratch=[
                pltpu.VMEM((slots * PAGE, HD), bf),
                pltpu.VMEM((slots * PAGE, HD), bf),
                pltpu.VMEM((1, columns), f32),
                pltpu.VMEM((1, columns), f32),
                pltpu.VMEM((HD, columns), f32),
                table,
            ],
            ins=4 + chips,
            smem=(0, 1),
            name=name,
        )(cache_lens, page_table, requests_tile, q, *near, *far)

    (away,) = cached(q_away, chips // 2, [((HD + 16, columns), bf)], "attend_cached_away")
    here = cached(
        q_rows, 0, [((1, columns), f32), ((1, columns), f32), ((HD, columns), f32)], "attend_cached_here"
    )
    new[-2], new[2] = ring_send(chips, [new[-1]], 1)[0], ring_send(chips, [new[1]], -1)[0]
    right, left, away = lax.optimization_barrier((new[-2], new[2], away))
    new[-3], new[3] = ring_send(chips, [right], 1)[0], ring_send(chips, [left], -1)[0]
    right, here = lax.optimization_barrier((new[-3], here))
    (new[chips // 2],) = ring_send(chips, [right], 1)
    back = exchange(away, chips // 2)
    top, total, acc = here

    att_other, att_mine, rows_other, rows_mine, info = call(
        functools.partial(fresh_kernel, chips, pages_dev),
        [
            ((rows, group * HD), bf),
            ((rows, group * HD), bf),
            ((pages_dev, PAGE, 2 * HD), bf),
            ((pages_dev, PAGE, 2 * HD), bf),
            ((2 * pages_dev,), i32),
        ],
        scratch=[
            pltpu.VMEM(((chips + 2) * toks, 2 * HD), bf),
            pltpu.VMEM((1, columns), f32),
            pltpu.VMEM((1, columns), f32),
            pltpu.VMEM((HD, columns), f32),
            pltpu.VMEM((toks, group * HD), bf),
            table,
            table,
            table,
        ],
        ins=8 + chips,
        smem=(0, 1),
        out_smem=(4,),
        name="attend_new",
    )(
        cache_lens,
        page_table,
        requests_tile,
        q_rows,
        top,
        total,
        acc,
        back,
        *[new[o] for o in offsets],
    )
    rows_got = lax.ppermute(rows_other, "dp", core_pairs)
    att_got = lax.ppermute(att_other, "dp", core_pairs)
    attended, keys_out, values_out = call(
        join_kernel,
        [(queries.shape, bf), (key_pool.shape, bf), (value_pool.shape, bf)],
        ins=7,
        smem=(0,),
        name="join",
    )(info, att_mine, att_got, rows_mine, rows_got, key_pool, value_pool)
    return attended, keys_out, values_out


def solution(mesh):
    in_specs = (
        P("dp", "mp"),
        P(),
        P("dp", "mp"),
        P("dp", "mp"),
        P("dp", "mp"),
        P("dp", None, "mp"),
        P("dp", None, "mp"),
        P(),
        P(),
        P(),
    )
    out_specs = (P("dp", "mp"), P("dp", None, "mp"), P("dp", None, "mp"))
    dp_count, mp_count = mesh.shape["dp"], mesh.shape["mp"]

    def body(*args):
        even = mp_count == 2 and dp_count == 16
        if even and args[2].shape == (256, 2 * HD):
            return ring_body(dp_count, *args)
        return general_body(*args)

    return jax.shard_map(body, mesh=mesh, in_specs=in_specs, out_specs=out_specs, check_vma=False)
```

```python
import functools
import math

import jax
import jax.numpy as jnp
import numpy as np
from jax import lax
from jax.experimental import pallas as pl
from jax.experimental.pallas import tpu as pltpu
from jax.sharding import PartitionSpec as P

HD = 128
PAGE = 128
SHORT = 512
CTX_DEV = 120


THETA = 500000.0
NEG_FILL = -1e30
NEG_START = -1e29
LOG2E = 1.4426950408889634
VMEM_LIMIT = 32 * 1024 * 1024
SPLIT_LIMIT = 63 * 1024 * 1024
STEP_PAGES = 4


def rotate(values, positions, head_size):
    halfway = head_size // 2
    inverse = THETA ** (-(jnp.arange(halfway, dtype=jnp.float32) * 2.0) / head_size)
    angles = positions.astype(jnp.float32)[:, None] * inverse[None, :]
    cosine = jnp.cos(angles)[:, None, :]
    sine = jnp.sin(angles)[:, None, :]
    first_half = values[..., :halfway]
    second_half = values[..., halfway:]
    return jnp.concatenate(
        [first_half * cosine - second_half * sine, second_half * cosine + first_half * sine],
        axis=-1,
    )


def general_body(
    features,
    norm_gain,
    w_key,
    w_value,
    queries,
    key_pool,
    value_pool,
    cache_lens,
    page_table,
    token_request,
):
    gathered = lax.all_gather(features, "mp", axis=1, tiled=True)
    widened = gathered.astype(jnp.float32)
    mean_square = jnp.mean(widened * widened, axis=1, keepdims=True)
    normed = (widened * lax.rsqrt(mean_square + 1e-05) * norm_gain.astype(jnp.float32)).astype(
        jnp.bfloat16
    )
    tok_rows = features.shape[0]
    kv_width = w_key.shape[1]
    head_size = HD
    kv_heads = kv_width // head_size
    q_heads = queries.shape[1] // head_size
    group_size = q_heads // kv_heads
    scale = 1.0 / math.sqrt(head_size)
    pieces = (
        lax.all_gather(w_key, "dp", axis=0, tiled=True),
        lax.all_gather(w_value, "dp", axis=0, tiled=True),
    )
    key_sums = jnp.dot(normed, pieces[0], preferred_element_type=jnp.float32)
    value_sums = jnp.dot(normed, pieces[1], preferred_element_type=jnp.float32)
    total_new = token_request.shape[0]
    requests = cache_lens.shape[0]
    request_ids = jnp.arange(requests, dtype=jnp.int32)
    member = (token_request[:, None] == request_ids[None, :]).astype(jnp.int32)
    counts = jnp.sum(member, axis=0)
    starts = jnp.cumsum(counts) - counts
    token_index = jnp.arange(total_new, dtype=jnp.int32)
    token_pos = jnp.sum(member * (cache_lens - starts)[None, :], axis=1) + token_index
    dp_index = lax.axis_index("dp")
    dp_count = lax.axis_size("dp")
    first_token = dp_index * tok_rows
    my_request = lax.dynamic_slice_in_dim(token_request, first_token, tok_rows)
    my_pos = lax.dynamic_slice_in_dim(token_pos, first_token, tok_rows)
    key_heads = rotate(key_sums.reshape(tok_rows, kv_heads, head_size), my_pos, head_size)
    new_keys = key_heads.reshape(tok_rows, kv_width).astype(jnp.bfloat16)
    new_values = value_sums.astype(jnp.bfloat16)
    pages_dev = key_pool.shape[0]
    page_rows = key_pool.shape[1]
    max_pages = page_table.shape[1]
    slot_all = jnp.take(page_table.reshape(-1), token_request * max_pages + token_pos // page_rows)
    local_slot = slot_all - dp_index * pages_dev
    owned = (local_slot >= 0) & (local_slot < pages_dev)
    dest_all = jnp.where(
        owned, local_slot * page_rows + token_pos % page_rows, pages_dev * page_rows
    )
    long_pages = (CTX_DEV * dp_count + PAGE - 1) // PAGE
    old_dev = (long_pages + 2 * ((SHORT + PAGE - 1) // PAGE) + dp_count - 1) // dp_count
    old_total = old_dev * dp_count
    old_ids = jnp.arange(old_total, dtype=jnp.int32)
    old_phys = old_ids // old_dev * pages_dev + old_ids % old_dev
    matches = (page_table[None, :, :] == old_phys[:, None, None]).astype(jnp.int32)
    page_has = jnp.sum(matches, axis=(1, 2)) > 0
    page_request = jnp.sum(matches * request_ids[None, :, None], axis=(1, 2))
    page_logical = jnp.sum(
        matches * jnp.arange(max_pages, dtype=jnp.int32)[None, None, :], axis=(1, 2)
    )
    page_limit = jnp.sum(matches * cache_lens[None, :, None], axis=(1, 2))
    q_local = queries.reshape(tok_rows, kv_heads, group_size, head_size)

    def attend(att_state, keys_flat, values_flat, key_info):
        key_request, key_pos, key_ok = key_info
        visible = (
            key_ok[None, :]
            & (key_request[None, :] == my_request[:, None])
            & (key_pos[None, :] <= my_pos[:, None])
        )
        keys_shaped = keys_flat.reshape(keys_flat.shape[0], kv_heads, head_size)
        values_shaped = values_flat.reshape(values_flat.shape[0], kv_heads, head_size)
        running_max, running_sum, running_acc = att_state
        scores = (
            jnp.einsum("thgd,khd->thgk", q_local, keys_shaped, preferred_element_type=jnp.float32)
            * scale
        )
        mask_full = visible[:, None, None, :]
        masked = jnp.where(mask_full, scores, NEG_FILL)
        new_max = jnp.maximum(running_max, jnp.max(masked, axis=-1))
        factor = jnp.exp(running_max - new_max)
        soft_weights = jnp.where(mask_full, jnp.exp(masked - new_max[..., None]), 0.0)
        new_sum = running_sum * factor + jnp.sum(soft_weights, axis=-1)
        new_acc = running_acc * factor[..., None] + jnp.einsum(
            "thgk,khd->thgd",
            soft_weights.astype(jnp.bfloat16),
            values_shaped,
            preferred_element_type=jnp.float32,
        )
        return (new_max, new_sum, new_acc)

    def attend_rows(att_state, keys_flat, values_flat, key_info):
        row_count = keys_flat.shape[0]
        key_block = 2048
        if row_count > key_block and row_count % key_block == 0:
            blocks = row_count // key_block
            stacked = (
                keys_flat.reshape(blocks, key_block, kv_width),
                values_flat.reshape(blocks, key_block, kv_width),
                key_info[0].reshape(blocks, key_block),
                key_info[1].reshape(blocks, key_block),
                key_info[2].reshape(blocks, key_block),
            )

            def step_block(inner_state, slab_parts):
                return (
                    attend(
                        inner_state,
                        slab_parts[0],
                        slab_parts[1],
                        (slab_parts[2], slab_parts[3], slab_parts[4]),
                    ),
                    None,
                )

            att_state, unused = lax.scan(step_block, att_state, stacked)
            return att_state
        return attend(att_state, keys_flat, values_flat, key_info)

    start_state = (
        jnp.full((tok_rows, kv_heads, group_size), NEG_FILL, jnp.float32),
        jnp.zeros((tok_rows, kv_heads, group_size), jnp.float32),
        jnp.zeros((tok_rows, kv_heads, group_size, head_size), jnp.float32),
    )
    flat_keys = key_pool.reshape(pages_dev * page_rows, kv_width)
    flat_values = value_pool.reshape(pages_dev * page_rows, kv_width)
    old_keys = key_pool[:old_dev]
    old_values = value_pool[:old_dev]
    pieces = (
        lax.all_gather(old_keys, "dp", axis=0, tiled=True),
        lax.all_gather(old_values, "dp", axis=0, tiled=True),
    )
    page_count = pieces[0].shape[0]
    cached_keys = pieces[0].reshape(page_count * page_rows, kv_width)
    cached_values = pieces[1].reshape(page_count * page_rows, kv_width)
    row_ids = jnp.arange(page_rows, dtype=jnp.int32)[None, :]
    key_pos = page_logical[:, None] * page_rows + row_ids
    key_ok = page_has[:, None] & (key_pos < page_limit[:, None])
    key_request = jnp.broadcast_to(page_request[:, None], (page_count, page_rows))
    middle_state = attend_rows(
        start_state,
        cached_keys,
        cached_values,
        (key_request.reshape(-1), key_pos.reshape(-1), key_ok.reshape(-1)),
    )
    pieces = (
        lax.all_gather(new_keys, "dp", axis=0, tiled=True),
        lax.all_gather(new_values, "dp", axis=0, tiled=True),
    )
    att_state = middle_state
    pool_keys = flat_keys
    pool_values = flat_values
    key_request = token_request
    key_pos = token_pos
    att_state = attend_rows(
        att_state,
        pieces[0],
        pieces[1],
        (key_request, key_pos, jnp.ones((pieces[0].shape[0],), jnp.bool_)),
    )
    pool_keys, pool_values = (
        pool_keys.at[dest_all].set(pieces[0], mode="drop"),
        pool_values.at[dest_all].set(pieces[1], mode="drop"),
    )
    final_state, pool_keys, pool_values = (att_state, pool_keys, pool_values)
    final_max, final_sum, final_acc = final_state
    attended = (
        (final_acc / final_sum[..., None])
        .reshape(tok_rows, q_heads * head_size)
        .astype(jnp.bfloat16)
    )
    return (attended, pool_keys.reshape(key_pool.shape), pool_values.reshape(value_pool.shape))


def ring_chip(pos, chips):
    pos = pos % chips
    return jnp.where(pos < chips // 2, 2 * pos, 2 * chips - 1 - 2 * pos)


def ring_place(chip, chips):
    return jnp.where(chip % 2 == 0, chip // 2, (2 * chips - 1 - chip) // 2)


def ring_pairs(chips, step, swap):
    order = [2 * k if k < chips // 2 else 2 * chips - 1 - 2 * k for k in range(chips)]
    return [
        (2 * order[k] + core, 2 * order[(k + step) % chips] + (core ^ swap))
        for k in range(chips)
        for core in range(2)
    ]


def ring_offsets(chips):
    return [0] + [o for d in range(1, chips // 2) for o in (d, -d)] + [chips // 2]


def request_starts(tr_ref, requests):
    tr = tr_ref[...]
    starts = [jnp.int32(0)]
    for r in range(1, requests):
        starts.append(jnp.sum(jnp.where(tr < r, 1.0, 0.0)).astype(jnp.int32))
    starts.append(jnp.int32(tr.shape[0] * tr.shape[1]))
    return starts


def pick(cond_starts, values, tokens):
    out = jnp.zeros_like(tokens) + values[0]
    for r in range(1, len(values)):
        out = jnp.where(tokens >= cond_starts[r], values[r], out)
    return out


def chip_requests(chip, toks, starts):
    first, last = jnp.int32(0), jnp.int32(0)
    for start in starts[1:-1]:
        first = first + (chip * toks >= start).astype(jnp.int32)
        last = last + (chip * toks + toks - 1 >= start).astype(jnp.int32)
    return first, last


def split_kernel(old, f_ref, q_ref, kp_ref, vp_ref, xc_ref, xo_ref, kvc_ref, out_ref, sems):
    core = lax.axis_index("dp") % 2
    copies = []

    def copy(source, target):
        copies.append(pltpu.make_async_copy(source, target, sems.at[len(copies)]))
        copies[-1].start()

    rows = f_ref.shape[0]
    half = q_ref.shape[1] // 2
    mine = pl.ds(pl.multiple_of(core * HD, HD), HD)
    other = pl.ds(pl.multiple_of((1 - core) * HD, HD), HD)
    for out, own in ((xo_ref, 1 - core), (xc_ref, core)):
        for m in range(f_ref.shape[1] // 512):
            at = pl.ds(pl.multiple_of((2 * m + own) * 256, 256), 256)
            copy(f_ref.at[:, at], out.at[:, pl.ds(m * 256, 256)])
    at = 0
    for n, ref in enumerate((kp_ref, vp_ref)):
        copy(ref.at[pl.ds(0, old), :, mine], kvc_ref.at[pl.ds(n * old, old)])
        for p in range(old):
            copy(ref.at[p, :, other], out_ref.at[pl.ds(at, PAGE), :])
            at += PAGE
    for h in range(half // HD):
        lane = pl.multiple_of((1 - core) * half + h * HD, HD)
        copy(q_ref.at[:, pl.ds(lane, HD)], out_ref.at[pl.ds(at, rows), :])
        at += rows
    for c in copies:
        c.wait()


def merge_kernel(q_ref, got_ref, qs_ref, kv_ref):
    core = lax.axis_index("dp") % 2
    count = kv_ref.shape[0]
    rows, group = q_ref.shape[0], q_ref.shape[1] // (2 * HD)
    for n in range(count):
        kv_ref[n] = got_ref[n * PAGE : (n + 1) * PAGE, :]
    for h in range(group):
        mine = pl.ds(pl.multiple_of((2 * h + core) * rows, rows), rows)
        other = pl.ds(pl.multiple_of((2 * h + 1 - core) * rows, rows), rows)
        qs_ref[mine, :] = q_ref[:, pl.ds(pl.multiple_of((core * group + h) * HD, HD), HD)]
        first = count * PAGE + h * rows
        qs_ref[other, :] = got_ref[first : first + rows, :]


def scale_kernel(
    chips, lens_ref, tr_ref, inv_ref, gain_ref, a_ref, b_ref, c_ref, d_ref, xs_ref, ss_ref, cos_ref, sin_ref
):
    dp = lax.axis_index("dp")
    mp = lax.axis_index("mp")
    chip, core = dp // 2, dp % 2
    rows = a_ref.shape[0]
    per_half = a_ref.shape[1] // 256
    for first, second, owner in ((a_ref, b_ref, core), (c_ref, d_ref, 1 - core)):
        at = pl.ds(pl.multiple_of(owner * rows, rows), rows)
        total = jnp.zeros((rows, 256), jnp.float32)
        for ref, half in ((first, mp), (second, 1 - mp)):
            for m in range(per_half):
                wide = ref[:, m * 256 : (m + 1) * 256].astype(jnp.float32)
                block = half * (2 * per_half) + 2 * m + core
                gain = gain_ref[:, pl.ds(pl.multiple_of(block * 256, 256), 256)].astype(jnp.float32)
                total = total + wide * wide
                xs_ref[half * per_half + m, at, :] = (wide * gain).astype(jnp.bfloat16)
        ss_ref[at, :] = jnp.broadcast_to(jnp.sum(total, axis=1, keepdims=True), (rows, 128))
    requests = lens_ref.shape[0]
    starts = request_starts(tr_ref, requests)
    tokens = chip * (2 * rows) + lax.broadcasted_iota(jnp.int32, (2 * rows, 128), 0)
    shift = pick(starts, [lens_ref[r] - starts[r] for r in range(requests)], tokens)
    angles = (tokens + shift).astype(jnp.float32) * inv_ref[...]
    lane = lax.broadcasted_iota(jnp.int32, (2 * rows, 128), 1)
    sine = jnp.sin(angles)
    cos_ref[...] = jnp.cos(angles)
    sin_ref[...] = jnp.where(lane < HD // 2, -sine, sine)


def project_kernel(chips, xs_ref, ss_ref, *refs):
    keys, values = refs[:chips], refs[chips : 2 * chips]
    send_ref, keep_ref, acc_ref = refs[2 * chips :]
    dp = lax.axis_index("dp")
    chip, core = dp // 2, dp % 2
    place = ring_place(chip, chips)
    ksum = jnp.zeros((xs_ref.shape[1], 2 * HD), jnp.float32)
    vsum = jnp.zeros((xs_ref.shape[1], 2 * HD), jnp.float32)
    for n, offset in enumerate(ring_offsets(chips)):
        x = xs_ref[ring_chip(place + offset + chips, chips)]
        ksum = ksum + jnp.dot(x, keys[n][...], preferred_element_type=jnp.float32)
        vsum = vsum + jnp.dot(x, values[n][...], preferred_element_type=jnp.float32)
    acc_ref[:, : 2 * HD] = ksum
    acc_ref[:, 2 * HD :] = vsum
    for ref, head in ((send_ref, 1 - core), (keep_ref, core)):
        ref[:, :HD] = acc_ref[:, pl.ds(pl.multiple_of(head * HD, HD), HD)]
        ref[:, HD : 2 * HD] = acc_ref[:, pl.ds(pl.multiple_of((2 + head) * HD, HD), HD)]
        ref[:, 2 * HD :] = ss_ref[...]


def rotate_kernel(width, keep_ref, got_ref, cos_ref, sin_ref, out_ref):
    total = keep_ref[...] + got_ref[...]
    inverse = lax.rsqrt(total[:, 2 * HD :] * (1.0 / width) + 1e-05)
    key = total[:, :HD] * inverse
    rolled = pltpu.roll(key, HD // 2, 1)
    out_ref[:, :HD] = (key * cos_ref[...] + rolled * sin_ref[...]).astype(jnp.bfloat16)
    out_ref[:, HD:] = (total[:, HD : 2 * HD] * inverse).astype(jnp.bfloat16)


def attend_block(qs_ref, keys, values, first, low, high, m_ref, l_ref, acc_ref):
    scores = lax.dot_general(keys, qs_ref[...], (((1,), (1,)), ((), ())), preferred_element_type=jnp.float32)
    ids = first + lax.broadcasted_iota(jnp.int32, scores.shape, 0)
    scores = jnp.where((ids >= low) & (ids < high), scores * (LOG2E / math.sqrt(HD)), NEG_FILL)
    before = m_ref[...]
    top = jnp.maximum(before, jnp.max(scores, axis=0, keepdims=True))
    shrink = jnp.exp2(before - top)
    weights = jnp.exp2(scores - top)
    m_ref[...] = top
    l_ref[...] = l_ref[...] * shrink + jnp.sum(weights, axis=0, keepdims=True)
    acc_ref[...] = acc_ref[...] * shrink + lax.dot_general(
        values,
        weights.astype(jnp.bfloat16),
        (((0,), (0,)), ((), ())),
        preferred_element_type=jnp.float32,
    )


def three_parts(x):
    first = x.astype(jnp.bfloat16).astype(jnp.float32)
    second = (x - first).astype(jnp.bfloat16).astype(jnp.float32)
    return jnp.concatenate([first, second, x - first - second], axis=0)


def cached_kernel(chips, pages_dev, old, away, lens_ref, table_ref, tr_ref, qs_ref, *refs):
    members = chips // 2
    near, far = refs[:members], refs[members : 2 * members]
    outs, (kbuf, vbuf, m_ref, l_ref, acc_ref, slot_of) = refs[2 * members : -6], refs[-6:]
    dp = lax.axis_index("dp")
    chip, core = dp // 2, dp % 2
    who = chip ^ away
    requests = lens_ref.shape[0]
    width = qs_ref.shape[0]
    toks = tr_ref.shape[0] * tr_ref.shape[1] // chips
    starts = request_starts(tr_ref, requests)
    first_req, last_req = chip_requests(who, toks, starts)

    def clear(i, carry):
        slot_of[i] = -1
        return carry

    lax.fori_loop(0, slot_of.shape[0], clear, 0)
    base = jnp.int32(0)
    lows, highs = [], []
    for r in range(requests):
        length = lens_ref[r]
        relevant = (r >= first_req) & (r <= last_req)
        count = jnp.where(relevant, (length + PAGE - 1) // PAGE, 0)

        def place(l, at, r=r):
            page = table_ref[r, l]
            held = page // (2 * pages_dev * members) == chip // members

            @pl.when(held)
            def _():
                slot_of[page] = at

            return at + held.astype(jnp.int32)

        end = lax.fori_loop(0, count, place, base)
        last_page = table_ref[r, (length + PAGE - 1) // PAGE - 1]
        cut = jnp.where(
            (end > base) & (last_page // (2 * pages_dev * members) == chip // members),
            (length + PAGE - 1) // PAGE * PAGE - length,
            0,
        )
        lows.append(base * PAGE)
        highs.append(end * PAGE - cut)
        base = end

    for e in range(members):
        source = chip ^ e
        for block, owner in ((near[e], 2 * source + core), (far[e], 2 * source + 1 - core)):
            for s in range(old):
                slot = slot_of[owner * pages_dev + s]

                @pl.when(slot >= 0)
                def _(block=block, s=s, slot=slot):
                    at = pl.ds(pl.multiple_of(slot * PAGE, PAGE), PAGE)
                    kbuf[at, :] = block[s]
                    vbuf[at, :] = block[old + s]

    step_pages = STEP_PAGES
    pad = pl.ds(pl.multiple_of(base * PAGE, PAGE), (step_pages - 1) * PAGE)
    kbuf[pad, :] = jnp.zeros(((step_pages - 1) * PAGE, HD), kbuf.dtype)
    vbuf[pad, :] = jnp.zeros(((step_pages - 1) * PAGE, HD), vbuf.dtype)
    tokens = who * toks + lax.broadcasted_iota(jnp.int32, (1, width), 1) % toks
    low = pick(starts, lows, tokens)
    high = pick(starts, highs, tokens)
    m_ref[...] = jnp.full(m_ref.shape, NEG_START, jnp.float32)
    l_ref[...] = jnp.zeros(l_ref.shape, jnp.float32)
    acc_ref[...] = jnp.zeros(acc_ref.shape, jnp.float32)

    def step(i, carry):
        size = step_pages * PAGE
        at = pl.ds(pl.multiple_of(i * size, size), size)
        attend_block(qs_ref, kbuf[at, :], vbuf[at, :], i * size, low, high, m_ref, l_ref, acc_ref)
        return carry

    lax.fori_loop(0, (base + step_pages - 1) // step_pages, step, 0)
    if away:
        outs[0][:HD, :] = acc_ref[...].astype(jnp.bfloat16)
        outs[0][HD:, :] = jnp.concatenate(
            [three_parts(m_ref[...]), three_parts(l_ref[...]), jnp.zeros((10, width), jnp.float32)], axis=0
        ).astype(jnp.bfloat16)
    else:
        outs[0][...], outs[1][...], outs[2][...] = m_ref[...], l_ref[...], acc_ref[...]


def fresh_kernel(
    chips, pages_dev, lens_ref, table_ref, tr_ref, qs_ref, m0_ref, l0_ref, acc0_ref, back_ref, *refs
):
    fresh = refs[:chips]
    atto_ref, attc_ref, no_ref, nc_ref, info_ref = refs[chips : chips + 5]
    nbuf, m_ref, l_ref, acc_ref, out_ref, new_at, new_lo, new_hi = refs[chips + 5 :]
    dp = lax.axis_index("dp")
    chip, core = dp // 2, dp % 2
    place = ring_place(chip, chips)
    toks = fresh[0].shape[0]
    rows = toks // 2
    requests = lens_ref.shape[0]
    width = qs_ref.shape[0]
    group = width // toks
    starts = request_starts(tr_ref, requests)
    reqs = chip_requests(chip, toks, starts)
    first_req = reqs[0]
    parts = back_ref[HD : HD + 6, :].astype(jnp.float32)
    m0, m1 = m0_ref[...], parts[0:1] + parts[1:2] + parts[2:3]
    top = jnp.maximum(m0, m1)
    f0, f1 = jnp.exp2(m0 - top), jnp.exp2(m1 - top)
    m_ref[...] = top
    l_ref[...] = l0_ref[...] * f0 + (parts[3:4] + parts[4:5] + parts[5:6]) * f1
    acc_ref[...] = acc0_ref[...] * f0 + back_ref[:HD, :].astype(jnp.float32) * f1

    def clear(i, carry):
        new_lo[i] = 0
        new_hi[i] = 0
        return carry

    lax.fori_loop(0, new_lo.shape[0], clear, 0)
    for r in range(requests):
        length = lens_ref[r]

        def place_new(l, carry, r=r, length=length):
            at = l * PAGE - length + starts[r]
            page = table_ref[r, l]
            new_at[page] = at
            new_lo[page] = jnp.maximum(starts[r] - at, 0)
            new_hi[page] = jnp.minimum(starts[r + 1] - at, PAGE)
            return carry

        end = (length + starts[r + 1] - starts[r] + PAGE - 1) // PAGE
        lax.fori_loop(length // PAGE, end, place_new, 0)

    for n, offset in enumerate(ring_offsets(chips)):
        source = ring_chip(place + offset + chips, chips)
        nbuf[pl.ds(pl.multiple_of((source + 1) * toks, toks), toks), :] = fresh[n][...]
    nbuf[:toks, :] = jnp.zeros((toks, 2 * HD), nbuf.dtype)
    nbuf[(chips + 1) * toks :, :] = jnp.zeros((toks, 2 * HD), nbuf.dtype)

    tokens = chip * toks + lax.broadcasted_iota(jnp.int32, (1, width), 1) % toks
    low = pick(starts, starts[:requests], tokens)
    first_start = starts[0]
    for r in range(1, requests):
        first_start = jnp.where(first_req == r, starts[r], first_start)

    def step(b, carry):
        at = pl.ds(pl.multiple_of((b + 1) * toks, toks), toks)
        attend_block(qs_ref, nbuf[at, :HD], nbuf[at, HD:], b * toks, low, tokens + 1, m_ref, l_ref, acc_ref)
        return carry

    lax.fori_loop(first_start // toks, chip + 1, step, 0)
    result = acc_ref[...] / l_ref[...]
    for h in range(group):
        out_ref[:, h * HD : (h + 1) * HD] = result[:, h * toks : (h + 1) * toks].T.astype(jnp.bfloat16)
    attc_ref[...] = out_ref[pl.ds(pl.multiple_of(core * rows, rows), rows), :]
    atto_ref[...] = out_ref[pl.ds(pl.multiple_of((1 - core) * rows, rows), rows), :]

    row = lax.broadcasted_iota(jnp.int32, (PAGE, 2 * toks), 0)
    column = lax.broadcasted_iota(jnp.int32, (PAGE, 2 * toks), 1)
    for ref, owner in ((no_ref, dp + 1 - 2 * core), (nc_ref, dp)):
        for s in range(pages_dev):
            page = owner * pages_dev + s
            at, low_row, high_row = new_at[page], new_lo[page], new_hi[page]

            @pl.when(high_row > low_row)
            def _(ref=ref, s=s, at=at, low_row=low_row, high_row=high_row):
                shifted = at + toks
                first = pl.multiple_of(shifted // toks * toks, toks)
                chosen = (column + first == row + shifted) & (row >= low_row) & (row < high_row)
                ref[s] = jnp.dot(
                    jnp.where(chosen, 1.0, 0.0).astype(jnp.bfloat16),
                    nbuf[pl.ds(first, 2 * toks), :],
                    preferred_element_type=jnp.float32,
                ).astype(jnp.bfloat16)

    for s in range(pages_dev):
        info_ref[2 * s] = new_lo[dp * pages_dev + s]
        info_ref[2 * s + 1] = new_hi[dp * pages_dev + s]


def join_kernel(info_ref, attc_ref, attr_ref, nc_ref, nr_ref, kp_ref, vp_ref, att_ref, ko_ref, vo_ref):
    core = lax.axis_index("dp") % 2
    half = attc_ref.shape[1]
    att_ref[:, pl.ds(pl.multiple_of(core * half, HD), half)] = attc_ref[...]
    att_ref[:, pl.ds(pl.multiple_of((1 - core) * half, HD), half)] = attr_ref[...]
    row = lax.broadcasted_iota(jnp.int32, (PAGE, HD), 0)
    for s in range(kp_ref.shape[0]):
        chosen = (row >= info_ref[2 * s]) & (row < info_ref[2 * s + 1])
        for ref, head in ((nc_ref, core), (nr_ref, 1 - core)):
            at = pl.ds(pl.multiple_of(head * HD, HD), HD)
            ko_ref[s, :, at] = jnp.where(chosen, ref[s, :, :HD], kp_ref[s, :, at])
            vo_ref[s, :, at] = jnp.where(chosen, ref[s, :, HD:], vp_ref[s, :, at])


def call(
    kernel, outs, scratch=(), ins=None, smem=(), far=(), out_smem=(), out_far=(), limit=VMEM_LIMIT, name=None
):
    vmem, sm = pl.BlockSpec(memory_space=pltpu.VMEM), pl.BlockSpec(memory_space=pltpu.SMEM)
    hbm = pl.BlockSpec(memory_space=pl.ANY)
    return pl.pallas_call(
        kernel,
        out_shape=[jax.ShapeDtypeStruct(s, d) for s, d in outs],
        in_specs=[sm if n in smem else hbm if n in far else vmem for n in range(ins)],
        out_specs=[sm if n in out_smem else hbm if n in out_far else vmem for n in range(len(outs))],
        scratch_shapes=list(scratch),
        compiler_params=pltpu.CompilerParams(vmem_limit_bytes=limit),
        name=name,
    )


def ring_send(chips, arrays, step, swap=0):
    return [lax.ppermute(a, "dp", ring_pairs(chips, step, swap * n)) for n, a in enumerate(arrays)]


def ring_body(
    dp_count,
    features,
    norm_gain,
    w_key,
    w_value,
    queries,
    key_pool,
    value_pool,
    cache_lens,
    page_table,
    token_request,
):
    bf, f32, i32 = jnp.bfloat16, jnp.float32, jnp.int32
    chips = dp_count // 2
    offsets = ring_offsets(chips)
    rows, half_width = features.shape
    width = norm_gain.shape[0]
    toks = 2 * rows
    pages_dev = key_pool.shape[0]
    long_pages = (CTX_DEV * dp_count + PAGE - 1) // PAGE
    old = (long_pages + 2 * ((SHORT + PAGE - 1) // PAGE) + dp_count - 1) // dp_count
    group = queries.shape[1] // (2 * HD)
    columns = group * toks
    core_pairs = [(i, i ^ 1) for i in range(dp_count)]
    mp_pairs = [(0, 1), (1, 0)]
    both_pairs = [(2 * i + j, 2 * (i ^ 1) + (1 - j)) for i in range(dp_count) for j in range(2)]
    requests_tile = token_request.reshape(-1, 128)

    def exchange(array, e, swap=0):
        return lax.ppermute(array, "dp", [(i, i ^ (2 * e) ^ swap) for i in range(dp_count)])

    w_got = {0: [w_key, w_value]}
    right, left = ring_send(chips, [w_key, w_value], 1), ring_send(chips, [w_key, w_value], -1)
    w_got[-1], w_got[1] = right, left
    bundle = 2 * old * PAGE + group * rows
    x_mine, x_other, kv_mine, core_send = call(
        functools.partial(split_kernel, old),
        [
            ((rows, half_width // 2), bf),
            ((rows, half_width // 2), bf),
            ((2 * old, PAGE, HD), bf),
            ((bundle, HD), bf),
        ],
        scratch=[pltpu.SemaphoreType.DMA((2 * (half_width // 512) + 2 + 2 * old + group,))],
        ins=4,
        far=(0, 1, 2, 3),
        limit=SPLIT_LIMIT,
        name="split",
    )(features, queries, key_pool, value_pool)
    core_send, _ = lax.optimization_barrier((core_send, w_got[-1]))
    core_got = lax.ppermute(core_send, "dp", core_pairs)
    x_b = lax.ppermute(x_mine, "mp", mp_pairs)
    x_c = lax.ppermute(x_other, "dp", core_pairs)
    x_d = lax.ppermute(x_other, ("dp", "mp"), both_pairs)
    q_rows, kv_other = call(
        merge_kernel,
        [((columns, HD), bf), ((2 * old, PAGE, HD), bf)],
        ins=2,
        name="merge",
    )(queries, core_got)
    for d in range(2, chips // 2):
        right, left = ring_send(chips, right, 1), ring_send(chips, left, -1)
        w_got[-d], w_got[d] = right, left
    inverse = (THETA ** (-(np.arange(HD) % (HD // 2)) * 2.0 / HD)).astype(np.float32)[None, :]
    scaled, squares, cosine, sine = call(
        functools.partial(scale_kernel, chips),
        [((chips, toks, 256), bf), ((toks, 128), f32), ((toks, HD), f32), ((toks, HD), f32)],
        ins=8,
        smem=(0,),
        name="scale",
    )(
        cache_lens,
        requests_tile,
        jnp.asarray(inverse),
        norm_gain.reshape(1, -1),
        x_mine,
        x_b,
        x_c,
        x_d,
    )
    w_got[chips // 2] = ring_send(chips, right[:1], 1) + ring_send(chips, left[1:], -1)
    scaled, q_rows, kv_other = lax.optimization_barrier((scaled, q_rows, kv_other))
    part_send, part_keep = call(
        functools.partial(project_kernel, chips),
        [((toks, 3 * HD), f32), ((toks, 3 * HD), f32)],
        scratch=[pltpu.VMEM((toks, 4 * HD), f32)],
        ins=2 + 2 * chips,
        name="project",
    )(scaled, squares, *[w_got[o][0] for o in offsets], *[w_got[o][1] for o in offsets])
    part_got = lax.ppermute(part_send, "dp", core_pairs)

    first_near, first_far, _ = lax.optimization_barrier((kv_mine, kv_other, part_send))
    z_near, z_far = exchange(first_near, 2), exchange(first_far, 2)
    y_near, y_far = exchange(first_near, 1), exchange(first_far, 1)
    (fresh,) = call(
        functools.partial(rotate_kernel, width),
        [((toks, 2 * HD), bf)],
        ins=4,
        name="rotary",
    )(part_keep, part_got, cosine, sine)
    new = {0: fresh}
    new[-1], new[1] = ring_send(chips, [fresh], 1)[0], ring_send(chips, [fresh], -1)[0]
    late_q, right = lax.optimization_barrier((q_rows, new[-1]))
    q_away = exchange(late_q, chips // 2)
    late_y, late_z, q_away, _ = lax.optimization_barrier((y_near, z_far, q_away, (new[-1], new[1])))
    near = [kv_mine, y_near, z_near, exchange(late_y, 2)]
    far = [kv_other, y_far, z_far, exchange(late_z, 1)]
    slots = dp_count // 2 * old + STEP_PAGES
    table = pltpu.SMEM((dp_count * pages_dev,), i32)

    def cached(q, away, outs, name):
        return call(
            functools.partial(cached_kernel, chips, pages_dev, old, away),
            outs,
            scratch=[
                pltpu.VMEM((slots * PAGE, HD), bf),
                pltpu.VMEM((slots * PAGE, HD), bf),
                pltpu.VMEM((1, columns), f32),
                pltpu.VMEM((1, columns), f32),
                pltpu.VMEM((HD, columns), f32),
                table,
            ],
            ins=4 + chips,
            smem=(0, 1),
            name=name,
        )(cache_lens, page_table, requests_tile, q, *near, *far)

    (away,) = cached(q_away, chips // 2, [((HD + 16, columns), bf)], "attend_cached_away")
    here = cached(
        q_rows, 0, [((1, columns), f32), ((1, columns), f32), ((HD, columns), f32)], "attend_cached_here"
    )
    new[-2], new[2] = ring_send(chips, [new[-1]], 1)[0], ring_send(chips, [new[1]], -1)[0]
    right, left = lax.optimization_barrier((new[-2], new[2]))
    new[-3], new[3] = ring_send(chips, [right], 1)[0], ring_send(chips, [left], -1)[0]
    right, new[3], away = lax.optimization_barrier((new[-3], new[3], away))
    (new[chips // 2],) = ring_send(chips, [right], 1)
    back = exchange(away, chips // 2)
    top, total, acc = here

    att_other, att_mine, rows_other, rows_mine, info = call(
        functools.partial(fresh_kernel, chips, pages_dev),
        [
            ((rows, group * HD), bf),
            ((rows, group * HD), bf),
            ((pages_dev, PAGE, 2 * HD), bf),
            ((pages_dev, PAGE, 2 * HD), bf),
            ((2 * pages_dev,), i32),
        ],
        scratch=[
            pltpu.VMEM(((chips + 2) * toks, 2 * HD), bf),
            pltpu.VMEM((1, columns), f32),
            pltpu.VMEM((1, columns), f32),
            pltpu.VMEM((HD, columns), f32),
            pltpu.VMEM((toks, group * HD), bf),
            table,
            table,
            table,
        ],
        ins=8 + chips,
        smem=(0, 1),
        out_smem=(4,),
        name="attend_new",
    )(
        cache_lens,
        page_table,
        requests_tile,
        q_rows,
        top,
        total,
        acc,
        back,
        *[new[o] for o in offsets],
    )
    rows_got = lax.ppermute(rows_other, "dp", core_pairs)
    att_got = lax.ppermute(att_other, "dp", core_pairs)
    attended, keys_out, values_out = call(
        join_kernel,
        [(queries.shape, bf), (key_pool.shape, bf), (value_pool.shape, bf)],
        ins=7,
        smem=(0,),
        name="join",
    )(info, att_mine, att_got, rows_mine, rows_got, key_pool, value_pool)
    return attended, keys_out, values_out


def solution(mesh):
    in_specs = (
        P("dp", "mp"),
        P(),
        P("dp", "mp"),
        P("dp", "mp"),
        P("dp", "mp"),
        P("dp", None, "mp"),
        P("dp", None, "mp"),
        P(),
        P(),
        P(),
    )
    out_specs = (P("dp", "mp"), P("dp", None, "mp"), P("dp", None, "mp"))
    dp_count, mp_count = mesh.shape["dp"], mesh.shape["mp"]

    def body(*args):
        even = mp_count == 2 and dp_count == 16
        if even and args[2].shape == (256, 2 * HD):
            return ring_body(dp_count, *args)
        return general_body(*args)

    return jax.shard_map(body, mesh=mesh, in_specs=in_specs, out_specs=out_specs, check_vma=False)
```
